32 devices in a mesh: gx: 4 (over z), gy: 4 (over x, core), ha: 2 (over y).
Axes of the slice: x: 2, y: 2, z: 4, core: 2. Of those that a mesh axis runs over, the one named last changes fastest.
Arguments:
- wavefield: float32 [4, 4, 2, 32, 9, 512], P('gx', 'gy', 'ha'), may hold values from -6 to 6
- deriv_ops: float32 [3, 512, 512], replicated, may hold values from -0.25 to 0.25
- density: float32 [4, 4, 2, 32], P('gx', 'gy', 'ha'), may hold values from 1 to 3
- lame_first: float32 [4, 4, 2, 32], P('gx', 'gy', 'ha'), may hold values from 0.5 to 2
- shear_modulus: float32 [4, 4, 2, 32], P('gx', 'gy', 'ha'), may hold values from 0.3 to 1
- high_order: int32 [4, 4, 2, 32], P('gx', 'gy', 'ha'), may hold values from 0 to 1, as said below
- element_cell: int32 [4, 4, 2, 32], P('gx', 'gy', 'ha'), may hold values from 0 to 31, each once within a row
- face_orient: int32 [4, 4, 2, 6, 32], P('gx', 'gy', 'ha'), may hold values from 0 to 7
Outputs:
- advanced: float32 [4, 4, 2, 32, 9, 512], P('gx', 'gy', 'ha')
The draws below stay inside these ranges and needn't reach their ends.
Inputs may be any that keep to these rules, and one draw needn't show every extreme that they name: `high_order`: within each group of devices along ha that share gx and gy, exactly half of the devices have 16 flagged elements and the others none; which devices and which elements are drawn. `element_cell`: on every device a permutation of the cells 0 to 31.
All inputs are finite; a program needn't handle non-finite values.
Results may differ from the reference program's by a relative error of at most 0.0001.
Values sent between devices are 32-bit elements; how exact they have to be, the bound alone decides.
No kernel may reach another device: no remote copies, remote signals or barrier semaphores. Data moves between devices by JAX's collectives and lax.ppermute only.
A program may use at most 128 MiB of HBM per device.

```python
import math
import jax
import jax.numpy as jnp
from jax import lax

P_SIZE = 8
NODES = 512
FIELDS = 9
EXY = 4
EZ = 2
E_DEV = 32
HOT = 16
STEPS = 2
N_GX = 4
N_GY = 4
N_HA = 2


def shuffled_devices(one_key):
    return jax.random.permutation(one_key, N_HA)


def shuffled_elements(one_key):
    return jax.random.permutation(one_key, E_DEV)


def draw_high_order(key, part):
    base_key = jax.random.fold_in(key, 7)
    heavy_key, element_key = jax.random.split(base_key)
    column_count = N_GX * N_GY
    heavy_keys = jax.random.split(heavy_key, column_count)
    overloaded = jax.vmap(shuffled_devices)(heavy_keys) < N_HA // 2
    element_keys = jax.random.split(element_key, column_count * N_HA)
    element_ranks = jax.vmap(shuffled_elements)(element_keys)
    marked = (element_ranks < HOT) & overloaded.reshape(column_count * N_HA, 1)
    return marked.astype(jnp.int32).reshape(N_GX, N_GY, N_HA, E_DEV)


def place_ends(values, rng, low, largest):
    spot = [jax.random.randint(jax.random.fold_in(rng, axis), (), 0, length) for axis, length in enumerate(values.shape)]
    main_axis = values.shape.index(max(values.shape))
    beside = spot[:main_axis] + [(spot[main_axis] + 1) % values.shape[main_axis]] + spot[main_axis + 1:]
    return values.at[tuple(spot)].set(low).at[tuple(beside)].set(largest)


def steps_of(stream_key, extent, cuts, smallest, top_value):
    loudness, own = 1.0, jax.random.fold_in(stream_key, 6)
    for axis_at, shards_of in cuts:
        heights = jnp.exp(jax.random.uniform(jax.random.fold_in(own, axis_at), (shards_of,), jnp.float32, smallest / len(cuts), top_value / len(cuts)))
        loudness = loudness * jnp.repeat(heights, extent[axis_at] // shards_of).reshape([-1 if axis == axis_at else 1 for axis in range(len(extent))])
    return loudness


def normal_values(own_key, shape, width, most, cuts=(), dtype=jnp.bfloat16):
    entries = jax.random.normal(own_key, shape, jnp.float32) * width
    if len(cuts) > 0:
        entries = steps_of(own_key, shape, cuts, -0.22, 0.18) * entries
    return jnp.clip(entries, min=-most, max=most).astype(dtype)


def setup_inputs(seed: int = 0) -> dict:
    keys = jax.random.split(jax.random.key(seed), 9)
    wavefield = normal_values(keys[0], (N_GX, N_GY, N_HA, E_DEV, FIELDS, NODES), 1.0, 6.0, ((0, 4), (1, 4), (2, 2)), jnp.float32)
    deriv_ops = normal_values(keys[1], (3, NODES, NODES), NODES ** -0.5, 0.25, (), jnp.float32)
    density = jnp.clip(jnp.exp(math.log(3.0) - 1.0986123 * jax.random.uniform(keys[2], (N_GX, N_GY, N_HA, E_DEV), jnp.float32) ** steps_of(keys[2], (N_GX, N_GY, N_HA, E_DEV), ((0, 4), (1, 4), (2, 2)), -0.2, 0.2)), 1.0, 3.0)
    lame_first = jnp.clip(jnp.exp(math.log(2.0) - 1.3862944 * jax.random.uniform(keys[3], (N_GX, N_GY, N_HA, E_DEV), jnp.float32) ** steps_of(keys[3], (N_GX, N_GY, N_HA, E_DEV), ((0, 4), (1, 4), (2, 2)), -0.2, 0.2)), 0.5, 2.0)
    shear_modulus = jnp.clip(jnp.exp(math.log(1.0) - 1.2039728 * jax.random.uniform(keys[4], (N_GX, N_GY, N_HA, E_DEV), jnp.float32) ** steps_of(keys[4], (N_GX, N_GY, N_HA, E_DEV), ((0, 4), (1, 4), (2, 2)), -0.2, 0.2)), 0.3, 1.0)
    high_order = draw_high_order(jax.random.fold_in(keys[8], 71), 0)
    element_cell = jax.vmap(lambda own: jax.random.permutation(own, E_DEV))(jax.random.split(keys[6], N_GX * N_GY * N_HA)).reshape((N_GX, N_GY, N_HA, E_DEV)).astype(jnp.int32)
    face_orient = place_ends(jax.random.randint(keys[7], (N_GX, N_GY, N_HA, 6, E_DEV), 0, 8), jax.random.fold_in(keys[7], 1), 0, 7).astype(jnp.int32)
    return dict(wavefield=wavefield, deriv_ops=deriv_ops, density=density, lame_first=lame_first, shear_modulus=shear_modulus, high_order=high_order, element_cell=element_cell, face_orient=face_orient)


X_FIELDS = (0, 1, 2, 3, 6, 8)
Y_FIELDS = (0, 1, 2, 6, 4, 7)
Z_FIELDS = (0, 1, 2, 8, 7, 5)
DT_STEP = 0.8
LIFT_COEF = 2.0

def derive_along(field_rows, deriv_ops, picked, axis_index):
    chosen = field_rows[..., list(picked), :]
    return jnp.dot(chosen, deriv_ops[axis_index], precision=lax.Precision.HIGHEST, preferred_element_type=jnp.float32)

def time_rate(field_rows, inv_density, lame_coef, shear_coef, deriv_ops):
    x_deriv = derive_along(field_rows, deriv_ops, X_FIELDS, 0)
    y_deriv = derive_along(field_rows, deriv_ops, Y_FIELDS, 1)
    z_deriv = derive_along(field_rows, deriv_ops, Z_FIELDS, 2)
    inv_rho = inv_density[..., None]
    lame_col = lame_coef[..., None]
    shear_col = shear_coef[..., None]
    div_vel = x_deriv[..., 0, :] + y_deriv[..., 1, :] + z_deriv[..., 2, :]
    rate_rows = [inv_rho * (x_deriv[..., 3, :] + y_deriv[..., 3, :] + z_deriv[..., 3, :]), inv_rho * (x_deriv[..., 4, :] + y_deriv[..., 4, :] + z_deriv[..., 4, :]), inv_rho * (x_deriv[..., 5, :] + y_deriv[..., 5, :] + z_deriv[..., 5, :]), lame_col * div_vel + 2.0 * shear_col * x_deriv[..., 0, :], lame_col * div_vel + 2.0 * shear_col * y_deriv[..., 1, :], lame_col * div_vel + 2.0 * shear_col * z_deriv[..., 2, :], shear_col * (x_deriv[..., 1, :] + y_deriv[..., 0, :]), shear_col * (y_deriv[..., 2, :] + z_deriv[..., 1, :]), shear_col * (x_deriv[..., 2, :] + z_deriv[..., 0, :])]
    return jnp.stack(rate_rows, axis=-2)

def normal_flux(jump_face, inv_rho, lame_col, shear_col, direction):
    parts_list = [jump_face[..., index_value, :] for index_value in range(9)]
    zeros_face = jnp.zeros_like(parts_list[0])
    stiff_col = lame_col + 2.0 * shear_col
    if direction == 0:
        rows_out = [inv_rho * parts_list[3], inv_rho * parts_list[6], inv_rho * parts_list[8], stiff_col * parts_list[0], lame_col * parts_list[0], lame_col * parts_list[0], shear_col * parts_list[1], zeros_face, shear_col * parts_list[2]]
    elif direction == 1:
        rows_out = [inv_rho * parts_list[6], inv_rho * parts_list[4], inv_rho * parts_list[7], lame_col * parts_list[1], stiff_col * parts_list[1], lame_col * parts_list[1], shear_col * parts_list[0], shear_col * parts_list[2], zeros_face]
    else:
        rows_out = [inv_rho * parts_list[8], inv_rho * parts_list[7], inv_rho * parts_list[5], lame_col * parts_list[2], lame_col * parts_list[2], stiff_col * parts_list[2], zeros_face, shear_col * parts_list[1], shear_col * parts_list[0]]
    return -jnp.stack(rows_out, axis=-2)

def face_select(edge_nodes):
    node_count = edge_nodes ** 3
    face_nodes = edge_nodes * edge_nodes
    node_ids = jnp.arange(node_count)
    first_index = node_ids // face_nodes
    second_index = node_ids // edge_nodes % edge_nodes
    third_index = node_ids % edge_nodes
    column_ids = jnp.arange(6 * face_nodes)
    layout = [(first_index == 0, second_index, third_index), (first_index == edge_nodes - 1, second_index, third_index), (second_index == 0, first_index, third_index), (second_index == edge_nodes - 1, first_index, third_index), (third_index == 0, first_index, second_index), (third_index == edge_nodes - 1, first_index, second_index)]
    face_table = jnp.zeros((node_count, 6 * face_nodes), jnp.float32)
    for face_index in range(6):
        on_face, row_pos, col_pos = layout[face_index]
        target = face_index * face_nodes + row_pos * edge_nodes + col_pos
        picked = (column_ids[None, :] == target[:, None]) & on_face[:, None]
        face_table = face_table + picked.astype(jnp.float32)
    return face_table

def orient_faces(outside, orient_codes, edge_nodes):
    face_grid = outside.reshape(outside.shape[:-1] + (edge_nodes, edge_nodes))
    result = jnp.zeros_like(face_grid)
    for orient_code in range(8):
        variant = face_grid
        if orient_code & 4:
            variant = jnp.swapaxes(variant, -1, -2)
        if orient_code & 1:
            variant = jnp.flip(variant, -2)
        if orient_code & 2:
            variant = jnp.flip(variant, -1)
        result = jnp.where((orient_codes == orient_code)[..., None, None], variant, result)
    return result.reshape(outside.shape)

def face_correction(own_traces, oriented, inv_density, lame_coef, shear_coef):
    inv_rho = inv_density[..., None]
    lame_col = lame_coef[..., None]
    shear_col = shear_coef[..., None]
    wave_speed = jnp.sqrt((lame_col + 2.0 * shear_col) * inv_rho)
    trace_jump = oriented - own_traces
    corrections = []
    for face_index in range(6):
        normal_sign = -1.0 if face_index % 2 == 0 else 1.0
        jump_face = trace_jump[..., face_index, :]
        flux_face = normal_flux(jump_face, inv_rho, lame_col, shear_col, face_index // 2)
        corrections.append(0.5 * (wave_speed[..., None] * jump_face - normal_sign * flux_face))
    return jnp.stack(corrections, axis=-2)

def extra_series(start_rows, inv_density, lame_coef, shear_coef, deriv_ops):
    series_term = start_rows
    series_sum = jnp.zeros_like(start_rows)
    for order_index in (3, 4, 5):
        series_term = time_rate(series_term, inv_density, lame_coef, shear_coef, deriv_ops)
        series_sum = series_sum + DT_STEP ** order_index / math.factorial(order_index + 1) * series_term
    return series_sum

def shift_along(block, axis_index, from_lower):
    zero_layer = jnp.zeros_like(lax.slice_in_dim(block, 0, 1, axis=axis_index))
    length = block.shape[axis_index]
    if from_lower:
        return jnp.concatenate([zero_layer, lax.slice_in_dim(block, 0, length - 1, axis=axis_index)], axis=axis_index)
    return jnp.concatenate([lax.slice_in_dim(block, 1, length, axis=axis_index), zero_layer], axis=axis_index)

def reference(wavefield, deriv_ops, density, lame_first, shear_modulus, high_order, element_cell, face_orient):
    face_table = face_select(P_SIZE)
    face_nodes = P_SIZE * P_SIZE
    inv_density = 1.0 / density
    orient_codes = jnp.swapaxes(face_orient, -1, -2)[..., None, :]
    row_total = N_GX * N_GY * N_HA * E_DEV
    flat_flagged = jnp.nonzero(high_order.reshape(-1), size=N_GX * N_GY * N_HA // 2 * HOT)[0].astype(jnp.int32)
    inverse = jnp.argsort(element_cell, axis=-1).astype(jnp.int32)
    cell_index = element_cell.astype(jnp.int32)
    flat_inv = inv_density.reshape(row_total)[flat_flagged]
    flat_lame = lame_first.reshape(row_total)[flat_flagged]
    flat_shear = shear_modulus.reshape(row_total)[flat_flagged]
    current = wavefield
    for step_index in range(STEPS):
        first_rate = time_rate(current, inv_density, lame_first, shear_modulus, deriv_ops)
        second_rate = time_rate(first_rate, inv_density, lame_first, shear_modulus, deriv_ops)
        integrated = current + DT_STEP / 2.0 * first_rate + DT_STEP ** 2 / 6.0 * second_rate
        flat_second = second_rate.reshape(row_total, FIELDS, NODES)[flat_flagged]
        extra_term = extra_series(flat_second, flat_inv, flat_lame, flat_shear, deriv_ops)
        integrated = integrated.reshape(row_total, FIELDS, NODES).at[flat_flagged].add(extra_term).reshape(current.shape)
        traces = jnp.dot(integrated, face_table, precision=lax.Precision.HIGHEST, preferred_element_type=jnp.float32)
        cell_traces = jnp.take_along_axis(traces, inverse[..., None, None], axis=3)
        cell_brick = cell_traces.reshape(N_GX, N_GY, N_HA, EXY, EXY, EZ, FIELDS, 6, face_nodes)
        cell_brick = cell_brick.transpose(0, 3, 1, 4, 2, 5, 6, 7, 8).reshape(N_GX * EXY, N_GY * EXY, N_HA * EZ, FIELDS, 6, face_nodes)
        outside_list = [shift_along(cell_brick[..., 1, :], 0, True), shift_along(cell_brick[..., 0, :], 0, False), shift_along(cell_brick[..., 3, :], 1, True), shift_along(cell_brick[..., 2, :], 1, False), shift_along(cell_brick[..., 5, :], 2, True), shift_along(cell_brick[..., 4, :], 2, False)]
        outside = jnp.stack(outside_list, axis=-2)
        outside = outside.reshape(N_GX, EXY, N_GY, EXY, N_HA, EZ, FIELDS, 6, face_nodes)
        outside = outside.transpose(0, 2, 4, 1, 3, 5, 6, 7, 8).reshape(N_GX, N_GY, N_HA, E_DEV, FIELDS, 6, face_nodes)
        outside = jnp.take_along_axis(outside, cell_index[..., None, None, None], axis=3)
        oriented = orient_faces(outside, orient_codes, P_SIZE)
        own_traces = traces.reshape(N_GX, N_GY, N_HA, E_DEV, FIELDS, 6, face_nodes)
        correction = face_correction(own_traces, oriented, inv_density, lame_first, shear_modulus)
        correction = correction.reshape(N_GX, N_GY, N_HA, E_DEV, FIELDS, 6 * face_nodes)
        lifted = jnp.dot(correction, face_table.T, precision=lax.Precision.HIGHEST, preferred_element_type=jnp.float32)
        volume_rate = time_rate(integrated, inv_density, lame_first, shear_modulus, deriv_ops)
        current = current + DT_STEP * (volume_rate + LIFT_COEF * lifted)
    return current
```

```python
import functools
import math

import jax
import jax.numpy as jnp
from jax import lax
from jax.experimental import pallas as pl
from jax.experimental.pallas import tpu as pltpu
from jax.sharding import PartitionSpec as P

STEPS = 2
DT = 0.8
LIFT = 2.0
PICKED = ((0, 1, 2, 3, 6, 8), (0, 1, 2, 6, 4, 7), (0, 1, 2, 8, 7, 5))
F32 = jnp.float32
BF16 = jnp.bfloat16
VMEM_LIMIT = 48 << 20


def wide(column, count):
    return jnp.concatenate([column] * count, axis=1)


def get(field, rows, cols):
    return jnp.concatenate([field[t, rows, :] for t in range(cols.start // 128, cols.stop // 128)], axis=1)


def put(field, rows, cols, value):
    for t in range(cols.start // 128, cols.stop // 128):
        field[t, rows, :] = value[:, t * 128 - cols.start : (t + 1) * 128 - cols.start]


def add(field, rows, cols, value):
    put(field, rows, cols, get(field, rows, cols) + value)


def split(value):
    high = value.astype(BF16)
    return high, (value - high.astype(F32)).astype(BF16)


def dot(left, right):
    return jnp.dot(left, right, preferred_element_type=F32)


def lanes_of(rows):
    return lax.broadcasted_iota(jnp.int32, (rows, 128), 1)


def rate(high, low, w_high, w_low, par, stride, rows, emit, block=256):
    nodes = w_high.shape[-1]
    inv_rho = wide(par[0:rows], block // 128)
    lame = wide(par[stride : stride + rows], block // 128)
    shear = wide(par[2 * stride : 2 * stride + rows], block // 128)
    shear2 = 2.0 * shear
    for start in range(0, nodes, block):
        cols = slice(start, start + block)
        deriv = []
        for dim in range(3):
            top = jnp.concatenate([high[f * stride : f * stride + rows] for f in PICKED[dim]], axis=0)
            rest = jnp.concatenate([low[f * stride : f * stride + rows] for f in PICKED[dim]], axis=0)
            both = dot(jnp.concatenate([top, rest], axis=0), w_high[dim, :, cols])
            deriv.append(both[: 6 * rows] + both[6 * rows :] + dot(top, w_low[dim, :, cols]))
        part = lambda dim, row: deriv[dim][row * rows : (row + 1) * rows]
        div = lame * (part(0, 0) + part(1, 1) + part(2, 2))
        emit(0, cols, inv_rho * (part(0, 3) + part(1, 3) + part(2, 3)))
        emit(1, cols, inv_rho * (part(0, 4) + part(1, 4) + part(2, 4)))
        emit(2, cols, inv_rho * (part(0, 5) + part(1, 5) + part(2, 5)))
        emit(3, cols, div + shear2 * part(0, 0))
        emit(4, cols, div + shear2 * part(1, 1))
        emit(5, cols, div + shear2 * part(2, 2))
        emit(6, cols, shear * (part(0, 1) + part(1, 0)))
        emit(7, cols, shear * (part(1, 2) + part(2, 1)))
        emit(8, cols, shear * (part(0, 2) + part(2, 0)))


def correction(jump, par, count, dim, rows):
    take = lambda k: par[k * count : k * count + rows] if not isinstance(rows, slice) else par[
        k * count + rows.start : k * count + rows.stop
    ]
    inv_rho, lame, shear, half_speed = take(0), take(1), take(2), take(3)
    size = jump[0].shape[0]
    sign = jnp.where(lanes_of(size) < 64, -0.5, 0.5)
    inv_rho, lame, shear = sign * inv_rho, sign * lame, sign * shear
    stiff = lame + 2.0 * shear
    if dim == 0:
        flux = [inv_rho * jump[3], inv_rho * jump[6], inv_rho * jump[8]]
        flux += [stiff * jump[0], lame * jump[0], lame * jump[0]]
        flux += [shear * jump[1], None, shear * jump[2]]
    elif dim == 1:
        flux = [inv_rho * jump[6], inv_rho * jump[4], inv_rho * jump[7]]
        flux += [lame * jump[1], stiff * jump[1], lame * jump[1]]
        flux += [shear * jump[0], shear * jump[2], None]
    else:
        flux = [inv_rho * jump[8], inv_rho * jump[7], inv_rho * jump[5]]
        flux += [lame * jump[2], lame * jump[2], stiff * jump[2]]
        flux += [None, shear * jump[1], shear * jump[0]]
    return [
        half_speed * jump[f] if flux[f] is None else half_speed * jump[f] + flux[f] for f in range(len(jump))
    ]


def orient(value, index):
    return jnp.take_along_axis(value, index, axis=1, mode="promise_in_bounds")


def lift_edges(target, face, f, rows, count):
    lanes = lanes_of(face.shape[0])
    scaled = DT * LIFT * face
    top = slice(f * count + rows.start, f * count + rows.stop)
    last = target.shape[0] - 1
    target[0, top] = target[0, top] + jnp.where(lanes < 64, scaled, 0.0)
    target[last, top] = target[last, top] + jnp.where(lanes < 64, 0.0, scaled)


def lift_inner(target, face_high, face_low, lift_table):
    rows, nodes = target.shape[1], lift_table.shape[1]
    for start in range(0, nodes, 256):
        cols = slice(start, start + 256)
        lifted = dot(face_high[...], lift_table[:, cols]) + dot(face_low[...], lift_table[:, cols])
        add(target, slice(0, rows), cols, DT * LIFT * lifted)


def predict(count, fields, q, par, w_high, w_low, face_table, cell_sm, flag_sm, outs, scratch):
    int_high, int_low, trace_x, trace_y, trace_z, edge_x, edge_y, edge_z = outs
    h0, l0, h1, l1, total, second, packed, packed_par, series, hot_rows = scratch
    nodes = h0.shape[1]
    tiles_of_node = nodes // 128
    every = slice(0, nodes)
    for f in range(fields):
        rows = slice(f * count, (f + 1) * count)
        h0[rows], l0[rows] = split(get(q, rows, every))

    def first(f, cols, value):
        rows = slice(f * count, (f + 1) * count)
        put(total, rows, cols, get(q, rows, cols) + DT / 2.0 * value)
        h1[rows, cols], l1[rows, cols] = split(value)

    rate(h0, l0, w_high, w_low, par, count, count, first)

    def then(f, cols, value):
        rows = slice(f * count, (f + 1) * count)
        add(total, rows, cols, DT**2 / 6.0 * value)
        put(second, rows, cols, value)

    rate(h1, l1, w_high, w_low, par, count, count, then)

    slot = jnp.int32(0)
    for e in range(count):
        hot_rows[slot] = cell_sm[e]
        slot = slot + flag_sm[e]
    half = count // 2

    @pl.when(slot > 0)
    def _():
        for k in range(half):
            row = hot_rows[k]
            for t in range(tiles_of_node):
                packed[t, pl.ds(k, fields, stride=count), :] = second[t, pl.ds(row, fields, stride=count), :]
            packed_par[pl.ds(k, 3, stride=count), :] = par[pl.ds(row, 3, stride=count), :]
        for f in range(fields):
            rows = slice(f * count, f * count + half)
            h0[rows], l0[rows] = split(get(packed, rows, every))
        buffers = [(h0, l0), (h1, l1)]
        for order in (3, 4, 5):
            weight = DT**order / math.factorial(order + 1)
            source, target = buffers[(order - 3) % 2], buffers[(order - 2) % 2]

            def more(f, cols, value, order=order, weight=weight, target=target):
                rows = slice(f * count, f * count + half)
                (put if order == 3 else add)(series, rows, cols, weight * value)
                if order < 5:
                    target[0][rows, cols], target[1][rows, cols] = split(value)

            rate(source[0], source[1], w_high, w_low, packed_par, count, half, more)
        for k in range(half):
            row = hot_rows[k]
            spot = pl.ds(row, fields, stride=count)
            for t in range(tiles_of_node):
                total[t, spot, :] = total[t, spot, :] + series[t, pl.ds(k, fields, stride=count), :]

    for f in range(fields):
        rows = slice(f * count, (f + 1) * count)
        int_high[rows], int_low[rows] = split(get(total, rows, every))
        trace_x[rows] = jnp.where(lanes_of(count) < 64, total[0, rows], total[tiles_of_node - 1, rows])
    faces = dot(int_high[...], face_table[...]) + dot(int_low[...], face_table[...])
    trace_y[...] = faces[:, 0:128]
    trace_z[...] = faces[:, 128:256]
    for f in range(fields):
        edge_x[f * 8 : f * 8 + 8] = jnp.where(
            lanes_of(8) < 64, trace_x[f * count : f * count + 8], trace_x[(f + 1) * count - 8 : (f + 1) * count]
        )
    tiles = fields * count // 8
    minus = lanes_of(tiles) < 64
    pad = edge_y.shape[0] // 2
    for m in range(2):
        edge_y[m * pad : m * pad + tiles] = jnp.where(
            minus, trace_y[pl.ds(m, tiles, stride=8), :], trace_y[pl.ds(6 + m, tiles, stride=8), :]
        )
        if pad > tiles:
            edge_y[m * pad + tiles : (m + 1) * pad] = jnp.zeros((pad - tiles, 128), F32)
    pairs = fields * count // 2
    edge_z[...] = jnp.where(
        lanes_of(pairs) < 64, trace_z[pl.ds(0, pairs, stride=2), :], trace_z[pl.ds(1, pairs, stride=2), :]
    )


def inner(count, fields, q, int_high, int_low, trace_x, trace_y, trace_z, par, index, w_high, w_low, lift_table,
          base, face_high, face_low):
    def volume(f, cols, value):
        rows = slice(f * count, (f + 1) * count)
        put(base, rows, cols, get(q, rows, cols) + DT * value)

    rate(int_high, int_low, w_high, w_low, par, count, count, volume)
    lanes = lanes_of(count)
    sub = lax.broadcasted_iota(jnp.int32, (count, 128), 0)
    minus = lanes < 64
    zero = jnp.zeros((8, 128), F32)
    for dim, trace in enumerate((trace_x, trace_y, trace_z)):
        jump = []
        for f in range(fields):
            own = trace[f * count : (f + 1) * count]
            if dim == 0:
                above = jnp.concatenate([own[8:], zero], axis=0)
                below = jnp.concatenate([zero, own[:-8]], axis=0)
            elif dim == 1:
                above = jnp.where(sub % 8 < 6, pltpu.roll(own, count - 2, 0), 0.0)
                below = jnp.where(sub % 8 < 2, 0.0, pltpu.roll(own, 2, 0))
            else:
                above = jnp.where(sub % 2 < 1, pltpu.roll(own, count - 1, 0), 0.0)
                below = jnp.where(sub % 2 < 1, 0.0, pltpu.roll(own, 1, 0))
            beside = jnp.where(minus, above, below)
            jump.append(orient(beside, index[dim * count : (dim + 1) * count]) - own)
        fixed = correction(jump, par, count, dim, count)
        for f in range(fields):
            if dim == 0:
                lift_edges(base, fixed[f], f, slice(0, count), count)
            else:
                cols = slice((dim - 1) * 128, dim * 128)
                rows = slice(f * count, (f + 1) * count)
                face_high[rows, cols], face_low[rows, cols] = split(fixed[f])
    lift_inner(base, face_high, face_low, lift_table)


def outer(count, fields, sizes, got, base, par, index, lift_table, out, halo, face_high, face_low):
    lower, upper = [], []
    for dim, (axis, size) in enumerate(sizes):
        here = lax.axis_index(axis)
        odd = here % 2 == 1
        first, second = got[dim]
        second = first if second is None else second
        lower.append((jnp.logical_and(odd, here > 0) if size == 2 else None, odd, here > 0, first, second))
        upper.append((None, odd, here < size - 1, first, second))

    def from_lower(dim, rows, minus):
        _, odd, there, first, second = lower[dim]
        value = jnp.where(odd, first[rows], second[rows])
        return jnp.where(jnp.logical_and(there, jnp.logical_not(minus)), value, 0.0)

    def from_upper(dim, rows, minus):
        _, odd, there, first, second = upper[dim]
        value = jnp.where(odd, second[rows], first[rows])
        return jnp.where(jnp.logical_and(there, minus), value, 0.0)

    out[...] = base[...]
    minus8 = lanes_of(8) < 64
    for end in range(2):
        rows = slice(0, 8) if end == 0 else slice(count - 8, count)
        jump = []
        for f in range(fields):
            here = slice(f * 8, f * 8 + 8)
            value = from_lower(0, here, minus8) if end == 0 else from_upper(0, here, minus8)
            jump.append(orient(value, index[rows]))
        fixed = correction(jump, par, count, 0, rows)
        for f in range(fields):
            lift_edges(out, fixed[f], f, rows, count)
    tiles = fields * count // 8
    pad = got[1][0].shape[0] // 2
    pairs = fields * count // 2
    for dim in (1, 2):
        if dim == 1:
            halo[...] = jnp.zeros_like(halo)
            minus = lanes_of(tiles) < 64
            for m in range(2):
                here = slice(m * pad, m * pad + tiles)
                halo[pl.ds(m, tiles, stride=8), :] = from_lower(1, here, minus)
                halo[pl.ds(6 + m, tiles, stride=8), :] = from_upper(1, here, minus)
        else:
            minus = lanes_of(pairs) < 64
            halo[pl.ds(0, pairs, stride=2), :] = from_lower(2, slice(0, pairs), minus)
            halo[pl.ds(1, pairs, stride=2), :] = from_upper(2, slice(0, pairs), minus)
        jump = [
            orient(halo[f * count : (f + 1) * count], index[dim * count : (dim + 1) * count]) for f in range(fields)
        ]
        fixed = correction(jump, par, count, dim, count)
        for f in range(fields):
            cols = slice((dim - 1) * 128, dim * 128)
            rows = slice(f * count, (f + 1) * count)
            face_high[rows, cols], face_low[rows, cols] = split(fixed[f])
    lift_inner(out, face_high, face_low, lift_table)


def first_kernel(count, fields, wave, ops, density, lame, shear, cell, orient_code, cell_sm, flag_sm,
                 q, w_high, w_low, par, index, face_table, lift_table, *rest):
    outs, scratch = rest[:8], rest[8:]
    staged = scratch[4]
    put(staged, slice(0, fields * count), slice(0, wave.shape[1]), wave[...])
    for e in range(count):
        for t in range(q.shape[0]):
            q[t, pl.ds(cell_sm[e], fields, stride=count), :] = staged[t, pl.ds(e, fields, stride=count), :]
    for dim in range(3):
        for start in range(0, ops.shape[1], 128):
            rows = slice(start, start + 128)
            w_high[dim, rows, :], w_low[dim, rows, :] = split(ops[dim, rows, :])
    fills = cell[...] == lax.broadcasted_iota(jnp.int32, (count, count), 0)
    in_cell = lambda row: jnp.broadcast_to(
        jnp.sum(jnp.where(fills, row, 0.0), axis=1, keepdims=True), (count, 128)
    )
    inv_rho = in_cell(1.0 / density[...])
    lame_col = in_cell(lame[...])
    shear_col = in_cell(shear[...])
    par[0:count] = inv_rho
    par[count : 2 * count] = lame_col
    par[2 * count : 3 * count] = shear_col
    par[3 * count : 4 * count] = 0.5 * jnp.sqrt((lame_col + 2.0 * shear_col) * inv_rho)
    lanes = lanes_of(count)
    p_lane, r_lane = lanes % 64 // 8, lanes % 8
    for dim in range(3):
        code = jnp.where(
            lanes < 64,
            in_cell(orient_code[2 * dim].astype(F32)),
            in_cell(orient_code[2 * dim + 1].astype(F32)),
        ).astype(jnp.int32)
        p_from = jnp.where(code % 2 == 1, 7 - p_lane, p_lane)
        r_from = jnp.where(code // 2 % 2 == 1, 7 - r_lane, r_lane)
        source = jnp.where(code >= 4, r_from * 8 + p_from, p_from * 8 + r_from)
        index[dim * count : (dim + 1) * count] = source + jnp.where(lanes < 64, 64, 0)

    def on_face(node, column):
        i, j, k = node // 64, node // 8 % 8, node % 8
        plus = column // 64 % 2 * 7
        p, r = column % 64 // 8, column % 8
        along_y = (column < 128) & (j == plus) & (i == p) & (k == r)
        along_z = (column >= 128) & (k == plus) & (i == p) & (j == r)
        return jnp.where(along_y | along_z, 1.0, 0.0).astype(BF16)

    table = (face_table.shape[0], face_table.shape[1])
    face_table[...] = on_face(lax.broadcasted_iota(jnp.int32, table, 0), lax.broadcasted_iota(jnp.int32, table, 1))
    table = table[::-1]
    lift_table[...] = on_face(lax.broadcasted_iota(jnp.int32, table, 1), lax.broadcasted_iota(jnp.int32, table, 0))
    predict(count, fields, q, par, w_high, w_low, face_table, cell_sm, flag_sm, outs, scratch)


def inner_kernel(count, fields, *refs):
    inner(count, fields, *refs)


def unpack_got(sizes, refs):
    got, at = [], 0
    for _, size in sizes:
        pair = [None, None]
        for k in range(1 if size == 2 else 2):
            pair[k] = refs[at]
            at += 1
        got.append(pair)
    return got, refs[at:]


def middle_kernel(count, fields, sizes, *refs):
    got, refs = unpack_got(sizes, refs)
    base, par, index, w_high, w_low, face_table, lift_table, cell_sm, flag_sm = refs[:9]
    q, outs = refs[9], refs[10:18]
    halo, face_high, face_low = refs[18:21]
    outer(count, fields, sizes, got, base, par, index, lift_table, q, halo, face_high, face_low)
    predict(count, fields, q, par, w_high, w_low, face_table, cell_sm, flag_sm, outs, refs[21:])


def last_kernel(count, fields, sizes, *refs):
    got, refs = unpack_got(sizes, refs)
    base, par, index, lift_table, cell_sm, out, q, staged, halo, face_high, face_low = refs
    outer(count, fields, sizes, got, base, par, index, lift_table, q, halo, face_high, face_low)
    for e in range(count):
        for t in range(q.shape[0]):
            staged[t, pl.ds(e, fields, stride=count), :] = q[t, pl.ds(cell_sm[e], fields, stride=count), :]
    out[...] = get(staged, slice(0, fields * count), slice(0, out.shape[1]))


def exchange(edges, sizes):
    got = []
    for edge, (axis, size) in zip(edges, sizes):
        first, second = [], []
        for low in range(size):
            high = (low + 1) % size
            if high == 0 and (size % 2 or size == 2):
                continue
            (second if low % 2 else first).extend([(low, high), (high, low)])
        got.append(lax.ppermute(edge, axis, first))
        if size > 2:
            got.append(lax.ppermute(edge, axis, second))
    return got


def shards(sizes, wavefield, deriv_ops, density, lame_first, shear_modulus, high_order, element_cell, face_orient):
    count, fields, nodes = wavefield.shape[-3:]
    rows = fields * count
    wave = wavefield[0, 0, 0].swapaxes(0, 1).reshape(rows, nodes)
    row = lambda value: value.reshape(1, count)
    cell_sm = element_cell.reshape(count)
    flag_sm = high_order.reshape(count)
    codes = face_orient.reshape(6, 1, count)
    vmem = pl.BlockSpec(memory_space=pltpu.VMEM)
    smem = pl.BlockSpec(memory_space=pltpu.SMEM)
    shape = jax.ShapeDtypeStruct
    field_shape = shape((nodes // 128, rows, 128), F32)
    pad = -(-(rows // 8) // 8) * 8
    predicted = [
        shape((rows, nodes), BF16),
        shape((rows, nodes), BF16),
        shape((rows, 128), F32),
        shape((rows, 128), F32),
        shape((rows, 128), F32),
        shape((fields * 8, 128), F32),
        shape((2 * pad, 128), F32),
        shape((rows // 2, 128), F32),
    ]
    predict_scratch = [
        pltpu.VMEM((rows, nodes), BF16),
        pltpu.VMEM((rows, nodes), BF16),
        pltpu.VMEM((rows, nodes), BF16),
        pltpu.VMEM((rows, nodes), BF16),
        pltpu.VMEM(field_shape.shape, F32),
        pltpu.VMEM(field_shape.shape, F32),
        pltpu.VMEM(field_shape.shape, F32),
        pltpu.VMEM((3 * count, 128), F32),
        pltpu.VMEM(field_shape.shape, F32),
        pltpu.SMEM((count + 1,), jnp.int32),
    ]
    face_scratch = [pltpu.VMEM((rows, 256), BF16), pltpu.VMEM((rows, 256), BF16)]
    halo_scratch = [pltpu.VMEM((rows, 128), F32)] + face_scratch
    params = pltpu.CompilerParams(vmem_limit_bytes=VMEM_LIMIT)

    def call(kernel, operands, in_specs, out_shape, scratch, products, name):
        single = not isinstance(out_shape, list)
        return pl.pallas_call(
            kernel,
            out_shape=out_shape,
            in_specs=in_specs,
            out_specs=vmem if single else [vmem] * len(out_shape),
            scratch_shapes=scratch,
            compiler_params=params,
            cost_estimate=pl.CostEstimate(
                flops=products * 6 * rows * nodes * nodes * 4, bytes_accessed=4 * rows * nodes * 4, transcendentals=0
            ),
            name=name,
        )(*operands)

    q, w_high, w_low, par, index, face_table, lift_table, *ahead = call(
        functools.partial(first_kernel, count, fields),
        [wave, deriv_ops, row(density), row(lame_first), row(shear_modulus), row(element_cell), codes, cell_sm, flag_sm],
        [vmem] * 7 + [smem] * 2,
        [
            field_shape,
            shape(deriv_ops.shape, BF16),
            shape(deriv_ops.shape, BF16),
            shape((4 * count, 128), F32),
            shape((3 * count, 128), jnp.int32),
            shape((nodes, 256), BF16),
            shape((256, nodes), BF16),
        ]
        + predicted,
        predict_scratch,
        4,
        "first_predictor",
    )
    for step in range(STEPS):
        traces, edges = ahead[:5], ahead[5:]
        got = exchange(edges, sizes)
        base = call(
            functools.partial(inner_kernel, count, fields),
            [q, *traces, par, index, w_high, w_low, lift_table],
            [vmem] * 11,
            field_shape,
            face_scratch,
            1,
            "inner_update",
        )
        if step < STEPS - 1:
            q, *ahead = call(
                functools.partial(middle_kernel, count, fields, sizes),
                [*got, base, par, index, w_high, w_low, face_table, lift_table, cell_sm, flag_sm],
                [vmem] * (len(got) + 7) + [smem] * 2,
                [field_shape] + predicted,
                halo_scratch + predict_scratch,
                4,
                "outer_update_predictor",
            )
        else:
            out = call(
                functools.partial(last_kernel, count, fields, sizes),
                [*got, base, par, index, lift_table, cell_sm],
                [vmem] * (len(got) + 4) + [smem],
                shape((rows, nodes), F32),
                [pltpu.VMEM(field_shape.shape, F32)] * 2 + halo_scratch,
                1,
                "outer_update",
            )
    return out.reshape(fields, count, nodes).swapaxes(0, 1)[None, None, None]


def solution(mesh):
    sizes = tuple((axis, mesh.shape[axis]) for axis in mesh.axis_names)
    lead = ("gx", "gy", "ha")
    placed = (
        P(*lead, None, None, None),
        P(),
        P(*lead, None),
        P(*lead, None),
        P(*lead, None),
        P(*lead, None),
        P(*lead, None),
        P(*lead, None, None),
    )
    return jax.shard_map(
        functools.partial(shards, sizes),
        mesh=mesh,
        in_specs=placed,
        out_specs=P(*lead, None, None, None),
        check_vma=False,
    )
```

```python
import functools
import itertools
import math

import jax
import jax.numpy as jnp
from jax import lax
from jax.experimental import pallas as pl
from jax.experimental.pallas import tpu as pltpu
from jax.sharding import PartitionSpec as P

STEPS = 2
DT = 0.8
LIFT = 2.0
PICKED = ((0, 1, 2, 3, 6, 8), (0, 1, 2, 6, 4, 7), (0, 1, 2, 8, 7, 5))
F32 = jnp.float32
BF16 = jnp.bfloat16
VMEM_LIMIT = 24 << 20


def wide(column, count):
    return jnp.concatenate([column] * count, axis=1)


def get(field, rows, cols):
    return jnp.concatenate([field[t, rows, :] for t in range(cols.start // 128, cols.stop // 128)], axis=1)


def put(field, rows, cols, value):
    for t in range(cols.start // 128, cols.stop // 128):
        field[t, rows, :] = value[:, t * 128 - cols.start : (t + 1) * 128 - cols.start]


def add(field, rows, cols, value):
    put(field, rows, cols, get(field, rows, cols) + value)


def split(value):
    high = value.astype(BF16)
    return high, (value - high.astype(F32)).astype(BF16)


def dot(left, right):
    return jnp.dot(left, right, preferred_element_type=F32)


def lanes_of(rows):
    return lax.broadcasted_iota(jnp.int32, (rows, 128), 1)


def rate(high, low, w_high, w_low, par, stride, rows, emit, block=256):
    nodes = w_high.shape[-1]
    inv_rho = wide(par[0:rows], block // 128)
    lame = wide(par[stride : stride + rows], block // 128)
    shear = wide(par[2 * stride : 2 * stride + rows], block // 128)
    shear2 = 2.0 * shear
    for start in range(0, nodes, block):
        cols = slice(start, start + block)
        deriv = []
        for dim in range(3):
            top = jnp.concatenate([high[f * stride : f * stride + rows] for f in PICKED[dim]], axis=0)
            rest = jnp.concatenate([low[f * stride : f * stride + rows] for f in PICKED[dim]], axis=0)
            both = dot(jnp.concatenate([top, rest], axis=0), w_high[dim, :, cols])
            deriv.append(both[: 6 * rows] + both[6 * rows :] + dot(top, w_low[dim, :, cols]))
        part = lambda dim, row: deriv[dim][row * rows : (row + 1) * rows]
        div = lame * (part(0, 0) + part(1, 1) + part(2, 2))
        emit(0, cols, inv_rho * (part(0, 3) + part(1, 3) + part(2, 3)))
        emit(1, cols, inv_rho * (part(0, 4) + part(1, 4) + part(2, 4)))
        emit(2, cols, inv_rho * (part(0, 5) + part(1, 5) + part(2, 5)))
        emit(3, cols, div + shear2 * part(0, 0))
        emit(4, cols, div + shear2 * part(1, 1))
        emit(5, cols, div + shear2 * part(2, 2))
        emit(6, cols, shear * (part(0, 1) + part(1, 0)))
        emit(7, cols, shear * (part(1, 2) + part(2, 1)))
        emit(8, cols, shear * (part(0, 2) + part(2, 0)))


def correction(jump, par, count, dim, rows):
    take = lambda k: par[k * count : k * count + rows] if not isinstance(rows, slice) else par[
        k * count + rows.start : k * count + rows.stop
    ]
    inv_rho, lame, shear, half_speed = take(0), take(1), take(2), take(3)
    size = jump[0].shape[0]
    sign = jnp.where(lanes_of(size) < 64, -0.5, 0.5)
    inv_rho, lame, shear = sign * inv_rho, sign * lame, sign * shear
    stiff = lame + 2.0 * shear
    if dim == 0:
        flux = [inv_rho * jump[3], inv_rho * jump[6], inv_rho * jump[8]]
        flux += [stiff * jump[0], lame * jump[0], lame * jump[0]]
        flux += [shear * jump[1], None, shear * jump[2]]
    elif dim == 1:
        flux = [inv_rho * jump[6], inv_rho * jump[4], inv_rho * jump[7]]
        flux += [lame * jump[1], stiff * jump[1], lame * jump[1]]
        flux += [shear * jump[0], shear * jump[2], None]
    else:
        flux = [inv_rho * jump[8], inv_rho * jump[7], inv_rho * jump[5]]
        flux += [lame * jump[2], lame * jump[2], stiff * jump[2]]
        flux += [None, shear * jump[1], shear * jump[0]]
    return [
        half_speed * jump[f] if flux[f] is None else half_speed * jump[f] + flux[f] for f in range(len(jump))
    ]


def orient(value, index):
    return jnp.take_along_axis(value, index, axis=1, mode="promise_in_bounds")


def lift_edges(target, face, f, rows, count):
    lanes = lanes_of(face.shape[0])
    scaled = DT * LIFT * face
    top = slice(f * count + rows.start, f * count + rows.stop)
    last = target.shape[0] - 1
    target[0, top] = target[0, top] + jnp.where(lanes < 64, scaled, 0.0)
    target[last, top] = target[last, top] + jnp.where(lanes < 64, 0.0, scaled)


def lift_inner(target, face_high, face_low, lift_table):
    rows, nodes = target.shape[1], lift_table.shape[1]
    for start in range(0, nodes, 256):
        cols = slice(start, start + 256)
        lifted = dot(face_high[...], lift_table[:, cols]) + dot(face_low[...], lift_table[:, cols])
        add(target, slice(0, rows), cols, DT * LIFT * lifted)


def fetch(copies):
    started = [pltpu.make_async_copy(*copy) for copy in copies]
    for copy in started:
        copy.start()
    return started


def predict(count, fields, q, par, w_high, w_low, face_table, cell_sm, flag_sm, outs, scratch):
    int_high, int_low, trace_x, trace_y, trace_z, edge_x, edge_y, edge_z = outs
    h0, l0, h1, l1, total, second, packed, packed_par, series, hot_rows = scratch
    nodes = h0.shape[1]
    tiles_of_node = nodes // 128
    every = slice(0, nodes)
    for f in range(fields):
        rows = slice(f * count, (f + 1) * count)
        h0[rows], l0[rows] = split(get(q, rows, every))

    def first(f, cols, value):
        rows = slice(f * count, (f + 1) * count)
        put(total, rows, cols, get(q, rows, cols) + DT / 2.0 * value)
        h1[rows, cols], l1[rows, cols] = split(value)

    rate(h0, l0, w_high, w_low, par, count, count, first)

    def then(f, cols, value):
        rows = slice(f * count, (f + 1) * count)
        add(total, rows, cols, DT**2 / 6.0 * value)
        put(second, rows, cols, value)

    rate(h1, l1, w_high, w_low, par, count, count, then)

    slot = jnp.int32(0)
    for e in range(count):
        hot_rows[slot] = cell_sm[e]
        slot = slot + flag_sm[e]
    half = count // 2

    @pl.when(slot > 0)
    def _():
        for k in range(half):
            row = hot_rows[k]
            for t in range(tiles_of_node):
                packed[t, pl.ds(k, fields, stride=count), :] = second[t, pl.ds(row, fields, stride=count), :]
            packed_par[pl.ds(k, 3, stride=count), :] = par[pl.ds(row, 3, stride=count), :]
        for f in range(fields):
            rows = slice(f * count, f * count + half)
            h0[rows], l0[rows] = split(get(packed, rows, every))
        buffers = [(h0, l0), (h1, l1)]
        for order in (3, 4, 5):
            weight = DT**order / math.factorial(order + 1)
            source, target = buffers[(order - 3) % 2], buffers[(order - 2) % 2]

            def more(f, cols, value, order=order, weight=weight, target=target):
                rows = slice(f * count, f * count + half)
                (put if order == 3 else add)(series, rows, cols, weight * value)
                if order < 5:
                    target[0][rows, cols], target[1][rows, cols] = split(value)

            rate(source[0], source[1], w_high, w_low, packed_par, count, half, more)
        for k in range(half):
            row = hot_rows[k]
            spot = pl.ds(row, fields, stride=count)
            for t in range(tiles_of_node):
                total[t, spot, :] = total[t, spot, :] + series[t, pl.ds(k, fields, stride=count), :]

    for f in range(fields):
        rows = slice(f * count, (f + 1) * count)
        int_high[rows], int_low[rows] = split(get(total, rows, every))
        trace_x[rows] = jnp.where(lanes_of(count) < 64, total[0, rows], total[tiles_of_node - 1, rows])
    faces = dot(int_high[...], face_table[...]) + dot(int_low[...], face_table[...])
    trace_y[...] = faces[:, 0:128]
    trace_z[...] = faces[:, 128:256]
    for f in range(fields):
        edge_x[f * 8 : f * 8 + 8] = jnp.where(
            lanes_of(8) < 64, trace_x[f * count : f * count + 8], trace_x[(f + 1) * count - 8 : (f + 1) * count]
        )
    tiles = fields * count // 8
    minus = lanes_of(tiles) < 64
    pad = edge_y.shape[0] // 2
    for m in range(2):
        edge_y[m * pad : m * pad + tiles] = jnp.where(
            minus, trace_y[pl.ds(m, tiles, stride=8), :], trace_y[pl.ds(6 + m, tiles, stride=8), :]
        )
        if pad > tiles:
            edge_y[m * pad + tiles : (m + 1) * pad] = jnp.zeros((pad - tiles, 128), F32)
    pairs = fields * count // 2
    edge_z[...] = jnp.where(
        lanes_of(pairs) < 64, trace_z[pl.ds(0, pairs, stride=2), :], trace_z[pl.ds(1, pairs, stride=2), :]
    )


def inner(count, fields, q, int_high, int_low, trace_x, trace_y, trace_z, par, index, w_high, w_low, lift_table,
          base, face_high, face_low):
    def volume(f, cols, value):
        rows = slice(f * count, (f + 1) * count)
        put(base, rows, cols, get(q, rows, cols) + DT * value)

    rate(int_high, int_low, w_high, w_low, par, count, count, volume)
    lanes = lanes_of(count)
    sub = lax.broadcasted_iota(jnp.int32, (count, 128), 0)
    minus = lanes < 64
    zero = jnp.zeros((8, 128), F32)
    for dim, trace in enumerate((trace_x, trace_y, trace_z)):
        jump = []
        for f in range(fields):
            own = trace[f * count : (f + 1) * count]
            if dim == 0:
                above = jnp.concatenate([own[8:], zero], axis=0)
                below = jnp.concatenate([zero, own[:-8]], axis=0)
            elif dim == 1:
                above = jnp.where(sub % 8 < 6, pltpu.roll(own, count - 2, 0), 0.0)
                below = jnp.where(sub % 8 < 2, 0.0, pltpu.roll(own, 2, 0))
            else:
                above = jnp.where(sub % 2 < 1, pltpu.roll(own, count - 1, 0), 0.0)
                below = jnp.where(sub % 2 < 1, 0.0, pltpu.roll(own, 1, 0))
            beside = jnp.where(minus, above, below)
            jump.append(orient(beside, index[dim * count : (dim + 1) * count]) - own)
        fixed = correction(jump, par, count, dim, count)
        for f in range(fields):
            if dim == 0:
                lift_edges(base, fixed[f], f, slice(0, count), count)
            else:
                cols = slice((dim - 1) * 128, dim * 128)
                rows = slice(f * count, (f + 1) * count)
                face_high[rows, cols], face_low[rows, cols] = split(fixed[f])
    lift_inner(base, face_high, face_low, lift_table)


def outer(count, fields, sizes, got, base, par, index, lift_table, out, halo, face_high, face_low):
    lower, upper = [], []
    for dim, (axis, size) in enumerate(sizes):
        here = lax.axis_index(axis)
        odd = here % 2 == 1
        first, second = got[dim]
        second = first if second is None else second
        lower.append((jnp.logical_and(odd, here > 0) if size == 2 else None, odd, here > 0, first, second))
        upper.append((None, odd, here < size - 1, first, second))

    def from_lower(dim, rows, minus):
        _, odd, there, first, second = lower[dim]
        value = jnp.where(odd, first[rows], second[rows])
        return jnp.where(jnp.logical_and(there, jnp.logical_not(minus)), value, 0.0)

    def from_upper(dim, rows, minus):
        _, odd, there, first, second = upper[dim]
        value = jnp.where(odd, second[rows], first[rows])
        return jnp.where(jnp.logical_and(there, minus), value, 0.0)

    out[...] = base[...]
    minus8 = lanes_of(8) < 64
    for end in range(2):
        rows = slice(0, 8) if end == 0 else slice(count - 8, count)
        jump = []
        for f in range(fields):
            here = slice(f * 8, f * 8 + 8)
            value = from_lower(0, here, minus8) if end == 0 else from_upper(0, here, minus8)
            jump.append(orient(value, index[rows]))
        fixed = correction(jump, par, count, 0, rows)
        for f in range(fields):
            lift_edges(out, fixed[f], f, rows, count)
    tiles = fields * count // 8
    pad = got[1][0].shape[0] // 2
    pairs = fields * count // 2
    for dim in (1, 2):
        if dim == 1:
            halo[...] = jnp.zeros_like(halo)
            minus = lanes_of(tiles) < 64
            for m in range(2):
                here = slice(m * pad, m * pad + tiles)
                halo[pl.ds(m, tiles, stride=8), :] = from_lower(1, here, minus)
                halo[pl.ds(6 + m, tiles, stride=8), :] = from_upper(1, here, minus)
        else:
            minus = lanes_of(pairs) < 64
            halo[pl.ds(0, pairs, stride=2), :] = from_lower(2, slice(0, pairs), minus)
            halo[pl.ds(1, pairs, stride=2), :] = from_upper(2, slice(0, pairs), minus)
        jump = [
            orient(halo[f * count : (f + 1) * count], index[dim * count : (dim + 1) * count]) for f in range(fields)
        ]
        fixed = correction(jump, par, count, dim, count)
        for f in range(fields):
            cols = slice((dim - 1) * 128, dim * 128)
            rows = slice(f * count, (f + 1) * count)
            face_high[rows, cols], face_low[rows, cols] = split(fixed[f])
    lift_inner(out, face_high, face_low, lift_table)


def first_kernel(count, fields, wave, ops_any, density_any, lame_any, shear_any, cell_any, orient_any, cells_any,
                 flags_any, q, w_high, w_low, par, index, face_table, lift_table, *rest):
    outs, scratch = rest[:8], rest[8:18]
    ops, density, lame, shear, cell, orient_code, cell_sm, flag_sm, sems = rest[18:]
    staged = scratch[4]
    tiles_of_node = q.shape[0]
    pairs = [(density_any, density), (lame_any, lame), (shear_any, shear), (cell_any, cell)]
    pairs += [(orient_any, orient_code), (cells_any, cell_sm), (flags_any, flag_sm)]
    pairs += [(wave.at[:, t * 128 : (t + 1) * 128], staged.at[t]) for t in range(tiles_of_node)]
    pairs += [(ops_any.at[dim], ops.at[dim]) for dim in range(3)]
    waits = fetch([(*pair, sems.at[k]) for k, pair in enumerate(pairs)])
    for wait in waits[:7]:
        wait.wait()
    fills = cell[...] == lax.broadcasted_iota(jnp.int32, (count, count), 0)
    in_cell = lambda row: jnp.broadcast_to(
        jnp.sum(jnp.where(fills, row, 0.0), axis=1, keepdims=True), (count, 128)
    )
    inv_rho = in_cell(1.0 / density[...])
    lame_col = in_cell(lame[...])
    shear_col = in_cell(shear[...])
    par[0:count] = inv_rho
    par[count : 2 * count] = lame_col
    par[2 * count : 3 * count] = shear_col
    par[3 * count : 4 * count] = 0.5 * jnp.sqrt((lame_col + 2.0 * shear_col) * inv_rho)
    lanes = lanes_of(count)
    p_lane, r_lane = lanes % 64 // 8, lanes % 8
    for dim in range(3):
        code = jnp.where(
            lanes < 64,
            in_cell(orient_code[2 * dim].astype(F32)),
            in_cell(orient_code[2 * dim + 1].astype(F32)),
        ).astype(jnp.int32)
        p_from = jnp.where(code % 2 == 1, 7 - p_lane, p_lane)
        r_from = jnp.where(code // 2 % 2 == 1, 7 - r_lane, r_lane)
        source = jnp.where(code >= 4, r_from * 8 + p_from, p_from * 8 + r_from)
        index[dim * count : (dim + 1) * count] = source + jnp.where(lanes < 64, 64, 0)

    def on_face(node, column):
        i, j, k = node // 64, node // 8 % 8, node % 8
        plus = column // 64 % 2 * 7
        p, r = column % 64 // 8, column % 8
        along_y = (column < 128) & (j == plus) & (i == p) & (k == r)
        along_z = (column >= 128) & (k == plus) & (i == p) & (j == r)
        return jnp.where(along_y | along_z, 1.0, 0.0).astype(BF16)

    table = (face_table.shape[0], face_table.shape[1])
    face_table[...] = on_face(lax.broadcasted_iota(jnp.int32, table, 0), lax.broadcasted_iota(jnp.int32, table, 1))
    table = table[::-1]
    lift_table[...] = on_face(lax.broadcasted_iota(jnp.int32, table, 1), lax.broadcasted_iota(jnp.int32, table, 0))
    for wait in waits[7 : 7 + tiles_of_node]:
        wait.wait()
    for e in range(count):
        for t in range(tiles_of_node):
            q[t, pl.ds(cell_sm[e], fields, stride=count), :] = staged[t, pl.ds(e, fields, stride=count), :]
    for dim in range(3):
        waits[7 + tiles_of_node + dim].wait()
        for start in range(0, ops.shape[1], 128):
            rows = slice(start, start + 128)
            w_high[dim, rows, :], w_low[dim, rows, :] = split(ops[dim, rows, :])
    predict(count, fields, q, par, w_high, w_low, face_table, cell_sm, flag_sm, outs, scratch)


def inner_kernel(count, fields, *refs):
    inner(count, fields, *refs)


def unpack_got(sizes, refs):
    got, at = [], 0
    for _, size in sizes:
        pair = [None, None]
        for k in range(1 if size == 2 else 2):
            pair[k] = refs[at]
            at += 1
        got.append(pair)
    return got, refs[at:]


def middle_kernel(count, fields, sizes, *refs):
    got, refs = unpack_got(sizes, refs)
    base, par, index, w_high, w_low, face_table, lift_table, cells_any, flags_any = refs[:9]
    q, outs = refs[9], refs[10:18]
    halo, face_high, face_low = refs[18:21]
    scratch, (cell_sm, flag_sm, sems) = refs[21:31], refs[31:]
    waits = fetch([(cells_any, cell_sm, sems.at[0]), (flags_any, flag_sm, sems.at[1])])
    outer(count, fields, sizes, got, base, par, index, lift_table, q, halo, face_high, face_low)
    for wait in waits:
        wait.wait()
    predict(count, fields, q, par, w_high, w_low, face_table, cell_sm, flag_sm, outs, scratch)


def last_kernel(count, fields, sizes, *refs):
    got, refs = unpack_got(sizes, refs)
    base, par, index, lift_table, cells_any, out, q, staged, halo, face_high, face_low, cell_sm, sems = refs
    tiles_of_node = q.shape[0]
    waits = fetch([(cells_any, cell_sm, sems.at[tiles_of_node])])
    outer(count, fields, sizes, got, base, par, index, lift_table, q, halo, face_high, face_low)
    waits[0].wait()
    done = []
    for t in range(tiles_of_node):
        for e in range(count):
            staged[t, pl.ds(e, fields, stride=count), :] = q[t, pl.ds(cell_sm[e], fields, stride=count), :]
        done += fetch([(staged.at[t], out.at[:, t * 128 : (t + 1) * 128], sems.at[t])])
    for wait in done:
        wait.wait()


def swaps(sizes, dim, parity):
    lengths = [size for _, size in sizes]
    size, pairs = lengths[dim], []
    for place in itertools.product(*[range(length) for length in lengths]):
        other = list(place)
        other[dim] += 1 if place[dim] % 2 == parity else -1
        if not 0 <= other[dim] < size:
            if dim == 0 and lengths[1] % 2 == 0:
                other[dim], other[1] = place[dim], place[1] ^ 1
            else:
                other[dim] = other[dim] % size if size % 2 == 0 else place[dim]
        flat = [0, 0]
        for length, mine, theirs in zip(lengths, place, other):
            flat = [flat[0] * length + mine, flat[1] * length + theirs]
        pairs.append(tuple(flat))
    return pairs


def exchange(edges, sizes):
    axes = tuple(axis for axis, _ in sizes)
    got = []
    for dim, edge in enumerate(edges):
        for parity in range(1 if sizes[dim][1] == 2 else 2):
            got.append(lax.ppermute(edge, axes, swaps(sizes, dim, parity)))
    return got


def shards(sizes, wavefield, deriv_ops, density, lame_first, shear_modulus, high_order, element_cell, face_orient):
    count, fields, nodes = wavefield.shape[-3:]
    rows = fields * count
    wave = wavefield[0, 0, 0].swapaxes(0, 1).reshape(rows, nodes)
    row = lambda value: value.reshape(1, count)
    cell_sm = element_cell.reshape(count)
    flag_sm = high_order.reshape(count)
    codes = face_orient.reshape(6, 1, count)
    vmem = pl.BlockSpec(memory_space=pltpu.VMEM)
    hbm = pl.BlockSpec(memory_space=pltpu.HBM)
    index_scratch = pltpu.SMEM((count,), jnp.int32)
    shape = jax.ShapeDtypeStruct
    field_shape = shape((nodes // 128, rows, 128), F32)
    pad = -(-(rows // 8) // 8) * 8
    predicted = [
        shape((rows, nodes), BF16),
        shape((rows, nodes), BF16),
        shape((rows, 128), F32),
        shape((rows, 128), F32),
        shape((rows, 128), F32),
        shape((fields * 8, 128), F32),
        shape((2 * pad, 128), F32),
        shape((rows // 2, 128), F32),
    ]
    predict_scratch = [
        pltpu.VMEM((rows, nodes), BF16),
        pltpu.VMEM((rows, nodes), BF16),
        pltpu.VMEM((rows, nodes), BF16),
        pltpu.VMEM((rows, nodes), BF16),
        pltpu.VMEM(field_shape.shape, F32),
        pltpu.VMEM(field_shape.shape, F32),
        pltpu.VMEM(field_shape.shape, F32),
        pltpu.VMEM((3 * count, 128), F32),
        pltpu.VMEM(field_shape.shape, F32),
        pltpu.SMEM((count + 1,), jnp.int32),
    ]
    face_scratch = [pltpu.VMEM((rows, 256), BF16), pltpu.VMEM((rows, 256), BF16)]
    halo_scratch = [pltpu.VMEM((rows, 128), F32)] + face_scratch
    params = pltpu.CompilerParams(vmem_limit_bytes=VMEM_LIMIT)

    def call(kernel, operands, in_specs, out_shape, scratch, products, name, out_spec=vmem):
        single = not isinstance(out_shape, list)
        return pl.pallas_call(
            kernel,
            out_shape=out_shape,
            in_specs=in_specs,
            out_specs=out_spec if single else [out_spec] * len(out_shape),
            scratch_shapes=scratch,
            compiler_params=params,
            cost_estimate=pl.CostEstimate(
                flops=products * 6 * rows * nodes * nodes * 4, bytes_accessed=4 * rows * nodes * 4, transcendentals=0
            ),
            name=name,
        )(*operands)

    q, w_high, w_low, par, index, face_table, lift_table, *ahead = call(
        functools.partial(first_kernel, count, fields),
        [wave, deriv_ops, row(density), row(lame_first), row(shear_modulus), row(element_cell), codes, cell_sm, flag_sm],
        [hbm] * 9,
        [
            field_shape,
            shape(deriv_ops.shape, BF16),
            shape(deriv_ops.shape, BF16),
            shape((4 * count, 128), F32),
            shape((3 * count, 128), jnp.int32),
            shape((nodes, 256), BF16),
            shape((256, nodes), BF16),
        ]
        + predicted,
        predict_scratch
        + [
            pltpu.VMEM(deriv_ops.shape, F32),
            pltpu.VMEM((1, count), F32),
            pltpu.VMEM((1, count), F32),
            pltpu.VMEM((1, count), F32),
            pltpu.VMEM((1, count), jnp.int32),
            pltpu.VMEM((6, 1, count), jnp.int32),
            index_scratch,
            index_scratch,
            pltpu.SemaphoreType.DMA((10 + nodes // 128,)),
        ],
        4,
        "first_predictor",
    )
    for step in range(STEPS):
        traces, edges = ahead[:5], ahead[5:]
        got = exchange(edges, sizes)
        base = call(
            functools.partial(inner_kernel, count, fields),
            [q, *traces, par, index, w_high, w_low, lift_table],
            [vmem] * 11,
            field_shape,
            face_scratch,
            1,
            "inner_update",
        )
        if step < STEPS - 1:
            q, *ahead = call(
                functools.partial(middle_kernel, count, fields, sizes),
                [*got, base, par, index, w_high, w_low, face_table, lift_table, cell_sm, flag_sm],
                [vmem] * (len(got) + 7) + [hbm] * 2,
                [field_shape] + predicted,
                halo_scratch + predict_scratch + [index_scratch, index_scratch, pltpu.SemaphoreType.DMA((2,))],
                4,
                "outer_update_predictor",
            )
        else:
            out = call(
                functools.partial(last_kernel, count, fields, sizes),
                [*got, base, par, index, lift_table, cell_sm],
                [vmem] * (len(got) + 4) + [hbm],
                shape((rows, nodes), F32),
                [pltpu.VMEM(field_shape.shape, F32)] * 2
                + halo_scratch
                + [index_scratch, pltpu.SemaphoreType.DMA((nodes // 128 + 1,))],
                1,
                "outer_update",
                hbm,
            )
    return out.reshape(fields, count, nodes).swapaxes(0, 1)[None, None, None]


def solution(mesh):
    sizes = tuple((axis, mesh.shape[axis]) for axis in mesh.axis_names)
    lead = ("gx", "gy", "ha")
    placed = (
        P(*lead, None, None, None),
        P(),
        P(*lead, None),
        P(*lead, None),
        P(*lead, None),
        P(*lead, None),
        P(*lead, None),
        P(*lead, None, None),
    )
    return jax.shard_map(
        functools.partial(shards, sizes),
        mesh=mesh,
        in_specs=placed,
        out_specs=P(*lead, None, None, None),
        check_vma=False,
    )
```

```python
import functools
import itertools
import math

import jax
import jax.numpy as jnp
from jax import lax
from jax.experimental import pallas as pl
from jax.experimental.pallas import tpu as pltpu
from jax.sharding import PartitionSpec as P

STEPS = 2
DT = 0.8
LIFT = 2.0
PICKED = ((0, 1, 2, 3, 6, 8), (0, 1, 2, 6, 4, 7), (0, 1, 2, 8, 7, 5))
F32 = jnp.float32
BF16 = jnp.bfloat16
VMEM_LIMIT = 24 << 20
TABLE_LIMIT = 50 << 20


def wide(column, count):
    return jnp.concatenate([column] * count, axis=1)


def get(field, rows, cols):
    return jnp.concatenate([field[t, rows, :] for t in range(cols.start // 128, cols.stop // 128)], axis=1)


def put(field, rows, cols, value):
    for t in range(cols.start // 128, cols.stop // 128):
        field[t, rows, :] = value[:, t * 128 - cols.start : (t + 1) * 128 - cols.start]


def add(field, rows, cols, value):
    put(field, rows, cols, get(field, rows, cols) + value)


def split(value):
    high = value.astype(BF16)
    return high, (value - high.astype(F32)).astype(BF16)


def dot(left, right):
    return jnp.dot(left, right, preferred_element_type=F32)


def lanes_of(rows):
    return lax.broadcasted_iota(jnp.int32, (rows, 128), 1)


def rate(high, low, w_high, w_low, par, stride, rows, emit, block=256):
    nodes = w_high.shape[-1]
    inv_rho = wide(par[0:rows], block // 128)
    lame = wide(par[stride : stride + rows], block // 128)
    shear = wide(par[2 * stride : 2 * stride + rows], block // 128)
    shear2 = 2.0 * shear
    for start in range(0, nodes, block):
        cols = slice(start, start + block)
        deriv = []
        for dim in range(3):
            top = jnp.concatenate([high[f * stride : f * stride + rows] for f in PICKED[dim]], axis=0)
            rest = jnp.concatenate([low[f * stride : f * stride + rows] for f in PICKED[dim]], axis=0)
            both = dot(jnp.concatenate([top, rest], axis=0), w_high[dim, :, cols])
            deriv.append(both[: 6 * rows] + both[6 * rows :] + dot(top, w_low[dim, :, cols]))
        part = lambda dim, row: deriv[dim][row * rows : (row + 1) * rows]
        div = lame * (part(0, 0) + part(1, 1) + part(2, 2))
        emit(0, cols, inv_rho * (part(0, 3) + part(1, 3) + part(2, 3)))
        emit(1, cols, inv_rho * (part(0, 4) + part(1, 4) + part(2, 4)))
        emit(2, cols, inv_rho * (part(0, 5) + part(1, 5) + part(2, 5)))
        emit(3, cols, div + shear2 * part(0, 0))
        emit(4, cols, div + shear2 * part(1, 1))
        emit(5, cols, div + shear2 * part(2, 2))
        emit(6, cols, shear * (part(0, 1) + part(1, 0)))
        emit(7, cols, shear * (part(1, 2) + part(2, 1)))
        emit(8, cols, shear * (part(0, 2) + part(2, 0)))


def correction(jump, par, count, dim, rows):
    take = lambda k: par[k * count : k * count + rows] if not isinstance(rows, slice) else par[
        k * count + rows.start : k * count + rows.stop
    ]
    inv_rho, lame, shear, half_speed = take(0), take(1), take(2), take(3)
    size = jump[0].shape[0]
    sign = jnp.where(lanes_of(size) < 64, -0.5, 0.5)
    inv_rho, lame, shear = sign * inv_rho, sign * lame, sign * shear
    stiff = lame + 2.0 * shear
    if dim == 0:
        flux = [inv_rho * jump[3], inv_rho * jump[6], inv_rho * jump[8]]
        flux += [stiff * jump[0], lame * jump[0], lame * jump[0]]
        flux += [shear * jump[1], None, shear * jump[2]]
    elif dim == 1:
        flux = [inv_rho * jump[6], inv_rho * jump[4], inv_rho * jump[7]]
        flux += [lame * jump[1], stiff * jump[1], lame * jump[1]]
        flux += [shear * jump[0], shear * jump[2], None]
    else:
        flux = [inv_rho * jump[8], inv_rho * jump[7], inv_rho * jump[5]]
        flux += [lame * jump[2], lame * jump[2], stiff * jump[2]]
        flux += [None, shear * jump[1], shear * jump[0]]
    return [
        half_speed * jump[f] if flux[f] is None else half_speed * jump[f] + flux[f] for f in range(len(jump))
    ]


def orient(value, index):
    return jnp.take_along_axis(value, index, axis=1, mode="promise_in_bounds")


def lift_edges(target, face, f, rows, count):
    lanes = lanes_of(face.shape[0])
    scaled = DT * LIFT * face
    top = slice(f * count + rows.start, f * count + rows.stop)
    last = target.shape[0] - 1
    target[0, top] = target[0, top] + jnp.where(lanes < 64, scaled, 0.0)
    target[last, top] = target[last, top] + jnp.where(lanes < 64, 0.0, scaled)


def lift_inner(target, face_high, face_low, lift_table):
    rows, nodes = target.shape[1], lift_table.shape[1]
    for start in range(0, nodes, 256):
        cols = slice(start, start + 256)
        lifted = dot(face_high[...], lift_table[:, cols]) + dot(face_low[...], lift_table[:, cols])
        add(target, slice(0, rows), cols, DT * LIFT * lifted)


def fetch(copies):
    started = [pltpu.make_async_copy(*copy) for copy in copies]
    for copy in started:
        copy.start()
    return started


def predict(count, fields, q, par, w_high, w_low, face_table, cell_sm, flag_sm, outs, scratch):
    int_high, int_low, trace_x, trace_y, trace_z, edge_x, edge_y, edge_z = outs
    h0, l0, h1, l1, total, second, packed, packed_par, series, hot_rows = scratch
    nodes = h0.shape[1]
    tiles_of_node = nodes // 128
    every = slice(0, nodes)
    for f in range(fields):
        rows = slice(f * count, (f + 1) * count)
        h0[rows], l0[rows] = split(get(q, rows, every))

    def first(f, cols, value):
        rows = slice(f * count, (f + 1) * count)
        put(total, rows, cols, get(q, rows, cols) + DT / 2.0 * value)
        h1[rows, cols], l1[rows, cols] = split(value)

    rate(h0, l0, w_high, w_low, par, count, count, first)

    def then(f, cols, value):
        rows = slice(f * count, (f + 1) * count)
        add(total, rows, cols, DT**2 / 6.0 * value)
        put(second, rows, cols, value)

    rate(h1, l1, w_high, w_low, par, count, count, then)

    slot = jnp.int32(0)
    for e in range(count):
        hot_rows[slot] = cell_sm[e]
        slot = slot + flag_sm[e]
    half = count // 2

    @pl.when(slot > 0)
    def _():
        for k in range(half):
            row = hot_rows[k]
            for t in range(tiles_of_node):
                packed[t, pl.ds(k, fields, stride=count), :] = second[t, pl.ds(row, fields, stride=count), :]
            packed_par[pl.ds(k, 3, stride=count), :] = par[pl.ds(row, 3, stride=count), :]
        for f in range(fields):
            rows = slice(f * count, f * count + half)
            h0[rows], l0[rows] = split(get(packed, rows, every))
        buffers = [(h0, l0), (h1, l1)]
        for order in (3, 4, 5):
            weight = DT**order / math.factorial(order + 1)
            source, target = buffers[(order - 3) % 2], buffers[(order - 2) % 2]

            def more(f, cols, value, order=order, weight=weight, target=target):
                rows = slice(f * count, f * count + half)
                (put if order == 3 else add)(series, rows, cols, weight * value)
                if order < 5:
                    target[0][rows, cols], target[1][rows, cols] = split(value)

            rate(source[0], source[1], w_high, w_low, packed_par, count, half, more)
        for k in range(half):
            row = hot_rows[k]
            spot = pl.ds(row, fields, stride=count)
            for t in range(tiles_of_node):
                total[t, spot, :] = total[t, spot, :] + series[t, pl.ds(k, fields, stride=count), :]

    for f in range(fields):
        rows = slice(f * count, (f + 1) * count)
        int_high[rows], int_low[rows] = split(get(total, rows, every))
        trace_x[rows] = jnp.where(lanes_of(count) < 64, total[0, rows], total[tiles_of_node - 1, rows])
    faces = dot(int_high[...], face_table[...]) + dot(int_low[...], face_table[...])
    trace_y[...] = faces[:, 0:128]
    trace_z[...] = faces[:, 128:256]
    for f in range(fields):
        edge_x[f * 8 : f * 8 + 8] = jnp.where(
            lanes_of(8) < 64, trace_x[f * count : f * count + 8], trace_x[(f + 1) * count - 8 : (f + 1) * count]
        )
    tiles = fields * count // 8
    minus = lanes_of(tiles) < 64
    pad = edge_y.shape[0] // 2
    for m in range(2):
        edge_y[m * pad : m * pad + tiles] = jnp.where(
            minus, trace_y[pl.ds(m, tiles, stride=8), :], trace_y[pl.ds(6 + m, tiles, stride=8), :]
        )
        if pad > tiles:
            edge_y[m * pad + tiles : (m + 1) * pad] = jnp.zeros((pad - tiles, 128), F32)
    pairs = fields * count // 2
    edge_z[...] = jnp.where(
        lanes_of(pairs) < 64, trace_z[pl.ds(0, pairs, stride=2), :], trace_z[pl.ds(1, pairs, stride=2), :]
    )


def inner(count, fields, q, int_high, int_low, trace_x, trace_y, trace_z, par, index, w_high, w_low, lift_table,
          base, face_high, face_low):
    def volume(f, cols, value):
        rows = slice(f * count, (f + 1) * count)
        put(base, rows, cols, get(q, rows, cols) + DT * value)

    rate(int_high, int_low, w_high, w_low, par, count, count, volume)
    lanes = lanes_of(count)
    sub = lax.broadcasted_iota(jnp.int32, (count, 128), 0)
    minus = lanes < 64
    zero = jnp.zeros((8, 128), F32)
    for dim, trace in enumerate((trace_x, trace_y, trace_z)):
        jump = []
        for f in range(fields):
            own = trace[f * count : (f + 1) * count]
            if dim == 0:
                above = jnp.concatenate([own[8:], zero], axis=0)
                below = jnp.concatenate([zero, own[:-8]], axis=0)
            elif dim == 1:
                above = jnp.where(sub % 8 < 6, pltpu.roll(own, count - 2, 0), 0.0)
                below = jnp.where(sub % 8 < 2, 0.0, pltpu.roll(own, 2, 0))
            else:
                above = jnp.where(sub % 2 < 1, pltpu.roll(own, count - 1, 0), 0.0)
                below = jnp.where(sub % 2 < 1, 0.0, pltpu.roll(own, 1, 0))
            beside = jnp.where(minus, above, below)
            jump.append(orient(beside, index[dim * count : (dim + 1) * count]) - own)
        fixed = correction(jump, par, count, dim, count)
        for f in range(fields):
            if dim == 0:
                lift_edges(base, fixed[f], f, slice(0, count), count)
            else:
                cols = slice((dim - 1) * 128, dim * 128)
                rows = slice(f * count, (f + 1) * count)
                face_high[rows, cols], face_low[rows, cols] = split(fixed[f])
    lift_inner(base, face_high, face_low, lift_table)


def outer(count, fields, sizes, got, base, par, index, lift_table, out, halo, face_high, face_low):
    lower, upper = [], []
    for dim, (axis, size) in enumerate(sizes):
        here = lax.axis_index(axis)
        odd = here % 2 == 1
        first, second = got[dim]
        second = first if second is None else second
        lower.append((jnp.logical_and(odd, here > 0) if size == 2 else None, odd, here > 0, first, second))
        upper.append((None, odd, here < size - 1, first, second))

    def from_lower(dim, rows, minus):
        _, odd, there, first, second = lower[dim]
        value = jnp.where(odd, first[rows], second[rows])
        return jnp.where(jnp.logical_and(there, jnp.logical_not(minus)), value, 0.0)

    def from_upper(dim, rows, minus):
        _, odd, there, first, second = upper[dim]
        value = jnp.where(odd, second[rows], first[rows])
        return jnp.where(jnp.logical_and(there, minus), value, 0.0)

    out[...] = base[...]
    minus8 = lanes_of(8) < 64
    for end in range(2):
        rows = slice(0, 8) if end == 0 else slice(count - 8, count)
        jump = []
        for f in range(fields):
            here = slice(f * 8, f * 8 + 8)
            value = from_lower(0, here, minus8) if end == 0 else from_upper(0, here, minus8)
            jump.append(orient(value, index[rows]))
        fixed = correction(jump, par, count, 0, rows)
        for f in range(fields):
            lift_edges(out, fixed[f], f, rows, count)
    tiles = fields * count // 8
    pad = got[1][0].shape[0] // 2
    pairs = fields * count // 2
    for dim in (1, 2):
        if dim == 1:
            halo[...] = jnp.zeros_like(halo)
            minus = lanes_of(tiles) < 64
            for m in range(2):
                here = slice(m * pad, m * pad + tiles)
                halo[pl.ds(m, tiles, stride=8), :] = from_lower(1, here, minus)
                halo[pl.ds(6 + m, tiles, stride=8), :] = from_upper(1, here, minus)
        else:
            minus = lanes_of(pairs) < 64
            halo[pl.ds(0, pairs, stride=2), :] = from_lower(2, slice(0, pairs), minus)
            halo[pl.ds(1, pairs, stride=2), :] = from_upper(2, slice(0, pairs), minus)
        jump = [
            orient(halo[f * count : (f + 1) * count], index[dim * count : (dim + 1) * count]) for f in range(fields)
        ]
        fixed = correction(jump, par, count, dim, count)
        for f in range(fields):
            cols = slice((dim - 1) * 128, dim * 128)
            rows = slice(f * count, (f + 1) * count)
            face_high[rows, cols], face_low[rows, cols] = split(fixed[f])
    lift_inner(out, face_high, face_low, lift_table)


def table_kernel(ops_any, w_high, w_low, face_table, lift_table, ops, sems):
    dims, nodes = ops.shape[:2]
    step = nodes // 2
    parts = [(dim, slice(start, start + step)) for dim in range(dims) for start in range(0, nodes, step)]
    waits = fetch([(ops_any.at[dim, rows], ops.at[dim, rows], sems.at[k]) for k, (dim, rows) in enumerate(parts)])

    def on_face(node, column):
        i, j, k = node // 64, node // 8 % 8, node % 8
        plus = column // 64 % 2 * 7
        p, r = column % 64 // 8, column % 8
        along_y = (column < 128) & (j == plus) & (i == p) & (k == r)
        along_z = (column >= 128) & (k == plus) & (i == p) & (j == r)
        return jnp.where(along_y | along_z, 1.0, 0.0).astype(BF16)

    table = face_table.shape
    face_table[...] = on_face(lax.broadcasted_iota(jnp.int32, table, 0), lax.broadcasted_iota(jnp.int32, table, 1))
    table = table[::-1]
    lift_table[...] = on_face(lax.broadcasted_iota(jnp.int32, table, 1), lax.broadcasted_iota(jnp.int32, table, 0))
    for wait, (dim, rows) in zip(waits, parts):
        wait.wait()
        w_high[dim, rows, :], w_low[dim, rows, :] = split(ops[dim, rows, :])


def first_kernel(count, fields, wave, density, lame, shear, cell, orient_code, cells_any, flags_any,
                 w_high, w_low, face_table, q, par, index, *rest):
    outs, scratch = rest[:8], rest[8:18]
    cell_sm, flag_sm, sems = rest[18:]
    waits = fetch([(cells_any, cell_sm, sems.at[0]), (flags_any, flag_sm, sems.at[1])])
    staged = scratch[4]
    put(staged, slice(0, fields * count), slice(0, wave.shape[1]), wave[...])
    fills = cell[...] == lax.broadcasted_iota(jnp.int32, (count, count), 0)
    in_cell = lambda row: jnp.broadcast_to(
        jnp.sum(jnp.where(fills, row, 0.0), axis=1, keepdims=True), (count, 128)
    )
    inv_rho = in_cell(1.0 / density[...])
    lame_col = in_cell(lame[...])
    shear_col = in_cell(shear[...])
    par[0:count] = inv_rho
    par[count : 2 * count] = lame_col
    par[2 * count : 3 * count] = shear_col
    par[3 * count : 4 * count] = 0.5 * jnp.sqrt((lame_col + 2.0 * shear_col) * inv_rho)
    lanes = lanes_of(count)
    p_lane, r_lane = lanes % 64 // 8, lanes % 8
    for dim in range(3):
        code = jnp.where(
            lanes < 64,
            in_cell(orient_code[2 * dim].astype(F32)),
            in_cell(orient_code[2 * dim + 1].astype(F32)),
        ).astype(jnp.int32)
        p_from = jnp.where(code % 2 == 1, 7 - p_lane, p_lane)
        r_from = jnp.where(code // 2 % 2 == 1, 7 - r_lane, r_lane)
        source = jnp.where(code >= 4, r_from * 8 + p_from, p_from * 8 + r_from)
        index[dim * count : (dim + 1) * count] = source + jnp.where(lanes < 64, 64, 0)
    for wait in waits:
        wait.wait()
    for e in range(count):
        for t in range(q.shape[0]):
            q[t, pl.ds(cell_sm[e], fields, stride=count), :] = staged[t, pl.ds(e, fields, stride=count), :]
    predict(count, fields, q, par, w_high, w_low, face_table, cell_sm, flag_sm, outs, scratch)


def inner_kernel(count, fields, *refs):
    inner(count, fields, *refs)


def unpack_got(sizes, refs):
    got, at = [], 0
    for _, size in sizes:
        pair = [None, None]
        for k in range(1 if size == 2 else 2):
            pair[k] = refs[at]
            at += 1
        got.append(pair)
    return got, refs[at:]


def middle_kernel(count, fields, sizes, *refs):
    got, refs = unpack_got(sizes, refs)
    base, par, index, w_high, w_low, face_table, lift_table, cells_any, flags_any = refs[:9]
    q, outs = refs[9], refs[10:18]
    halo, face_high, face_low = refs[18:21]
    scratch, (cell_sm, flag_sm, sems) = refs[21:31], refs[31:]
    waits = fetch([(cells_any, cell_sm, sems.at[0]), (flags_any, flag_sm, sems.at[1])])
    outer(count, fields, sizes, got, base, par, index, lift_table, q, halo, face_high, face_low)
    for wait in waits:
        wait.wait()
    predict(count, fields, q, par, w_high, w_low, face_table, cell_sm, flag_sm, outs, scratch)


def last_kernel(count, fields, sizes, *refs):
    got, refs = unpack_got(sizes, refs)
    base, par, index, lift_table, cells_any, out, q, staged, halo, face_high, face_low, cell_sm, sems = refs
    tiles_of_node = q.shape[0]
    waits = fetch([(cells_any, cell_sm, sems.at[tiles_of_node])])
    outer(count, fields, sizes, got, base, par, index, lift_table, q, halo, face_high, face_low)
    waits[0].wait()
    done = []
    for t in range(tiles_of_node):
        for e in range(count):
            staged[t, pl.ds(e, fields, stride=count), :] = q[t, pl.ds(cell_sm[e], fields, stride=count), :]
        done += fetch([(staged.at[t], out.at[:, t * 128 : (t + 1) * 128], sems.at[t])])
    for wait in done:
        wait.wait()


def swaps(sizes, dim, parity):
    lengths = [size for _, size in sizes]
    size, pairs = lengths[dim], []
    for place in itertools.product(*[range(length) for length in lengths]):
        other = list(place)
        other[dim] += 1 if place[dim] % 2 == parity else -1
        if not 0 <= other[dim] < size:
            if dim == 0 and lengths[1] % 2 == 0:
                other[dim], other[1] = place[dim], place[1] ^ 1
            else:
                other[dim] = other[dim] % size if size % 2 == 0 else place[dim]
        flat = [0, 0]
        for length, mine, theirs in zip(lengths, place, other):
            flat = [flat[0] * length + mine, flat[1] * length + theirs]
        pairs.append(tuple(flat))
    return pairs


def exchange(edges, sizes):
    axes = tuple(axis for axis, _ in sizes)
    got = []
    for dim, edge in enumerate(edges):
        for parity in range(1 if sizes[dim][1] == 2 else 2):
            got.append(lax.ppermute(edge, axes, swaps(sizes, dim, parity)))
    return got


def shards(sizes, wavefield, deriv_ops, density, lame_first, shear_modulus, high_order, element_cell, face_orient):
    count, fields, nodes = wavefield.shape[-3:]
    rows = fields * count
    wave = wavefield[0, 0, 0].swapaxes(0, 1).reshape(rows, nodes)
    row = lambda value: value.reshape(1, count)
    cell_sm = element_cell.reshape(count)
    flag_sm = high_order.reshape(count)
    codes = face_orient.reshape(6, 1, count)
    vmem = pl.BlockSpec(memory_space=pltpu.VMEM)
    hbm = pl.BlockSpec(memory_space=pltpu.HBM)
    index_scratch = pltpu.SMEM((count,), jnp.int32)
    shape = jax.ShapeDtypeStruct
    field_shape = shape((nodes // 128, rows, 128), F32)
    pad = -(-(rows // 8) // 8) * 8
    predicted = [
        shape((rows, nodes), BF16),
        shape((rows, nodes), BF16),
        shape((rows, 128), F32),
        shape((rows, 128), F32),
        shape((rows, 128), F32),
        shape((fields * 8, 128), F32),
        shape((2 * pad, 128), F32),
        shape((rows // 2, 128), F32),
    ]
    predict_scratch = [
        pltpu.VMEM((rows, nodes), BF16),
        pltpu.VMEM((rows, nodes), BF16),
        pltpu.VMEM((rows, nodes), BF16),
        pltpu.VMEM((rows, nodes), BF16),
        pltpu.VMEM(field_shape.shape, F32),
        pltpu.VMEM(field_shape.shape, F32),
        pltpu.VMEM(field_shape.shape, F32),
        pltpu.VMEM((3 * count, 128), F32),
        pltpu.VMEM(field_shape.shape, F32),
        pltpu.SMEM((count + 1,), jnp.int32),
    ]
    face_scratch = [pltpu.VMEM((rows, 256), BF16), pltpu.VMEM((rows, 256), BF16)]
    halo_scratch = [pltpu.VMEM((rows, 128), F32)] + face_scratch

    def call(kernel, operands, in_specs, out_shape, scratch, products, name, out_spec=vmem, limit=VMEM_LIMIT):
        single = not isinstance(out_shape, list)
        return pl.pallas_call(
            kernel,
            out_shape=out_shape,
            in_specs=in_specs,
            out_specs=out_spec if single else [out_spec] * len(out_shape),
            scratch_shapes=scratch,
            compiler_params=pltpu.CompilerParams(vmem_limit_bytes=limit),
            cost_estimate=pl.CostEstimate(
                flops=products * 6 * rows * nodes * nodes * 4, bytes_accessed=4 * rows * nodes * 4, transcendentals=0
            ),
            name=name,
        )(*operands)

    w_high, w_low, face_table, lift_table = call(
        table_kernel,
        [deriv_ops],
        [hbm],
        [
            shape(deriv_ops.shape, BF16),
            shape(deriv_ops.shape, BF16),
            shape((nodes, 256), BF16),
            shape((256, nodes), BF16),
        ],
        [pltpu.VMEM(deriv_ops.shape, F32), pltpu.SemaphoreType.DMA((2 * deriv_ops.shape[0],))],
        2,
        "split_operators",
        limit=TABLE_LIMIT,
    )
    q, par, index, *ahead = call(
        functools.partial(first_kernel, count, fields),
        [wave, row(density), row(lame_first), row(shear_modulus), row(element_cell), codes, cell_sm, flag_sm]
        + [w_high, w_low, face_table],
        [vmem] * 6 + [hbm] * 2 + [vmem] * 3,
        [field_shape, shape((4 * count, 128), F32), shape((3 * count, 128), jnp.int32)] + predicted,
        predict_scratch + [index_scratch, index_scratch, pltpu.SemaphoreType.DMA((2,))],
        4,
        "first_predictor",
    )
    for step in range(STEPS):
        traces, edges = ahead[:5], ahead[5:]
        got = exchange(edges, sizes)
        base = call(
            functools.partial(inner_kernel, count, fields),
            [q, *traces, par, index, w_high, w_low, lift_table],
            [vmem] * 11,
            field_shape,
            face_scratch,
            1,
            "inner_update",
        )
        if step < STEPS - 1:
            q, *ahead = call(
                functools.partial(middle_kernel, count, fields, sizes),
                [*got, base, par, index, w_high, w_low, face_table, lift_table, cell_sm, flag_sm],
                [vmem] * (len(got) + 7) + [hbm] * 2,
                [field_shape] + predicted,
                halo_scratch + predict_scratch + [index_scratch, index_scratch, pltpu.SemaphoreType.DMA((2,))],
                4,
                "outer_update_predictor",
            )
        else:
            out = call(
                functools.partial(last_kernel, count, fields, sizes),
                [*got, base, par, index, lift_table, cell_sm],
                [vmem] * (len(got) + 4) + [hbm],
                shape((rows, nodes), F32),
                [pltpu.VMEM(field_shape.shape, F32)] * 2
                + halo_scratch
                + [index_scratch, pltpu.SemaphoreType.DMA((nodes // 128 + 1,))],
                1,
                "outer_update",
                hbm,
            )
    return out.reshape(fields, count, nodes).swapaxes(0, 1)[None, None, None]


def solution(mesh):
    sizes = tuple((axis, mesh.shape[axis]) for axis in mesh.axis_names)
    lead = ("gx", "gy", "ha")
    placed = (
        P(*lead, None, None, None),
        P(),
        P(*lead, None),
        P(*lead, None),
        P(*lead, None),
        P(*lead, None),
        P(*lead, None),
        P(*lead, None, None),
    )
    return jax.shard_map(
        functools.partial(shards, sizes),
        mesh=mesh,
        in_specs=placed,
        out_specs=P(*lead, None, None, None),
        check_vma=False,
    )
```

```python
import functools
import itertools
import math

import jax
import jax.numpy as jnp
from jax import lax
from jax.experimental import pallas as pl
from jax.experimental.pallas import tpu as pltpu
from jax.sharding import PartitionSpec as P

STEPS = 2
DT = 0.8
LIFT = 2.0
EXCHANGED = (2, 0, 1)
PICKED = ((0, 1, 2, 3, 6, 8), (0, 1, 2, 6, 4, 7), (0, 1, 2, 8, 7, 5))
F32 = jnp.float32
BF16 = jnp.bfloat16
VMEM_LIMIT = 24 << 20
TABLE_LIMIT = 50 << 20


def wide(column, count):
    return jnp.concatenate([column] * count, axis=1)


def get(field, rows, cols):
    return jnp.concatenate([field[t, rows, :] for t in range(cols.start // 128, cols.stop // 128)], axis=1)


def put(field, rows, cols, value):
    for t in range(cols.start // 128, cols.stop // 128):
        field[t, rows, :] = value[:, t * 128 - cols.start : (t + 1) * 128 - cols.start]


def add(field, rows, cols, value):
    put(field, rows, cols, get(field, rows, cols) + value)


def split(value):
    high = value.astype(BF16)
    return high, (value - high.astype(F32)).astype(BF16)


def dot(left, right):
    return jnp.dot(left, right, preferred_element_type=F32)


def moved(table, source, cols, rows_in, rows_out):
    body, whole = table.shape[1], source.shape[0]
    first = dot(table[...], source[0:body, cols])
    rest = dot(table[0:rows_out, 0:rows_in], source[body:whole, cols])
    return jnp.concatenate([first, rest], axis=0)


def lanes_of(rows):
    return lax.broadcasted_iota(jnp.int32, (rows, 128), 1)


def rate(high, low, w_high, w_low, par, stride, rows, emit, block=256):
    nodes = w_high.shape[-1]
    inv_rho = wide(par[0:rows], block // 128)
    lame = wide(par[stride : stride + rows], block // 128)
    shear = wide(par[2 * stride : 2 * stride + rows], block // 128)
    shear2 = 2.0 * shear
    for start in range(0, nodes, block):
        cols = slice(start, start + block)
        deriv = []
        for dim in range(3):
            top = jnp.concatenate([high[f * stride : f * stride + rows] for f in PICKED[dim]], axis=0)
            rest = jnp.concatenate([low[f * stride : f * stride + rows] for f in PICKED[dim]], axis=0)
            both = dot(jnp.concatenate([top, rest], axis=0), w_high[dim, :, cols])
            deriv.append(both[: 6 * rows] + both[6 * rows :] + dot(top, w_low[dim, :, cols]))
        part = lambda dim, row: deriv[dim][row * rows : (row + 1) * rows]
        div = lame * (part(0, 0) + part(1, 1) + part(2, 2))
        emit(0, cols, inv_rho * (part(0, 3) + part(1, 3) + part(2, 3)))
        emit(1, cols, inv_rho * (part(0, 4) + part(1, 4) + part(2, 4)))
        emit(2, cols, inv_rho * (part(0, 5) + part(1, 5) + part(2, 5)))
        emit(3, cols, div + shear2 * part(0, 0))
        emit(4, cols, div + shear2 * part(1, 1))
        emit(5, cols, div + shear2 * part(2, 2))
        emit(6, cols, shear * (part(0, 1) + part(1, 0)))
        emit(7, cols, shear * (part(1, 2) + part(2, 1)))
        emit(8, cols, shear * (part(0, 2) + part(2, 0)))


def correction(jump, par, count, dim, rows):
    take = lambda k: par[k * count : k * count + rows] if not isinstance(rows, slice) else par[
        k * count + rows.start : k * count + rows.stop
    ]
    inv_rho, lame, shear, half_speed = take(0), take(1), take(2), take(3)
    size = jump[0].shape[0]
    sign = jnp.where(lanes_of(size) < 64, -0.5, 0.5)
    inv_rho, lame, shear = sign * inv_rho, sign * lame, sign * shear
    stiff = lame + 2.0 * shear
    if dim == 0:
        flux = [inv_rho * jump[3], inv_rho * jump[6], inv_rho * jump[8]]
        flux += [stiff * jump[0], lame * jump[0], lame * jump[0]]
        flux += [shear * jump[1], None, shear * jump[2]]
    elif dim == 1:
        flux = [inv_rho * jump[6], inv_rho * jump[4], inv_rho * jump[7]]
        flux += [lame * jump[1], stiff * jump[1], lame * jump[1]]
        flux += [shear * jump[0], shear * jump[2], None]
    else:
        flux = [inv_rho * jump[8], inv_rho * jump[7], inv_rho * jump[5]]
        flux += [lame * jump[2], lame * jump[2], stiff * jump[2]]
        flux += [None, shear * jump[1], shear * jump[0]]
    return [
        half_speed * jump[f] if flux[f] is None else half_speed * jump[f] + flux[f] for f in range(len(jump))
    ]


def orient(value, index):
    return jnp.take_along_axis(value, index, axis=1, mode="promise_in_bounds")


def lift_edges(target, face, f, rows, count):
    lanes = lanes_of(face.shape[0])
    scaled = DT * LIFT * face
    top = slice(f * count + rows.start, f * count + rows.stop)
    last = target.shape[0] - 1
    target[0, top] = target[0, top] + jnp.where(lanes < 64, scaled, 0.0)
    target[last, top] = target[last, top] + jnp.where(lanes < 64, 0.0, scaled)


def lift_inner(target, face_high, face_low, lift_table):
    rows, nodes = target.shape[1], lift_table.shape[1]
    for start in range(0, nodes, 256):
        cols = slice(start, start + 256)
        lifted = dot(face_high[...], lift_table[:, cols]) + dot(face_low[...], lift_table[:, cols])
        add(target, slice(0, rows), cols, DT * LIFT * lifted)


def fetch(copies):
    started = [pltpu.make_async_copy(*copy) for copy in copies]
    for copy in started:
        copy.start()
    return started


def send(low, high, up, targets):
    minus = lanes_of(low.shape[0]) < 64
    plus_face = jnp.where(minus, pltpu.roll(low, 64, 1), high)
    minus_face = jnp.where(minus, low, pltpu.roll(high, 64, 1))
    targets[0][...] = jnp.where(up, plus_face, minus_face)
    if len(targets) > 1:
        targets[1][...] = jnp.where(up, minus_face, plus_face)


def received(pair, axis, size):
    here = lax.axis_index(axis)
    odd = here % 2 == 1
    first = pair[0][...]
    second = first if pair[1] is None else pair[1][...]
    minus = lanes_of(first.shape[0]) < 64
    lower = jnp.where(odd, first, second)
    upper = jnp.where(odd, second, first)
    plus_lane = jnp.logical_and(here > 0, jnp.logical_not(minus))
    minus_lane = jnp.logical_and(here < size - 1, minus)
    return (
        (jnp.where(plus_lane, pltpu.roll(lower, 64, 1), 0.0), jnp.where(plus_lane, lower, 0.0)),
        (jnp.where(minus_lane, upper, 0.0), jnp.where(minus_lane, pltpu.roll(upper, 64, 1), 0.0)),
    )


def predict(count, fields, sizes, q, par, hot_par, pack, unpack, w_high, w_low, face_table, outs, scratch):
    int_high, int_low, trace_x, trace_y, trace_z, *edges = outs
    h0, l0, h1, l1, total, p0, p1, p2, p3, series = scratch
    nodes = h0.shape[1]
    tiles_of_node = nodes // 128
    every = slice(0, nodes)
    half = count // 2

    def first(f, cols, value):
        rows = slice(f * count, (f + 1) * count)
        put(total, rows, cols, get(q, rows, cols) + DT / 2.0 * value)
        h1[rows, cols], l1[rows, cols] = split(value)

    rate(h0, l0, w_high, w_low, par, count, count, first)

    def then(f, cols, value):
        rows = slice(f * count, (f + 1) * count)
        add(total, rows, cols, DT**2 / 6.0 * value)
        h0[rows, cols], l0[rows, cols] = split(value)

    rate(h1, l1, w_high, w_low, par, count, count, then)

    @pl.when(jnp.max(hot_par[3 * half : 3 * half + 8]) > 0.0)
    def _():
        for start in range(0, nodes, 256):
            cols = slice(start, start + 256)
            p0[:, cols] = moved(pack, h0, cols, count, half).astype(BF16)
            p1[:, cols] = moved(pack, l0, cols, count, half).astype(BF16)
        buffers = [(p0, p1), (p2, p3)]
        for order in (3, 4, 5):
            weight = DT**order / math.factorial(order + 1)
            source, target = buffers[(order - 3) % 2], buffers[(order - 2) % 2]

            def more(f, cols, value, order=order, weight=weight, target=target):
                rows = slice(f * half, (f + 1) * half)
                part = weight * value
                if order > 3:
                    part = part + series[rows, cols]
                if order < 5:
                    series[rows, cols] = part
                    part = value
                target[0][rows, cols], target[1][rows, cols] = split(part)

            rate(source[0], source[1], w_high, w_low, hot_par, half, half, more)
        for start in range(0, nodes, 256):
            cols = slice(start, start + 256)
            extra = moved(unpack, p2, cols, half, count) + moved(unpack, p3, cols, half, count)
            add(total, slice(0, fields * count), cols, extra)

    for f in range(fields):
        rows = slice(f * count, (f + 1) * count)
        int_high[rows], int_low[rows] = split(get(total, rows, every))
        trace_x[rows] = jnp.where(lanes_of(count) < 64, total[0, rows], total[tiles_of_node - 1, rows])
    faces = dot(int_high[...], face_table[...]) + dot(int_low[...], face_table[...])
    trace_y[...] = faces[:, 0:128]
    trace_z[...] = faces[:, 128:256]
    targets, at = {}, 0
    for dim in EXCHANGED:
        number = 1 if sizes[dim][1] == 2 else 2
        targets[dim] = edges[at : at + number]
        at += number
    ups = [lax.axis_index(axis) % 2 == 0 for axis, _ in sizes]
    ends = []
    for f in range(fields):
        low, high = trace_x[f * count : f * count + 8], trace_x[(f + 1) * count - 8 : (f + 1) * count]
        ends.append(jnp.where(lanes_of(8) < 64, low, high))
    middle = (fields + 1) // 2
    ends.append(ends[-1])
    send(jnp.concatenate(ends[:middle]), jnp.concatenate(ends[middle : 2 * middle]), ups[0], targets[0])
    tiles = fields * count // 8
    pad = targets[1][0].shape[0] - tiles
    minus = lanes_of(tiles) < 64
    ends = []
    for m in range(2):
        value = jnp.where(minus, trace_y[pl.ds(m, tiles, stride=8), :], trace_y[pl.ds(6 + m, tiles, stride=8), :])
        ends.append(jnp.concatenate([value, jnp.zeros((pad, 128), F32)]) if pad else value)
    send(ends[0], ends[1], ups[1], targets[1])
    pairs = fields * count // 4
    minus = lanes_of(pairs) < 64
    ends = []
    for start in (0, 2 * pairs):
        value = jnp.where(
            minus, trace_z[pl.ds(start, pairs, stride=2), :], trace_z[pl.ds(start + 1, pairs, stride=2), :]
        )
        ends.append(value)
    send(ends[0], ends[1], ups[2], targets[2])


def inner(count, fields, q, int_high, int_low, trace_x, trace_y, trace_z, par, index, w_high, w_low, lift_table,
          base, face_high, face_low):
    def volume(f, cols, value):
        rows = slice(f * count, (f + 1) * count)
        put(base, rows, cols, get(q, rows, cols) + DT * value)

    rate(int_high, int_low, w_high, w_low, par, count, count, volume)
    lanes = lanes_of(count)
    sub = lax.broadcasted_iota(jnp.int32, (count, 128), 0)
    minus = lanes < 64
    zero = jnp.zeros((8, 128), F32)
    for dim, trace in enumerate((trace_x, trace_y, trace_z)):
        jump = []
        for f in range(fields):
            own = trace[f * count : (f + 1) * count]
            if dim == 0:
                above = jnp.concatenate([own[8:], zero], axis=0)
                below = jnp.concatenate([zero, own[:-8]], axis=0)
            elif dim == 1:
                above = jnp.where(sub % 8 < 6, pltpu.roll(own, count - 2, 0), 0.0)
                below = jnp.where(sub % 8 < 2, 0.0, pltpu.roll(own, 2, 0))
            else:
                above = jnp.where(sub % 2 < 1, pltpu.roll(own, count - 1, 0), 0.0)
                below = jnp.where(sub % 2 < 1, 0.0, pltpu.roll(own, 1, 0))
            beside = jnp.where(minus, above, below)
            jump.append(orient(beside, index[dim * count : (dim + 1) * count]) - own)
        fixed = correction(jump, par, count, dim, count)
        for f in range(fields):
            if dim == 0:
                lift_edges(base, fixed[f], f, slice(0, count), count)
            else:
                cols = slice((dim - 1) * 128, dim * 128)
                rows = slice(f * count, (f + 1) * count)
                face_high[rows, cols], face_low[rows, cols] = split(fixed[f])
    lift_inner(base, face_high, face_low, lift_table)


def outer(count, fields, sizes, got, base, par, index, lift_table, out, halo, face_high, face_low):
    middle = (fields + 1) // 2
    lower, upper = received(got[0], *sizes[0])
    out[...] = base[...]
    for end, (low, high) in enumerate((lower, upper)):
        rows = slice(0, 8) if end == 0 else slice(count - 8, count)
        jump = []
        for f in range(fields):
            part, at = (low, f) if f < middle else (high, f - middle)
            jump.append(orient(part[at * 8 : at * 8 + 8], index[rows]))
        fixed = correction(jump, par, count, 0, rows)
        for f in range(fields):
            lift_edges(out, fixed[f], f, rows, count)
    tiles = fields * count // 8
    pairs = fields * count // 4
    for dim in (1, 2):
        lower, upper = received(got[dim], *sizes[dim])
        if dim == 1:
            halo[...] = jnp.zeros_like(halo)
            for m in range(2):
                halo[pl.ds(m, tiles, stride=8), :] = lower[m][0:tiles]
                halo[pl.ds(6 + m, tiles, stride=8), :] = upper[m][0:tiles]
        else:
            for part in range(2):
                halo[pl.ds(2 * part * pairs, pairs, stride=2), :] = lower[part]
                halo[pl.ds(2 * part * pairs + 1, pairs, stride=2), :] = upper[part]
        jump = [
            orient(halo[f * count : (f + 1) * count], index[dim * count : (dim + 1) * count]) for f in range(fields)
        ]
        fixed = correction(jump, par, count, dim, count)
        for f in range(fields):
            cols = slice((dim - 1) * 128, dim * 128)
            rows = slice(f * count, (f + 1) * count)
            face_high[rows, cols], face_low[rows, cols] = split(fixed[f])
    lift_inner(out, face_high, face_low, lift_table)


def table_kernel(ops_any, w_high, w_low, face_table, lift_table, ops, sems):
    dims, nodes = ops.shape[:2]
    step = nodes // 2
    parts = [(dim, slice(start, start + step)) for dim in range(dims) for start in range(0, nodes, step)]
    waits = fetch([(ops_any.at[dim, rows], ops.at[dim, rows], sems.at[k]) for k, (dim, rows) in enumerate(parts)])

    def on_face(node, column):
        i, j, k = node // 64, node // 8 % 8, node % 8
        plus = column // 64 % 2 * 7
        p, r = column % 64 // 8, column % 8
        along_y = (column < 128) & (j == plus) & (i == p) & (k == r)
        along_z = (column >= 128) & (k == plus) & (i == p) & (j == r)
        return jnp.where(along_y | along_z, 1.0, 0.0).astype(BF16)

    table = face_table.shape
    face_table[...] = on_face(lax.broadcasted_iota(jnp.int32, table, 0), lax.broadcasted_iota(jnp.int32, table, 1))
    table = table[::-1]
    lift_table[...] = on_face(lax.broadcasted_iota(jnp.int32, table, 1), lax.broadcasted_iota(jnp.int32, table, 0))
    for wait, (dim, rows) in zip(waits, parts):
        wait.wait()
        w_high[dim, rows, :], w_low[dim, rows, :] = split(ops[dim, rows, :])


def first_kernel(count, fields, sizes, wave, density, lame, shear, cell, flag, orient_code, w_high, w_low, face_table,
                 q, par, index, hot_par, place, place_back, pack, unpack, *rest):
    outs, scratch = rest[:-10], rest[-10:]
    h0, l0, h1, l1 = scratch[:4]
    half, blocks = count // 2, fields - 1
    iota = lambda shape, axis: lax.broadcasted_iota(jnp.int32, shape, axis)
    ones = lambda mask: jnp.where(mask, 1.0, 0.0).astype(BF16)
    cells = cell[...]
    square = (count, count)
    tiled = dot(
        jnp.broadcast_to(cells.astype(F32).astype(BF16), (8, count)),
        ones(iota((count, blocks * count), 1) % count == iota((count, blocks * count), 0)),
    )[0:1].astype(jnp.int32)
    shape = place.shape
    target = tiled + iota((1, shape[1]), 1) // count * count
    place[...] = ones(iota(shape, 0) == target)
    for f in range(fields):
        rows = slice(f * count, (f + 1) * count)
        h1[rows], l1[rows] = split(wave[rows])
    for start in range(0, h0.shape[1], 256):
        cols = slice(start, start + 256)
        high = moved(place, h1, cols, count, count)
        low = moved(place, l1, cols, count, count)
        h0[:, cols], l0[:, cols] = high.astype(BF16), low.astype(BF16)
        put(q, slice(0, fields * count), cols, high + low)

    fills = cells == iota(square, 0)
    gather = lambda mask, row: jnp.sum(jnp.where(mask, row, 0.0), axis=1, keepdims=True)
    in_cell = lambda row: jnp.broadcast_to(gather(fills, row), (count, 128))
    inv_row = 1.0 / density[...]
    inv_rho = in_cell(inv_row)
    lame_col = in_cell(lame[...])
    shear_col = in_cell(shear[...])
    par[0:count] = inv_rho
    par[count : 2 * count] = lame_col
    par[2 * count : 3 * count] = shear_col
    par[3 * count : 4 * count] = 0.5 * jnp.sqrt((lame_col + 2.0 * shear_col) * inv_rho)

    flags = flag[...].astype(F32)
    before = ones(iota(square, 0) < iota(square, 1))
    rank = dot(jnp.broadcast_to(flags.astype(BF16), (8, count)), before)[0:1]
    slots = (rank.astype(jnp.int32) == iota((half, count), 0)) & (flags > 0.0)
    in_slot = lambda row: jnp.broadcast_to(gather(slots, row), (half, 128))
    hot_par[0:half] = in_slot(inv_row)
    hot_par[half : 2 * half] = in_slot(lame[...])
    hot_par[2 * half : 3 * half] = in_slot(shear[...])
    hot_par[3 * half : 4 * half] = in_slot(flags)
    twice = lambda column, times: jnp.concatenate([column] * times, axis=0).astype(jnp.int32)
    shape = pack.shape
    target = twice(in_slot(cells.astype(F32)), blocks) + iota((shape[0], 128), 0) // half * count
    used = twice(in_slot(flags), blocks) > 0
    target = jnp.where(used, target, -1)
    pack[...] = ones(iota(shape, 1) == wide(target, shape[1] // 128))
    shape = unpack.shape
    target = twice(in_cell(rank), blocks) + iota((shape[0], 128), 0) // count * half
    target = jnp.where(twice(in_cell(flags), blocks) > 0, target, -1)
    unpack[...] = ones(iota(shape, 1) == wide(target, shape[1] // 128))
    own = gather(iota(square, 0) == iota(square, 1), cells.astype(F32))
    shape = place_back.shape
    target = twice(jnp.broadcast_to(own, (count, 128)), blocks) + iota((shape[0], 128), 0) // count * count
    place_back[...] = ones(iota(shape, 1) == wide(target, shape[1] // 128))

    lanes = lanes_of(count)
    p_lane, r_lane = lanes % 64 // 8, lanes % 8
    for dim in range(3):
        code = jnp.where(
            lanes < 64,
            in_cell(orient_code[2 * dim].astype(F32)),
            in_cell(orient_code[2 * dim + 1].astype(F32)),
        ).astype(jnp.int32)
        p_from = jnp.where(code % 2 == 1, 7 - p_lane, p_lane)
        r_from = jnp.where(code // 2 % 2 == 1, 7 - r_lane, r_lane)
        source = jnp.where(code >= 4, r_from * 8 + p_from, p_from * 8 + r_from)
        index[dim * count : (dim + 1) * count] = source + jnp.where(lanes < 64, 64, 0)
    predict(count, fields, sizes, q, par, hot_par, pack, unpack, w_high, w_low, face_table, outs, scratch)


def inner_kernel(count, fields, *refs):
    inner(count, fields, *refs)


def unpack_got(sizes, refs):
    got, at = [[None, None] for _ in sizes], 0
    for dim in EXCHANGED:
        for k in range(1 if sizes[dim][1] == 2 else 2):
            got[dim][k] = refs[at]
            at += 1
    return got, refs[at:]


def middle_kernel(count, fields, sizes, *refs):
    got, refs = unpack_got(sizes, refs)
    base, par, index, hot_par, pack, unpack, w_high, w_low, face_table, lift_table, q = refs[:11]
    outs, (halo, face_high, face_low), scratch = refs[11:-13], refs[-13:-10], refs[-10:]
    outer(count, fields, sizes, got, base, par, index, lift_table, q, halo, face_high, face_low)
    h0, l0 = scratch[:2]
    for f in range(fields):
        rows = slice(f * count, (f + 1) * count)
        h0[rows], l0[rows] = split(get(q, rows, slice(0, h0.shape[1])))
    predict(count, fields, sizes, q, par, hot_par, pack, unpack, w_high, w_low, face_table, outs, scratch)


def last_kernel(count, fields, sizes, *refs):
    got, refs = unpack_got(sizes, refs)
    base, par, index, place_back, lift_table, out, q, high, low, staged, halo, face_high, face_low, sems = refs
    outer(count, fields, sizes, got, base, par, index, lift_table, q, halo, face_high, face_low)
    done = []
    for k, start in enumerate(range(0, staged.shape[1], 256)):
        cols = slice(start, start + 256)
        for f in range(fields):
            rows = slice(f * count, (f + 1) * count)
            high[rows, cols], low[rows, cols] = split(get(q, rows, cols))
        staged[:, cols] = moved(place_back, high, cols, count, count) + moved(place_back, low, cols, count, count)
        done += fetch([(staged.at[:, cols], out.at[:, cols], sems.at[k])])
    for wait in done:
        wait.wait()


def swaps(sizes, dim, parity):
    lengths = [size for _, size in sizes]
    size, pairs = lengths[dim], []
    for place in itertools.product(*[range(length) for length in lengths]):
        other = list(place)
        other[dim] += 1 if place[dim] % 2 == parity else -1
        if not 0 <= other[dim] < size:
            if dim == 0 and lengths[1] % 2 == 0:
                other[dim], other[1] = place[dim], place[1] ^ 1
            else:
                other[dim] = other[dim] % size if size % 2 == 0 else place[dim]
        flat = [0, 0]
        for length, mine, theirs in zip(lengths, place, other):
            flat = [flat[0] * length + mine, flat[1] * length + theirs]
        pairs.append(tuple(flat))
    return pairs


def exchange(edges, sizes):
    axes = tuple(axis for axis, _ in sizes)
    got = []
    for dim in EXCHANGED:
        for parity in range(1 if sizes[dim][1] == 2 else 2):
            got.append(lax.ppermute(edges[len(got)], axes, swaps(sizes, dim, parity)))
    return got


def shards(sizes, wavefield, deriv_ops, density, lame_first, shear_modulus, high_order, element_cell, face_orient):
    count, fields, nodes = wavefield.shape[-3:]
    rows = fields * count
    wave = wavefield[0, 0, 0].swapaxes(0, 1).reshape(rows, nodes)
    half, blocks = count // 2, fields - 1
    row = lambda value: value.reshape(1, count)
    codes = face_orient.reshape(6, 1, count)
    vmem = pl.BlockSpec(memory_space=pltpu.VMEM)
    hbm = pl.BlockSpec(memory_space=pltpu.HBM)
    shape = jax.ShapeDtypeStruct
    field_shape = shape((nodes // 128, rows, 128), F32)
    edge_rows = {0: (fields + 1) // 2 * 8, 1: -(-(rows // 8) // 8) * 8, 2: rows // 4}
    predicted = [
        shape((rows, nodes), BF16),
        shape((rows, nodes), BF16),
        shape((rows, 128), F32),
        shape((rows, 128), F32),
        shape((rows, 128), F32),
    ]
    for dim in EXCHANGED:
        predicted += [shape((edge_rows[dim], 128), F32)] * (1 if sizes[dim][1] == 2 else 2)
    hot_rows = half * fields
    predict_scratch = [pltpu.VMEM((rows, nodes), BF16)] * 4 + [pltpu.VMEM(field_shape.shape, F32)]
    predict_scratch += [pltpu.VMEM((hot_rows, nodes), BF16)] * 4 + [pltpu.VMEM((hot_rows, nodes), F32)]
    face_scratch = [pltpu.VMEM((rows, 256), BF16), pltpu.VMEM((rows, 256), BF16)]
    halo_scratch = [pltpu.VMEM((rows, 128), F32)] + face_scratch

    def call(kernel, operands, in_specs, out_shape, scratch, products, name, out_spec=vmem, limit=VMEM_LIMIT):
        single = not isinstance(out_shape, list)
        return pl.pallas_call(
            kernel,
            out_shape=out_shape,
            in_specs=in_specs,
            out_specs=out_spec if single else [out_spec] * len(out_shape),
            scratch_shapes=scratch,
            compiler_params=pltpu.CompilerParams(vmem_limit_bytes=limit),
            cost_estimate=pl.CostEstimate(
                flops=products * 6 * rows * nodes * nodes * 4, bytes_accessed=4 * rows * nodes * 4, transcendentals=0
            ),
            name=name,
        )(*operands)

    w_high, w_low, face_table, lift_table = call(
        table_kernel,
        [deriv_ops],
        [hbm],
        [
            shape(deriv_ops.shape, BF16),
            shape(deriv_ops.shape, BF16),
            shape((nodes, 256), BF16),
            shape((256, nodes), BF16),
        ],
        [pltpu.VMEM(deriv_ops.shape, F32), pltpu.SemaphoreType.DMA((2 * deriv_ops.shape[0],))],
        2,
        "split_operators",
        limit=TABLE_LIMIT,
    )
    q, par, index, hot_par, place, place_back, pack, unpack, *ahead = call(
        functools.partial(first_kernel, count, fields, sizes),
        [wave, row(density), row(lame_first), row(shear_modulus), row(element_cell), row(high_order), codes]
        + [w_high, w_low, face_table],
        [vmem] * 10,
        [
            field_shape,
            shape((4 * count, 128), F32),
            shape((3 * count, 128), jnp.int32),
            shape((4 * half, 128), F32),
            shape((blocks * count, blocks * count), BF16),
            shape((blocks * count, blocks * count), BF16),
            shape((blocks * half, blocks * count), BF16),
            shape((blocks * count, blocks * half), BF16),
        ]
        + predicted,
        predict_scratch,
        4,
        "first_predictor",
    )
    for step in range(STEPS):
        traces, edges = ahead[:5], ahead[5:]
        got = exchange(edges, sizes)
        base = call(
            functools.partial(inner_kernel, count, fields),
            [q, *traces, par, index, w_high, w_low, lift_table],
            [vmem] * 11,
            field_shape,
            face_scratch,
            1,
            "inner_update",
        )
        if step < STEPS - 1:
            q, *ahead = call(
                functools.partial(middle_kernel, count, fields, sizes),
                [*got, base, par, index, hot_par, pack, unpack, w_high, w_low, face_table, lift_table],
                [vmem] * (len(got) + 10),
                [field_shape] + predicted,
                halo_scratch + predict_scratch,
                4,
                "outer_update_predictor",
            )
        else:
            out = call(
                functools.partial(last_kernel, count, fields, sizes),
                [*got, base, par, index, place_back, lift_table],
                [vmem] * (len(got) + 5),
                shape((rows, nodes), F32),
                [pltpu.VMEM(field_shape.shape, F32)]
                + [pltpu.VMEM((rows, nodes), BF16)] * 2
                + [pltpu.VMEM((rows, nodes), F32)]
                + halo_scratch
                + [pltpu.SemaphoreType.DMA((nodes // 256,))],
                1,
                "outer_update",
                hbm,
            )
    return out.reshape(fields, count, nodes).swapaxes(0, 1)[None, None, None]


def solution(mesh):
    sizes = tuple((axis, mesh.shape[axis]) for axis in mesh.axis_names)
    lead = ("gx", "gy", "ha")
    placed = (
        P(*lead, None, None, None),
        P(),
        P(*lead, None),
        P(*lead, None),
        P(*lead, None),
        P(*lead, None),
        P(*lead, None),
        P(*lead, None, None),
    )
    return jax.shard_map(
        functools.partial(shards, sizes),
        mesh=mesh,
        in_specs=placed,
        out_specs=P(*lead, None, None, None),
        check_vma=False,
    )
```

```python
import functools
import itertools
import math

import jax
import jax.numpy as jnp
from jax import lax
from jax.experimental import pallas as pl
from jax.experimental.pallas import tpu as pltpu
from jax.sharding import PartitionSpec as P

STEPS = 2
DT = 0.8
LIFT = 2.0
EXCHANGED = (2, 0, 1)
PICKED = ((0, 1, 2, 3, 6, 8), (0, 1, 2, 6, 4, 7), (0, 1, 2, 8, 7, 5))
F32 = jnp.float32
BF16 = jnp.bfloat16
VMEM_LIMIT = 24 << 20
TABLE_LIMIT = 50 << 20


def wide(column, count):
    return jnp.concatenate([column] * count, axis=1)


def get(field, rows, cols):
    return jnp.concatenate([field[t, rows, :] for t in range(cols.start // 128, cols.stop // 128)], axis=1)


def put(field, rows, cols, value):
    for t in range(cols.start // 128, cols.stop // 128):
        field[t, rows, :] = value[:, t * 128 - cols.start : (t + 1) * 128 - cols.start]


def add(field, rows, cols, value):
    put(field, rows, cols, get(field, rows, cols) + value)


def split(value):
    high = value.astype(BF16)
    return high, (value - high.astype(F32)).astype(BF16)


def dot(left, right):
    return jnp.dot(left, right, preferred_element_type=F32)


def moved(table, source, cols, rows_in, rows_out):
    body, whole = table.shape[1], source.shape[0]
    first = dot(table[...], source[0:body, cols])
    rest = dot(table[0:rows_out, 0:rows_in], source[body:whole, cols])
    return jnp.concatenate([first, rest], axis=0)


def lanes_of(rows):
    return lax.broadcasted_iota(jnp.int32, (rows, 128), 1)


def combine(deriv, rows, inv_rho, lame, shear, shear2, cols, emit):
    part = lambda dim, row: deriv[dim][row * rows : (row + 1) * rows]
    div = lame * (part(0, 0) + part(1, 1) + part(2, 2))
    emit(0, cols, inv_rho * (part(0, 3) + part(1, 3) + part(2, 3)))
    emit(1, cols, inv_rho * (part(0, 4) + part(1, 4) + part(2, 4)))
    emit(2, cols, inv_rho * (part(0, 5) + part(1, 5) + part(2, 5)))
    emit(3, cols, div + shear2 * part(0, 0))
    emit(4, cols, div + shear2 * part(1, 1))
    emit(5, cols, div + shear2 * part(2, 2))
    emit(6, cols, shear * (part(0, 1) + part(1, 0)))
    emit(7, cols, shear * (part(1, 2) + part(2, 1)))
    emit(8, cols, shear * (part(0, 2) + part(2, 0)))


def rate(high, low, w_high, w_low, par, stride, rows, emit, block=256):
    nodes = w_high.shape[-1]
    inv_rho = wide(par[0:rows], block // 128)
    lame = wide(par[stride : stride + rows], block // 128)
    shear = wide(par[2 * stride : 2 * stride + rows], block // 128)
    shear2 = 2.0 * shear
    for start in range(0, nodes, block):
        cols = slice(start, start + block)
        deriv = [None] * 3
        for k in range(0, nodes, 256):
            depth = slice(k, k + 256)
            for dim in range(3):
                top = jnp.concatenate([high[f * stride : f * stride + rows, depth] for f in PICKED[dim]], axis=0)
                rest = jnp.concatenate([low[f * stride : f * stride + rows, depth] for f in PICKED[dim]], axis=0)
                both = dot(jnp.concatenate([top, rest], axis=0), w_high[dim, depth, cols])
                part = both[: 6 * rows] + both[6 * rows :] + dot(top, w_low[dim, depth, cols])
                deriv[dim] = part if deriv[dim] is None else deriv[dim] + part
        combine(deriv, rows, inv_rho, lame, shear, shear2, cols, emit)


def correction(jump, par, count, dim, rows):
    take = lambda k: par[k * count : k * count + rows] if not isinstance(rows, slice) else par[
        k * count + rows.start : k * count + rows.stop
    ]
    inv_rho, lame, shear, half_speed = take(0), take(1), take(2), take(3)
    size = jump[0].shape[0]
    sign = jnp.where(lanes_of(size) < 64, -0.5, 0.5)
    inv_rho, lame, shear = sign * inv_rho, sign * lame, sign * shear
    stiff = lame + 2.0 * shear
    if dim == 0:
        flux = [inv_rho * jump[3], inv_rho * jump[6], inv_rho * jump[8]]
        flux += [stiff * jump[0], lame * jump[0], lame * jump[0]]
        flux += [shear * jump[1], None, shear * jump[2]]
    elif dim == 1:
        flux = [inv_rho * jump[6], inv_rho * jump[4], inv_rho * jump[7]]
        flux += [lame * jump[1], stiff * jump[1], lame * jump[1]]
        flux += [shear * jump[0], shear * jump[2], None]
    else:
        flux = [inv_rho * jump[8], inv_rho * jump[7], inv_rho * jump[5]]
        flux += [lame * jump[2], lame * jump[2], stiff * jump[2]]
        flux += [None, shear * jump[1], shear * jump[0]]
    return [
        half_speed * jump[f] if flux[f] is None else half_speed * jump[f] + flux[f] for f in range(len(jump))
    ]


def orient(value, index):
    return jnp.take_along_axis(value, index, axis=1, mode="promise_in_bounds")


def lift_edges(target, face, f, rows, count):
    lanes = lanes_of(face.shape[0])
    scaled = DT * LIFT * face
    top = slice(f * count + rows.start, f * count + rows.stop)
    last = target.shape[0] - 1
    target[0, top] = target[0, top] + jnp.where(lanes < 64, scaled, 0.0)
    target[last, top] = target[last, top] + jnp.where(lanes < 64, 0.0, scaled)


def lift_inner(target, source, face_high, face_low, lift_table):
    rows, nodes = target.shape[1], lift_table.shape[1]
    for start in range(0, nodes, 256):
        cols = slice(start, start + 256)
        lifted = dot(face_high[...], lift_table[:, cols]) + dot(face_low[...], lift_table[:, cols])
        put(target, slice(0, rows), cols, get(source, slice(0, rows), cols) + DT * LIFT * lifted)


def fetch(copies):
    started = [pltpu.make_async_copy(*copy) for copy in copies]
    for copy in started:
        copy.start()
    return started


def send(low, high, up, targets):
    minus = lanes_of(low.shape[0]) < 64
    plus_face = jnp.where(minus, pltpu.roll(low, 64, 1), high)
    minus_face = jnp.where(minus, low, pltpu.roll(high, 64, 1))
    targets[0][...] = jnp.where(up, plus_face, minus_face)
    if len(targets) > 1:
        targets[1][...] = jnp.where(up, minus_face, plus_face)


def received(pair, axis, size):
    here = lax.axis_index(axis)
    odd = here % 2 == 1
    first = pair[0][...]
    second = first if pair[1] is None else pair[1][...]
    minus = lanes_of(first.shape[0]) < 64
    lower = jnp.where(odd, first, second)
    upper = jnp.where(odd, second, first)
    plus_lane = jnp.logical_and(here > 0, jnp.logical_not(minus))
    minus_lane = jnp.logical_and(here < size - 1, minus)
    return (
        (jnp.where(plus_lane, pltpu.roll(lower, 64, 1), 0.0), jnp.where(plus_lane, lower, 0.0)),
        (jnp.where(minus_lane, upper, 0.0), jnp.where(minus_lane, pltpu.roll(upper, 64, 1), 0.0)),
    )


def predict(count, fields, sizes, q, par, hot_par, pack, unpack, w_high, w_low, face_table, outs, scratch):
    int_high, int_low, trace_x, trace_y, trace_z, *edges = outs
    h0, l0, h1, l1, total, p0, p1, p2, p3, series = scratch
    nodes = h0.shape[1]
    half = count // 2

    def first(f, cols, value):
        rows = slice(f * count, (f + 1) * count)
        put(total, rows, cols, get(q, rows, cols) + DT / 2.0 * value)
        h1[rows, cols], l1[rows, cols] = split(value)

    rate(h0, l0, w_high, w_low, par, count, count, first)

    def then(f, cols, value):
        rows = slice(f * count, (f + 1) * count)
        add(total, rows, cols, DT**2 / 6.0 * value)
        h0[rows, cols], l0[rows, cols] = split(value)

    rate(h1, l1, w_high, w_low, par, count, count, then)

    for start in range(0, nodes, 256):
        cols = slice(start, start + 256)
        p0[:, cols] = moved(pack, h0, cols, count, half).astype(BF16)
        p1[:, cols] = moved(pack, l0, cols, count, half).astype(BF16)
    buffers = [(p0, p1), (p2, p3)]
    for order in (3, 4, 5):
        weight = DT**order / math.factorial(order + 1)
        source, target = buffers[(order - 3) % 2], buffers[(order - 2) % 2]

        def more(f, cols, value, order=order, weight=weight, target=target):
            rows = slice(f * half, (f + 1) * half)
            part = weight * value
            if order > 3:
                part = part + series[rows, cols]
            if order < 5:
                series[rows, cols] = part
                part = value
            target[0][rows, cols], target[1][rows, cols] = split(part)

        rate(source[0], source[1], w_high, w_low, hot_par, half, half, more)
    for start in range(0, nodes, 256):
        cols = slice(start, start + 256)
        extra = moved(unpack, p2, cols, half, count) + moved(unpack, p3, cols, half, count)
        add(total, slice(0, fields * count), cols, extra)
    for f in range(fields):
        rows = slice(f * count, (f + 1) * count)
        int_high[rows], int_low[rows] = split(get(total, rows, slice(0, nodes)))
        trace_x[rows] = jnp.where(lanes_of(count) < 64, total[0, rows], total[total.shape[0] - 1, rows])
    faces = dot(int_high[...], face_table[...]) + dot(int_low[...], face_table[...])
    trace_y[...] = faces[:, 0:128]
    trace_z[...] = faces[:, 128:256]
    targets, at = {}, 0
    for dim in EXCHANGED:
        number = 1 if sizes[dim][1] == 2 else 2
        targets[dim] = edges[at : at + number]
        at += number
    ups = [lax.axis_index(axis) % 2 == 0 for axis, _ in sizes]
    ends = []
    for f in range(fields):
        low, high = trace_x[f * count : f * count + 8], trace_x[(f + 1) * count - 8 : (f + 1) * count]
        ends.append(jnp.where(lanes_of(8) < 64, low, high))
    middle = (fields + 1) // 2
    ends.append(ends[-1])
    send(jnp.concatenate(ends[:middle]), jnp.concatenate(ends[middle : 2 * middle]), ups[0], targets[0])
    tiles = fields * count // 8
    pad = targets[1][0].shape[0] - tiles
    minus = lanes_of(tiles) < 64
    ends = []
    for m in range(2):
        value = jnp.where(minus, trace_y[pl.ds(m, tiles, stride=8), :], trace_y[pl.ds(6 + m, tiles, stride=8), :])
        ends.append(jnp.concatenate([value, jnp.zeros((pad, 128), F32)]) if pad else value)
    send(ends[0], ends[1], ups[1], targets[1])
    pairs = fields * count // 4
    minus = lanes_of(pairs) < 64
    ends = []
    for start in (0, 2 * pairs):
        value = jnp.where(
            minus, trace_z[pl.ds(start, pairs, stride=2), :], trace_z[pl.ds(start + 1, pairs, stride=2), :]
        )
        ends.append(value)
    send(ends[0], ends[1], ups[2], targets[2])


def inner(count, fields, q, int_high, int_low, trace_x, trace_y, trace_z, par, index, w_high, w_low, lift_table,
          base, face_high, face_low):
    def volume(f, cols, value):
        rows = slice(f * count, (f + 1) * count)
        put(base, rows, cols, get(q, rows, cols) + DT * value)

    rate(int_high, int_low, w_high, w_low, par, count, count, volume)
    lanes = lanes_of(count)
    sub = lax.broadcasted_iota(jnp.int32, (count, 128), 0)
    minus = lanes < 64
    zero = jnp.zeros((8, 128), F32)
    for dim, trace in enumerate((trace_x, trace_y, trace_z)):
        jump = []
        for f in range(fields):
            own = trace[f * count : (f + 1) * count]
            if dim == 0:
                above = jnp.concatenate([own[8:], zero], axis=0)
                below = jnp.concatenate([zero, own[:-8]], axis=0)
            elif dim == 1:
                above = jnp.where(sub % 8 < 6, pltpu.roll(own, count - 2, 0), 0.0)
                below = jnp.where(sub % 8 < 2, 0.0, pltpu.roll(own, 2, 0))
            else:
                above = jnp.where(sub % 2 < 1, pltpu.roll(own, count - 1, 0), 0.0)
                below = jnp.where(sub % 2 < 1, 0.0, pltpu.roll(own, 1, 0))
            beside = jnp.where(minus, above, below)
            jump.append(orient(beside, index[dim * count : (dim + 1) * count]) - own)
        fixed = correction(jump, par, count, dim, count)
        for f in range(fields):
            if dim == 0:
                lift_edges(base, fixed[f], f, slice(0, count), count)
            else:
                cols = slice((dim - 1) * 128, dim * 128)
                rows = slice(f * count, (f + 1) * count)
                face_high[rows, cols], face_low[rows, cols] = split(fixed[f])
    lift_inner(base, base, face_high, face_low, lift_table)


def outer(count, fields, sizes, got, base, par, index, lift_table, out, halo, face_high, face_low):
    tiles = fields * count // 8
    pairs = fields * count // 4
    for dim in (1, 2):
        lower, upper = received(got[dim], *sizes[dim])
        if dim == 1:
            halo[...] = jnp.zeros_like(halo)
            for m in range(2):
                halo[pl.ds(m, tiles, stride=8), :] = lower[m][0:tiles]
                halo[pl.ds(6 + m, tiles, stride=8), :] = upper[m][0:tiles]
        else:
            for part in range(2):
                halo[pl.ds(2 * part * pairs, pairs, stride=2), :] = lower[part]
                halo[pl.ds(2 * part * pairs + 1, pairs, stride=2), :] = upper[part]
        jump = [
            orient(halo[f * count : (f + 1) * count], index[dim * count : (dim + 1) * count]) for f in range(fields)
        ]
        fixed = correction(jump, par, count, dim, count)
        for f in range(fields):
            cols = slice((dim - 1) * 128, dim * 128)
            rows = slice(f * count, (f + 1) * count)
            face_high[rows, cols], face_low[rows, cols] = split(fixed[f])
    lift_inner(out, base, face_high, face_low, lift_table)
    middle = (fields + 1) // 2
    lower, upper = received(got[0], *sizes[0])
    for end, (low, high) in enumerate((lower, upper)):
        rows = slice(0, 8) if end == 0 else slice(count - 8, count)
        jump = []
        for f in range(fields):
            part, at = (low, f) if f < middle else (high, f - middle)
            jump.append(orient(part[at * 8 : at * 8 + 8], index[rows]))
        fixed = correction(jump, par, count, 0, rows)
        for f in range(fields):
            lift_edges(out, fixed[f], f, rows, count)


def table_kernel(ops_any, w_high, w_low, face_table, lift_table, ops, sems):
    dims, nodes = ops.shape[:2]
    step = nodes // 2
    parts = [(dim, slice(start, start + step)) for dim in range(dims) for start in range(0, nodes, step)]
    waits = fetch([(ops_any.at[dim, rows], ops.at[dim, rows], sems.at[k]) for k, (dim, rows) in enumerate(parts)])

    def on_face(node, column):
        i, j, k = node // 64, node // 8 % 8, node % 8
        plus = column // 64 % 2 * 7
        p, r = column % 64 // 8, column % 8
        along_y = (column < 128) & (j == plus) & (i == p) & (k == r)
        along_z = (column >= 128) & (k == plus) & (i == p) & (j == r)
        return jnp.where(along_y | along_z, 1.0, 0.0).astype(BF16)

    table = face_table.shape
    face_table[...] = on_face(lax.broadcasted_iota(jnp.int32, table, 0), lax.broadcasted_iota(jnp.int32, table, 1))
    table = table[::-1]
    lift_table[...] = on_face(lax.broadcasted_iota(jnp.int32, table, 1), lax.broadcasted_iota(jnp.int32, table, 0))
    for wait, (dim, rows) in zip(waits, parts):
        wait.wait()
        w_high[dim, rows, :], w_low[dim, rows, :] = split(ops[dim, rows, :])


def first_kernel(count, fields, sizes, wave, density, lame, shear, cell, flag, orient_code, w_high, w_low, face_table,
                 q, par, index, hot_par, place, place_back, pack, unpack, *rest):
    outs, scratch = rest[:-10], rest[-10:]
    h0, l0, h1, l1 = scratch[:4]
    half, blocks = count // 2, fields - 1
    iota = lambda shape, axis: lax.broadcasted_iota(jnp.int32, shape, axis)
    ones = lambda mask: jnp.where(mask, 1.0, 0.0).astype(BF16)
    cells = cell[...]
    square = (count, count)
    tiled = dot(
        jnp.broadcast_to(cells.astype(F32).astype(BF16), (8, count)),
        ones(iota((count, blocks * count), 1) % count == iota((count, blocks * count), 0)),
    )[0:1].astype(jnp.int32)
    shape = place.shape
    target = tiled + iota((1, shape[1]), 1) // count * count
    place[...] = ones(iota(shape, 0) == target)
    for f in range(fields):
        rows = slice(f * count, (f + 1) * count)
        h1[rows], l1[rows] = split(wave[rows])
    for start in range(0, h0.shape[1], 256):
        cols = slice(start, start + 256)
        high = moved(place, h1, cols, count, count)
        low = moved(place, l1, cols, count, count)
        h0[:, cols], l0[:, cols] = high.astype(BF16), low.astype(BF16)
        put(q, slice(0, fields * count), cols, high + low)

    fills = cells == iota(square, 0)
    gather = lambda mask, row: jnp.sum(jnp.where(mask, row, 0.0), axis=1, keepdims=True)
    in_cell = lambda row: jnp.broadcast_to(gather(fills, row), (count, 128))
    inv_row = 1.0 / density[...]
    inv_rho = in_cell(inv_row)
    lame_col = in_cell(lame[...])
    shear_col = in_cell(shear[...])
    par[0:count] = inv_rho
    par[count : 2 * count] = lame_col
    par[2 * count : 3 * count] = shear_col
    par[3 * count : 4 * count] = 0.5 * jnp.sqrt((lame_col + 2.0 * shear_col) * inv_rho)

    flags = flag[...].astype(F32)
    before = ones(iota(square, 0) < iota(square, 1))
    rank = dot(jnp.broadcast_to(flags.astype(BF16), (8, count)), before)[0:1]
    slots = (rank.astype(jnp.int32) == iota((half, count), 0)) & (flags > 0.0)
    in_slot = lambda row: jnp.broadcast_to(gather(slots, row), (half, 128))
    hot_par[0:half] = in_slot(inv_row)
    hot_par[half : 2 * half] = in_slot(lame[...])
    hot_par[2 * half : 3 * half] = in_slot(shear[...])
    hot_par[3 * half : 4 * half] = in_slot(flags)
    twice = lambda column, times: jnp.concatenate([column] * times, axis=0).astype(jnp.int32)
    shape = pack.shape
    target = twice(in_slot(cells.astype(F32)), blocks) + iota((shape[0], 128), 0) // half * count
    used = twice(in_slot(flags), blocks) > 0
    target = jnp.where(used, target, -1)
    pack[...] = ones(iota(shape, 1) == wide(target, shape[1] // 128))
    shape = unpack.shape
    target = twice(in_cell(rank), blocks) + iota((shape[0], 128), 0) // count * half
    target = jnp.where(twice(in_cell(flags), blocks) > 0, target, -1)
    unpack[...] = ones(iota(shape, 1) == wide(target, shape[1] // 128))
    own = gather(iota(square, 0) == iota(square, 1), cells.astype(F32))
    shape = place_back.shape
    target = twice(jnp.broadcast_to(own, (count, 128)), blocks) + iota((shape[0], 128), 0) // count * count
    place_back[...] = ones(iota(shape, 1) == wide(target, shape[1] // 128))

    lanes = lanes_of(count)
    p_lane, r_lane = lanes % 64 // 8, lanes % 8
    for dim in range(3):
        code = jnp.where(
            lanes < 64,
            in_cell(orient_code[2 * dim].astype(F32)),
            in_cell(orient_code[2 * dim + 1].astype(F32)),
        ).astype(jnp.int32)
        p_from = jnp.where(code % 2 == 1, 7 - p_lane, p_lane)
        r_from = jnp.where(code // 2 % 2 == 1, 7 - r_lane, r_lane)
        source = jnp.where(code >= 4, r_from * 8 + p_from, p_from * 8 + r_from)
        index[dim * count : (dim + 1) * count] = source + jnp.where(lanes < 64, 64, 0)
    predict(count, fields, sizes, q, par, hot_par, pack, unpack, w_high, w_low, face_table, outs, scratch)


def inner_kernel(count, fields, *refs):
    inner(count, fields, *refs)


def unpack_got(sizes, refs):
    got, at = [[None, None] for _ in sizes], 0
    for dim in EXCHANGED:
        for k in range(1 if sizes[dim][1] == 2 else 2):
            got[dim][k] = refs[at]
            at += 1
    return got, refs[at:]


def middle_kernel(count, fields, sizes, *refs):
    got, refs = unpack_got(sizes, refs)
    base, par, index, hot_par, pack, unpack, w_high, w_low, face_table, lift_table, q = refs[:11]
    outs, (halo, face_high, face_low), scratch = refs[11:-13], refs[-13:-10], refs[-10:]
    outer(count, fields, sizes, got, base, par, index, lift_table, q, halo, face_high, face_low)
    h0, l0 = scratch[:2]
    for f in range(fields):
        rows = slice(f * count, (f + 1) * count)
        h0[rows], l0[rows] = split(get(q, rows, slice(0, h0.shape[1])))
    predict(count, fields, sizes, q, par, hot_par, pack, unpack, w_high, w_low, face_table, outs, scratch)


def last_kernel(count, fields, sizes, *refs):
    got, refs = unpack_got(sizes, refs)
    base, par, index, place_back, lift_table, out, q, high, low, staged, halo, face_high, face_low, sems = refs
    outer(count, fields, sizes, got, base, par, index, lift_table, q, halo, face_high, face_low)
    done = []
    for k, start in enumerate(range(0, staged.shape[1], 256)):
        cols = slice(start, start + 256)
        for f in range(fields):
            rows = slice(f * count, (f + 1) * count)
            high[rows, cols], low[rows, cols] = split(get(q, rows, cols))
        staged[:, cols] = moved(place_back, high, cols, count, count) + moved(place_back, low, cols, count, count)
        done += fetch([(staged.at[:, cols], out.at[:, cols], sems.at[k])])
    for wait in done:
        wait.wait()


def swaps(sizes, dim, parity):
    lengths = [size for _, size in sizes]
    size, pairs = lengths[dim], []
    for place in itertools.product(*[range(length) for length in lengths]):
        other = list(place)
        other[dim] += 1 if place[dim] % 2 == parity else -1
        if not 0 <= other[dim] < size:
            if dim == 0 and lengths[1] % 2 == 0:
                other[dim], other[1] = place[dim], place[1] ^ 1
            else:
                other[dim] = other[dim] % size if size % 2 == 0 else place[dim]
        flat = [0, 0]
        for length, mine, theirs in zip(lengths, place, other):
            flat = [flat[0] * length + mine, flat[1] * length + theirs]
        pairs.append(tuple(flat))
    return pairs


def exchange(edges, sizes):
    axes = tuple(axis for axis, _ in sizes)
    got = []
    for dim in EXCHANGED:
        for parity in range(1 if sizes[dim][1] == 2 else 2):
            got.append(lax.ppermute(edges[len(got)], axes, swaps(sizes, dim, parity)))
    return got


def shards(sizes, wavefield, deriv_ops, density, lame_first, shear_modulus, high_order, element_cell, face_orient):
    count, fields, nodes = wavefield.shape[-3:]
    rows = fields * count
    wave = wavefield[0, 0, 0].swapaxes(0, 1).reshape(rows, nodes)
    half, blocks = count // 2, fields - 1
    row = lambda value: value.reshape(1, count)
    codes = face_orient.reshape(6, 1, count)
    vmem = pl.BlockSpec(memory_space=pltpu.VMEM)
    hbm = pl.BlockSpec(memory_space=pltpu.HBM)
    shape = jax.ShapeDtypeStruct
    field_shape = shape((nodes // 128, rows, 128), F32)
    edge_rows = {0: (fields + 1) // 2 * 8, 1: -(-(rows // 8) // 8) * 8, 2: rows // 4}
    predicted = [
        shape((rows, nodes), BF16),
        shape((rows, nodes), BF16),
        shape((rows, 128), F32),
        shape((rows, 128), F32),
        shape((rows, 128), F32),
    ]
    for dim in EXCHANGED:
        predicted += [shape((edge_rows[dim], 128), F32)] * (1 if sizes[dim][1] == 2 else 2)
    hot_rows = half * fields
    predict_scratch = [pltpu.VMEM((rows, nodes), BF16)] * 4 + [pltpu.VMEM(field_shape.shape, F32)]
    predict_scratch += [pltpu.VMEM((hot_rows, nodes), BF16)] * 4 + [pltpu.VMEM((hot_rows, nodes), F32)]
    face_scratch = [pltpu.VMEM((rows, 256), BF16), pltpu.VMEM((rows, 256), BF16)]
    halo_scratch = [pltpu.VMEM((rows, 128), F32)] + face_scratch

    def call(kernel, operands, in_specs, out_shape, scratch, products, name, out_spec=vmem, limit=VMEM_LIMIT):
        single = not isinstance(out_shape, list)
        return pl.pallas_call(
            kernel,
            out_shape=out_shape,
            in_specs=in_specs,
            out_specs=out_spec if single else [out_spec] * len(out_shape),
            scratch_shapes=scratch,
            compiler_params=pltpu.CompilerParams(vmem_limit_bytes=limit),
            cost_estimate=pl.CostEstimate(
                flops=products * 6 * rows * nodes * nodes * 4, bytes_accessed=4 * rows * nodes * 4, transcendentals=0
            ),
            name=name,
        )(*operands)

    w_high, w_low, face_table, lift_table = call(
        table_kernel,
        [deriv_ops],
        [hbm],
        [
            shape(deriv_ops.shape, BF16),
            shape(deriv_ops.shape, BF16),
            shape((nodes, 256), BF16),
            shape((256, nodes), BF16),
        ],
        [pltpu.VMEM(deriv_ops.shape, F32), pltpu.SemaphoreType.DMA((2 * deriv_ops.shape[0],))],
        2,
        "split_operators",
        limit=TABLE_LIMIT,
    )
    q, par, index, hot_par, place, place_back, pack, unpack, *ahead = call(
        functools.partial(first_kernel, count, fields, sizes),
        [wave, row(density), row(lame_first), row(shear_modulus), row(element_cell), row(high_order), codes]
        + [w_high, w_low, face_table],
        [vmem] * 10,
        [
            field_shape,
            shape((4 * count, 128), F32),
            shape((3 * count, 128), jnp.int32),
            shape((4 * half, 128), F32),
            shape((blocks * count, blocks * count), BF16),
            shape((blocks * count, blocks * count), BF16),
            shape((blocks * half, blocks * count), BF16),
            shape((blocks * count, blocks * half), BF16),
        ]
        + predicted,
        predict_scratch,
        4,
        "first_predictor",
    )
    for step in range(STEPS):
        traces, edges = ahead[:5], ahead[5:]
        got = exchange(edges, sizes)
        base = call(
            functools.partial(inner_kernel, count, fields),
            [q, *traces, par, index, w_high, w_low, lift_table],
            [vmem] * 11,
            field_shape,
            face_scratch,
            1,
            "inner_update",
        )
        if step < STEPS - 1:
            q, *ahead = call(
                functools.partial(middle_kernel, count, fields, sizes),
                [*got, base, par, index, hot_par, pack, unpack, w_high, w_low, face_table, lift_table],
                [vmem] * (len(got) + 10),
                [field_shape] + predicted,
                halo_scratch + predict_scratch,
                4,
                "outer_update_predictor",
            )
        else:
            out = call(
                functools.partial(last_kernel, count, fields, sizes),
                [*got, base, par, index, place_back, lift_table],
                [vmem] * (len(got) + 5),
                shape((rows, nodes), F32),
                [pltpu.VMEM(field_shape.shape, F32)]
                + [pltpu.VMEM((rows, nodes), BF16)] * 2
                + [pltpu.VMEM((rows, nodes), F32)]
                + halo_scratch
                + [pltpu.SemaphoreType.DMA((nodes // 256,))],
                1,
                "outer_update",
                hbm,
            )
    return out.reshape(fields, count, nodes).swapaxes(0, 1)[None, None, None]


def solution(mesh):
    sizes = tuple((axis, mesh.shape[axis]) for axis in mesh.axis_names)
    lead = ("gx", "gy", "ha")
    placed = (
        P(*lead, None, None, None),
        P(),
        P(*lead, None),
        P(*lead, None),
        P(*lead, None),
        P(*lead, None),
        P(*lead, None),
        P(*lead, None, None),
    )
    return jax.shard_map(
        functools.partial(shards, sizes),
        mesh=mesh,
        in_specs=placed,
        out_specs=P(*lead, None, None, None),
        check_vma=False,
    )
```

```python
import functools
import itertools
import math

import jax
import jax.numpy as jnp
from jax import lax
from jax.experimental import pallas as pl
from jax.experimental.pallas import tpu as pltpu
from jax.sharding import PartitionSpec as P

STEPS = 2
DT = 0.8
LIFT = 2.0
EXCHANGED = (2, 0, 1)
PICKED = ((0, 1, 2, 3, 6, 8), (0, 1, 2, 6, 4, 7), (0, 1, 2, 8, 7, 5))
F32 = jnp.float32
BF16 = jnp.bfloat16
VMEM_LIMIT = 24 << 20
TABLE_LIMIT = 50 << 20


def wide(column, count):
    return jnp.concatenate([column] * count, axis=1)


def get(field, rows, cols):
    return jnp.concatenate([field[t, rows, :] for t in range(cols.start // 128, cols.stop // 128)], axis=1)


def put(field, rows, cols, value):
    for t in range(cols.start // 128, cols.stop // 128):
        field[t, rows, :] = value[:, t * 128 - cols.start : (t + 1) * 128 - cols.start]


def add(field, rows, cols, value):
    put(field, rows, cols, get(field, rows, cols) + value)


def split(value):
    high = value.astype(BF16)
    return high, (value - high.astype(F32)).astype(BF16)


def dot(left, right):
    return jnp.dot(left, right, preferred_element_type=F32)


def moved(table, source, cols, rows_in, rows_out):
    body, whole = table.shape[1], source.shape[0]
    first = dot(table[...], source[0:body, cols])
    rest = dot(table[0:rows_out, 0:rows_in], source[body:whole, cols])
    return jnp.concatenate([first, rest], axis=0)


def lanes_of(rows):
    return lax.broadcasted_iota(jnp.int32, (rows, 128), 1)


def combine(deriv, rows, inv_rho, lame, shear, shear2, cols, emit):
    part = lambda dim, row: deriv[dim][row * rows : (row + 1) * rows]
    div = lame * (part(0, 0) + part(1, 1) + part(2, 2))
    emit(0, cols, inv_rho * (part(0, 3) + part(1, 3) + part(2, 3)))
    emit(1, cols, inv_rho * (part(0, 4) + part(1, 4) + part(2, 4)))
    emit(2, cols, inv_rho * (part(0, 5) + part(1, 5) + part(2, 5)))
    emit(3, cols, div + shear2 * part(0, 0))
    emit(4, cols, div + shear2 * part(1, 1))
    emit(5, cols, div + shear2 * part(2, 2))
    emit(6, cols, shear * (part(0, 1) + part(1, 0)))
    emit(7, cols, shear * (part(1, 2) + part(2, 1)))
    emit(8, cols, shear * (part(0, 2) + part(2, 0)))


def rate(high, low, w_high, w_low, par, stride, rows, emit, block=256):
    nodes = w_high.shape[-1]
    inv_rho = wide(par[0:rows], block // 128)
    lame = wide(par[stride : stride + rows], block // 128)
    shear = wide(par[2 * stride : 2 * stride + rows], block // 128)
    shear2 = 2.0 * shear
    for start in range(0, nodes, block):
        cols = slice(start, start + block)
        deriv = [None] * 3
        for k in range(0, nodes, 256):
            depth = slice(k, k + 256)
            for dim in range(3):
                top = jnp.concatenate([high[f * stride : f * stride + rows, depth] for f in PICKED[dim]], axis=0)
                rest = jnp.concatenate([low[f * stride : f * stride + rows, depth] for f in PICKED[dim]], axis=0)
                both = dot(jnp.concatenate([top, rest], axis=0), w_high[dim, depth, cols])
                part = both[: 6 * rows] + both[6 * rows :] + dot(top, w_low[dim, depth, cols])
                deriv[dim] = part if deriv[dim] is None else deriv[dim] + part
        combine(deriv, rows, inv_rho, lame, shear, shear2, cols, emit)


def correction(jump, par, count, dim, rows):
    take = lambda k: par[k * count : k * count + rows] if not isinstance(rows, slice) else par[
        k * count + rows.start : k * count + rows.stop
    ]
    inv_rho, lame, shear, half_speed = take(0), take(1), take(2), take(3)
    size = jump[0].shape[0]
    sign = jnp.where(lanes_of(size) < 64, -0.5, 0.5)
    inv_rho, lame, shear = sign * inv_rho, sign * lame, sign * shear
    stiff = lame + 2.0 * shear
    if dim == 0:
        flux = [inv_rho * jump[3], inv_rho * jump[6], inv_rho * jump[8]]
        flux += [stiff * jump[0], lame * jump[0], lame * jump[0]]
        flux += [shear * jump[1], None, shear * jump[2]]
    elif dim == 1:
        flux = [inv_rho * jump[6], inv_rho * jump[4], inv_rho * jump[7]]
        flux += [lame * jump[1], stiff * jump[1], lame * jump[1]]
        flux += [shear * jump[0], shear * jump[2], None]
    else:
        flux = [inv_rho * jump[8], inv_rho * jump[7], inv_rho * jump[5]]
        flux += [lame * jump[2], lame * jump[2], stiff * jump[2]]
        flux += [None, shear * jump[1], shear * jump[0]]
    return [
        half_speed * jump[f] if flux[f] is None else half_speed * jump[f] + flux[f] for f in range(len(jump))
    ]


def orient(value, index):
    return jnp.take_along_axis(value, index, axis=1, mode="promise_in_bounds")


def lift_edges(target, face, f, rows, count):
    lanes = lanes_of(face.shape[0])
    scaled = DT * LIFT * face
    top = slice(f * count + rows.start, f * count + rows.stop)
    last = target.shape[0] - 1
    target[0, top] = target[0, top] + jnp.where(lanes < 64, scaled, 0.0)
    target[last, top] = target[last, top] + jnp.where(lanes < 64, 0.0, scaled)


def lift_inner(target, source, face_high, face_low, lift_table):
    rows, nodes = target.shape[1], lift_table.shape[1]
    for start in range(0, nodes, 256):
        cols = slice(start, start + 256)
        lifted = dot(face_high[...], lift_table[:, cols]) + dot(face_low[...], lift_table[:, cols])
        put(target, slice(0, rows), cols, get(source, slice(0, rows), cols) + DT * LIFT * lifted)


def fetch(copies):
    started = [pltpu.make_async_copy(*copy) for copy in copies]
    for copy in started:
        copy.start()
    return started


def send(low, high, up, targets):
    minus = lanes_of(low.shape[0]) < 64
    plus_face = jnp.where(minus, pltpu.roll(low, 64, 1), high)
    minus_face = jnp.where(minus, low, pltpu.roll(high, 64, 1))
    rows = low.shape[0]
    for parity, target in enumerate(targets):
        target[0:rows] = jnp.where(up, plus_face, minus_face) if parity == 0 else jnp.where(up, minus_face, plus_face)
        if target.shape[0] > rows:
            target[rows:] = jnp.zeros((target.shape[0] - rows, 128), F32)


def received(pair, rows, axis, size):
    here = lax.axis_index(axis)
    odd = here % 2 == 1
    first = pair[0][0:rows]
    second = first if pair[1] is None else pair[1][0:rows]
    minus = lanes_of(first.shape[0]) < 64
    lower = jnp.where(odd, first, second)
    upper = jnp.where(odd, second, first)
    plus_lane = jnp.logical_and(here > 0, jnp.logical_not(minus))
    minus_lane = jnp.logical_and(here < size - 1, minus)
    return (
        (jnp.where(plus_lane, pltpu.roll(lower, 64, 1), 0.0), jnp.where(plus_lane, lower, 0.0)),
        (jnp.where(minus_lane, upper, 0.0), jnp.where(minus_lane, pltpu.roll(upper, 64, 1), 0.0)),
    )


def predict(count, fields, sizes, q, par, hot_par, pack, unpack, w_high, w_low, face_table, outs, scratch):
    int_high, int_low, trace_x, trace_y, trace_z, *edges = outs
    h0, l0, h1, l1, total, p0, p1, p2, p3, series = scratch
    nodes = h0.shape[1]
    half = count // 2

    def first(f, cols, value):
        rows = slice(f * count, (f + 1) * count)
        put(total, rows, cols, get(q, rows, cols) + DT / 2.0 * value)
        h1[rows, cols], l1[rows, cols] = split(value)

    rate(h0, l0, w_high, w_low, par, count, count, first)

    def then(f, cols, value):
        rows = slice(f * count, (f + 1) * count)
        add(total, rows, cols, DT**2 / 6.0 * value)
        h0[rows, cols], l0[rows, cols] = split(value)

    rate(h1, l1, w_high, w_low, par, count, count, then)

    for start in range(0, nodes, 256):
        cols = slice(start, start + 256)
        p0[:, cols] = moved(pack, h0, cols, count, half).astype(BF16)
        p1[:, cols] = moved(pack, l0, cols, count, half).astype(BF16)
    buffers = [(p0, p1), (p2, p3)]
    for order in (3, 4, 5):
        weight = DT**order / math.factorial(order + 1)
        source, target = buffers[(order - 3) % 2], buffers[(order - 2) % 2]

        def more(f, cols, value, order=order, weight=weight, target=target):
            rows = slice(f * half, (f + 1) * half)
            part = weight * value
            if order > 3:
                part = part + series[rows, cols]
            if order < 5:
                series[rows, cols] = part
                part = value
            target[0][rows, cols], target[1][rows, cols] = split(part)

        rate(source[0], source[1], w_high, w_low, hot_par, half, half, more)
    for start in range(0, nodes, 256):
        cols = slice(start, start + 256)
        extra = moved(unpack, p2, cols, half, count) + moved(unpack, p3, cols, half, count)
        add(total, slice(0, fields * count), cols, extra)
    for f in range(fields):
        rows = slice(f * count, (f + 1) * count)
        int_high[rows], int_low[rows] = split(get(total, rows, slice(0, nodes)))
        trace_x[rows] = jnp.where(lanes_of(count) < 64, total[0, rows], total[total.shape[0] - 1, rows])
    faces = dot(int_high[...], face_table[...]) + dot(int_low[...], face_table[...])
    trace_y[...] = faces[:, 0:128]
    trace_z[...] = faces[:, 128:256]
    targets, at = {}, 0
    for dim in EXCHANGED:
        number = 1 if sizes[dim][1] == 2 else 2
        targets[dim] = edges[at : at + number]
        at += number
    ups = [lax.axis_index(axis) % 2 == 0 for axis, _ in sizes]
    ends = []
    for f in range(fields):
        low, high = trace_x[f * count : f * count + 8], trace_x[(f + 1) * count - 8 : (f + 1) * count]
        ends.append(jnp.where(lanes_of(8) < 64, low, high))
    middle = (fields + 1) // 2
    ends.append(ends[-1])
    send(jnp.concatenate(ends[:middle]), jnp.concatenate(ends[middle : 2 * middle]), ups[0], targets[0])
    tiles = fields * count // 8
    pad = -tiles % 8
    minus = lanes_of(tiles) < 64
    ends = []
    for m in range(2):
        value = jnp.where(minus, trace_y[pl.ds(m, tiles, stride=8), :], trace_y[pl.ds(6 + m, tiles, stride=8), :])
        ends.append(jnp.concatenate([value, jnp.zeros((pad, 128), F32)]) if pad else value)
    send(ends[0], ends[1], ups[1], targets[1])
    pairs = fields * count // 4
    minus = lanes_of(pairs) < 64
    ends = []
    for start in (0, 2 * pairs):
        value = jnp.where(
            minus, trace_z[pl.ds(start, pairs, stride=2), :], trace_z[pl.ds(start + 1, pairs, stride=2), :]
        )
        ends.append(value)
    send(ends[0], ends[1], ups[2], targets[2])


def inner(count, fields, q, int_high, int_low, trace_x, trace_y, trace_z, par, index, w_high, w_low, lift_table,
          base, face_high, face_low):
    def volume(f, cols, value):
        rows = slice(f * count, (f + 1) * count)
        put(base, rows, cols, get(q, rows, cols) + DT * value)

    rate(int_high, int_low, w_high, w_low, par, count, count, volume)
    lanes = lanes_of(count)
    sub = lax.broadcasted_iota(jnp.int32, (count, 128), 0)
    minus = lanes < 64
    zero = jnp.zeros((8, 128), F32)
    for dim, trace in enumerate((trace_x, trace_y, trace_z)):
        jump = []
        for f in range(fields):
            own = trace[f * count : (f + 1) * count]
            if dim == 0:
                above = jnp.concatenate([own[8:], zero], axis=0)
                below = jnp.concatenate([zero, own[:-8]], axis=0)
            elif dim == 1:
                above = jnp.where(sub % 8 < 6, pltpu.roll(own, count - 2, 0), 0.0)
                below = jnp.where(sub % 8 < 2, 0.0, pltpu.roll(own, 2, 0))
            else:
                above = jnp.where(sub % 2 < 1, pltpu.roll(own, count - 1, 0), 0.0)
                below = jnp.where(sub % 2 < 1, 0.0, pltpu.roll(own, 1, 0))
            beside = jnp.where(minus, above, below)
            jump.append(orient(beside, index[dim * count : (dim + 1) * count]) - own)
        fixed = correction(jump, par, count, dim, count)
        for f in range(fields):
            if dim == 0:
                lift_edges(base, fixed[f], f, slice(0, count), count)
            else:
                cols = slice((dim - 1) * 128, dim * 128)
                rows = slice(f * count, (f + 1) * count)
                face_high[rows, cols], face_low[rows, cols] = split(fixed[f])
    lift_inner(base, base, face_high, face_low, lift_table)


def outer(count, fields, sizes, got, base, par, index, lift_table, out, halo, face_high, face_low):
    tiles = fields * count // 8
    pairs = fields * count // 4
    for dim in (1, 2):
        lower, upper = received(got[dim], pairs if dim == 2 else tiles + -tiles % 8, *sizes[dim])
        if dim == 1:
            halo[...] = jnp.zeros_like(halo)
            for m in range(2):
                halo[pl.ds(m, tiles, stride=8), :] = lower[m][0:tiles]
                halo[pl.ds(6 + m, tiles, stride=8), :] = upper[m][0:tiles]
        else:
            for part in range(2):
                halo[pl.ds(2 * part * pairs, pairs, stride=2), :] = lower[part]
                halo[pl.ds(2 * part * pairs + 1, pairs, stride=2), :] = upper[part]
        jump = [
            orient(halo[f * count : (f + 1) * count], index[dim * count : (dim + 1) * count]) for f in range(fields)
        ]
        fixed = correction(jump, par, count, dim, count)
        for f in range(fields):
            cols = slice((dim - 1) * 128, dim * 128)
            rows = slice(f * count, (f + 1) * count)
            face_high[rows, cols], face_low[rows, cols] = split(fixed[f])
    lift_inner(out, base, face_high, face_low, lift_table)
    middle = (fields + 1) // 2
    lower, upper = received(got[0], middle * 8, *sizes[0])
    for end, (low, high) in enumerate((lower, upper)):
        rows = slice(0, 8) if end == 0 else slice(count - 8, count)
        jump = []
        for f in range(fields):
            part, at = (low, f) if f < middle else (high, f - middle)
            jump.append(orient(part[at * 8 : at * 8 + 8], index[rows]))
        fixed = correction(jump, par, count, 0, rows)
        for f in range(fields):
            lift_edges(out, fixed[f], f, rows, count)


def table_kernel(ops_any, w_high, w_low, face_table, lift_table, ops, sems):
    dims, nodes = ops.shape[:2]
    step = nodes // 2
    parts = [(dim, slice(start, start + step)) for dim in range(dims) for start in range(0, nodes, step)]
    waits = fetch([(ops_any.at[dim, rows], ops.at[dim, rows], sems.at[k]) for k, (dim, rows) in enumerate(parts)])

    def on_face(node, column):
        i, j, k = node // 64, node // 8 % 8, node % 8
        plus = column // 64 % 2 * 7
        p, r = column % 64 // 8, column % 8
        along_y = (column < 128) & (j == plus) & (i == p) & (k == r)
        along_z = (column >= 128) & (k == plus) & (i == p) & (j == r)
        return jnp.where(along_y | along_z, 1.0, 0.0).astype(BF16)

    table = face_table.shape
    face_table[...] = on_face(lax.broadcasted_iota(jnp.int32, table, 0), lax.broadcasted_iota(jnp.int32, table, 1))
    table = table[::-1]
    lift_table[...] = on_face(lax.broadcasted_iota(jnp.int32, table, 1), lax.broadcasted_iota(jnp.int32, table, 0))
    for wait, (dim, rows) in zip(waits, parts):
        wait.wait()
        w_high[dim, rows, :], w_low[dim, rows, :] = split(ops[dim, rows, :])


def first_kernel(count, fields, sizes, wave, density, lame, shear, cell, flag, orient_code, w_high, w_low, face_table,
                 q, par, index, hot_par, place_back, pack, unpack, *rest):
    outs, place, scratch = rest[:-11], rest[-11], rest[-10:]
    h0, l0, h1, l1 = scratch[:4]
    half, blocks = count // 2, fields - 1
    iota = lambda shape, axis: lax.broadcasted_iota(jnp.int32, shape, axis)
    ones = lambda mask: jnp.where(mask, 1.0, 0.0).astype(BF16)
    cells = cell[...]
    square = (count, count)
    tiled = dot(
        jnp.broadcast_to(cells.astype(F32).astype(BF16), (8, count)),
        ones(iota((count, blocks * count), 1) % count == iota((count, blocks * count), 0)),
    )[0:1].astype(jnp.int32)
    shape = place.shape
    target = tiled + iota((1, shape[1]), 1) // count * count
    place[...] = ones(iota(shape, 0) == target)
    for f in range(fields):
        rows = slice(f * count, (f + 1) * count)
        h1[rows], l1[rows] = split(wave[rows])
    for start in range(0, h0.shape[1], 256):
        cols = slice(start, start + 256)
        high = moved(place, h1, cols, count, count)
        low = moved(place, l1, cols, count, count)
        h0[:, cols], l0[:, cols] = high.astype(BF16), low.astype(BF16)
        put(q, slice(0, fields * count), cols, high + low)

    fills = cells == iota(square, 0)
    gather = lambda mask, row: jnp.sum(jnp.where(mask, row, 0.0), axis=1, keepdims=True)
    in_cell = lambda row: jnp.broadcast_to(gather(fills, row), (count, 128))
    inv_row = 1.0 / density[...]
    inv_rho = in_cell(inv_row)
    lame_col = in_cell(lame[...])
    shear_col = in_cell(shear[...])
    par[0:count] = inv_rho
    par[count : 2 * count] = lame_col
    par[2 * count : 3 * count] = shear_col
    par[3 * count : 4 * count] = 0.5 * jnp.sqrt((lame_col + 2.0 * shear_col) * inv_rho)

    flags = flag[...].astype(F32)
    before = ones(iota(square, 0) < iota(square, 1))
    rank = dot(jnp.broadcast_to(flags.astype(BF16), (8, count)), before)[0:1]
    slots = (rank.astype(jnp.int32) == iota((half, count), 0)) & (flags > 0.0)
    in_slot = lambda row: jnp.broadcast_to(gather(slots, row), (half, 128))
    hot_par[0:half] = in_slot(inv_row)
    hot_par[half : 2 * half] = in_slot(lame[...])
    hot_par[2 * half : 3 * half] = in_slot(shear[...])
    hot_par[3 * half : 4 * half] = in_slot(flags)
    twice = lambda column, times: jnp.concatenate([column] * times, axis=0).astype(jnp.int32)
    shape = pack.shape
    target = twice(in_slot(cells.astype(F32)), blocks) + iota((shape[0], 128), 0) // half * count
    used = twice(in_slot(flags), blocks) > 0
    target = jnp.where(used, target, -1)
    pack[...] = ones(iota(shape, 1) == wide(target, shape[1] // 128))
    shape = unpack.shape
    target = twice(in_cell(rank), blocks) + iota((shape[0], 128), 0) // count * half
    target = jnp.where(twice(in_cell(flags), blocks) > 0, target, -1)
    unpack[...] = ones(iota(shape, 1) == wide(target, shape[1] // 128))
    own = gather(iota(square, 0) == iota(square, 1), cells.astype(F32))
    shape = place_back.shape
    target = twice(jnp.broadcast_to(own, (count, 128)), blocks) + iota((shape[0], 128), 0) // count * count
    place_back[...] = ones(iota(shape, 1) == wide(target, shape[1] // 128))

    lanes = lanes_of(count)
    p_lane, r_lane = lanes % 64 // 8, lanes % 8
    for dim in range(3):
        code = jnp.where(
            lanes < 64,
            in_cell(orient_code[2 * dim].astype(F32)),
            in_cell(orient_code[2 * dim + 1].astype(F32)),
        ).astype(jnp.int32)
        p_from = jnp.where(code % 2 == 1, 7 - p_lane, p_lane)
        r_from = jnp.where(code // 2 % 2 == 1, 7 - r_lane, r_lane)
        source = jnp.where(code >= 4, r_from * 8 + p_from, p_from * 8 + r_from)
        index[dim * count : (dim + 1) * count] = source + jnp.where(lanes < 64, 64, 0)
    predict(count, fields, sizes, q, par, hot_par, pack, unpack, w_high, w_low, face_table, outs, scratch)


def inner_kernel(count, fields, *refs):
    inner(count, fields, *refs)


def unpack_got(sizes, refs):
    got, at = [[None, None] for _ in sizes], 0
    for dim in EXCHANGED:
        for k in range(1 if sizes[dim][1] == 2 else 2):
            got[dim][k] = refs[at]
            at += 1
    return got, refs[at:]


def middle_kernel(count, fields, sizes, *refs):
    got, refs = unpack_got(sizes, refs)
    base, par, index, hot_par, pack, unpack, w_high, w_low, face_table, lift_table, q = refs[:11]
    outs, (halo, face_high, face_low), scratch = refs[11:-13], refs[-13:-10], refs[-10:]
    outer(count, fields, sizes, got, base, par, index, lift_table, q, halo, face_high, face_low)
    h0, l0 = scratch[:2]
    for f in range(fields):
        rows = slice(f * count, (f + 1) * count)
        h0[rows], l0[rows] = split(get(q, rows, slice(0, h0.shape[1])))
    predict(count, fields, sizes, q, par, hot_par, pack, unpack, w_high, w_low, face_table, outs, scratch)


def last_kernel(count, fields, sizes, *refs):
    got, refs = unpack_got(sizes, refs)
    base, par, index, place_back, lift_table, out, q, high, low, staged, halo, face_high, face_low, sems = refs
    outer(count, fields, sizes, got, base, par, index, lift_table, q, halo, face_high, face_low)
    done = []
    for k, start in enumerate(range(0, staged.shape[1], 256)):
        cols = slice(start, start + 256)
        for f in range(fields):
            rows = slice(f * count, (f + 1) * count)
            high[rows, cols], low[rows, cols] = split(get(q, rows, cols))
        staged[:, cols] = moved(place_back, high, cols, count, count) + moved(place_back, low, cols, count, count)
        done += fetch([(staged.at[:, cols], out.at[:, cols], sems.at[k])])
    for wait in done:
        wait.wait()


def swaps(sizes, dim, parity):
    lengths = [size for _, size in sizes]
    size, pairs = lengths[dim], []
    for place in itertools.product(*[range(length) for length in lengths]):
        other = list(place)
        other[dim] += 1 if place[dim] % 2 == parity else -1
        if not 0 <= other[dim] < size:
            if dim == 0 and lengths[1] % 2 == 0:
                other[dim], other[1] = place[dim], place[1] ^ 1
            else:
                other[dim] = other[dim] % size if size % 2 == 0 else place[dim]
        flat = [0, 0]
        for length, mine, theirs in zip(lengths, place, other):
            flat = [flat[0] * length + mine, flat[1] * length + theirs]
        pairs.append(tuple(flat))
    return pairs


def exchange(edges, sizes):
    axes = tuple(axis for axis, _ in sizes)
    got = []
    for dim in EXCHANGED:
        for parity in range(1 if sizes[dim][1] == 2 else 2):
            got.append(lax.ppermute(edges[len(got)], axes, swaps(sizes, dim, parity)))
    return got


def shards(sizes, wavefield, deriv_ops, density, lame_first, shear_modulus, high_order, element_cell, face_orient):
    count, fields, nodes = wavefield.shape[-3:]
    rows = fields * count
    wave = wavefield[0, 0, 0].swapaxes(0, 1).reshape(rows, nodes)
    half, blocks = count // 2, fields - 1
    row = lambda value: value.reshape(1, count)
    codes = face_orient.reshape(6, 1, count)
    vmem = pl.BlockSpec(memory_space=pltpu.VMEM)
    hbm = pl.BlockSpec(memory_space=pltpu.HBM)
    shape = jax.ShapeDtypeStruct
    field_shape = shape((nodes // 128, rows, 128), F32)
    edge_rows = {0: (fields + 1) // 2 * 8, 1: -(-(rows // 8) // 8) * 8, 2: rows // 4}
    predicted = [
        shape((rows, nodes), BF16),
        shape((rows, nodes), BF16),
        shape((rows, 128), F32),
        shape((rows, 128), F32),
        shape((rows, 128), F32),
    ]
    for dim in EXCHANGED:
        for parity in range(1 if sizes[dim][1] == 2 else 2):
            padded = edge_rows[dim] if (dim, parity) == (1, 1) else max(edge_rows.values())
            predicted.append(shape((padded, 128), F32))
    hot_rows = half * fields
    predict_scratch = [pltpu.VMEM((rows, nodes), BF16)] * 4 + [pltpu.VMEM(field_shape.shape, F32)]
    predict_scratch += [pltpu.VMEM((hot_rows, nodes), BF16)] * 4 + [pltpu.VMEM((hot_rows, nodes), F32)]
    face_scratch = [pltpu.VMEM((rows, 256), BF16), pltpu.VMEM((rows, 256), BF16)]
    halo_scratch = [pltpu.VMEM((rows, 128), F32)] + face_scratch

    def call(kernel, operands, in_specs, out_shape, scratch, products, name, out_spec=vmem, limit=VMEM_LIMIT):
        single = not isinstance(out_shape, list)
        return pl.pallas_call(
            kernel,
            out_shape=out_shape,
            in_specs=in_specs,
            out_specs=out_spec if single else [out_spec] * len(out_shape),
            scratch_shapes=scratch,
            compiler_params=pltpu.CompilerParams(vmem_limit_bytes=limit),
            cost_estimate=pl.CostEstimate(
                flops=products * 6 * rows * nodes * nodes * 4, bytes_accessed=4 * rows * nodes * 4, transcendentals=0
            ),
            name=name,
        )(*operands)

    w_high, w_low, face_table, lift_table = call(
        table_kernel,
        [deriv_ops],
        [hbm],
        [
            shape(deriv_ops.shape, BF16),
            shape(deriv_ops.shape, BF16),
            shape((nodes, 256), BF16),
            shape((256, nodes), BF16),
        ],
        [pltpu.VMEM(deriv_ops.shape, F32), pltpu.SemaphoreType.DMA((2 * deriv_ops.shape[0],))],
        2,
        "split_operators",
        limit=TABLE_LIMIT,
    )
    q, par, index, hot_par, place_back, pack, unpack, *ahead = call(
        functools.partial(first_kernel, count, fields, sizes),
        [wave, row(density), row(lame_first), row(shear_modulus), row(element_cell), row(high_order), codes]
        + [w_high, w_low, face_table],
        [vmem] * 10,
        [
            field_shape,
            shape((4 * count, 128), F32),
            shape((3 * count, 128), jnp.int32),
            shape((4 * half, 128), F32),
            shape((blocks * count, blocks * count), BF16),
            shape((blocks * half, blocks * count), BF16),
            shape((blocks * count, blocks * half), BF16),
        ]
        + predicted,
        [pltpu.VMEM((blocks * count, blocks * count), BF16)] + predict_scratch,
        4,
        "first_predictor",
    )
    for step in range(STEPS):
        traces, edges = ahead[:5], ahead[5:]
        got = exchange(edges, sizes)
        base = call(
            functools.partial(inner_kernel, count, fields),
            [q, *traces, par, index, w_high, w_low, lift_table],
            [vmem] * 11,
            field_shape,
            face_scratch,
            1,
            "inner_update",
        )
        if step < STEPS - 1:
            q, *ahead = call(
                functools.partial(middle_kernel, count, fields, sizes),
                [*got, base, par, index, hot_par, pack, unpack, w_high, w_low, face_table, lift_table],
                [vmem] * (len(got) + 10),
                [field_shape] + predicted,
                halo_scratch + predict_scratch,
                4,
                "outer_update_predictor",
            )
        else:
            out = call(
                functools.partial(last_kernel, count, fields, sizes),
                [*got, base, par, index, place_back, lift_table],
                [vmem] * (len(got) + 5),
                shape((rows, nodes), F32),
                [pltpu.VMEM(field_shape.shape, F32)]
                + [pltpu.VMEM((rows, nodes), BF16)] * 2
                + [pltpu.VMEM((rows, nodes), F32)]
                + halo_scratch
                + [pltpu.SemaphoreType.DMA((nodes // 256,))],
                1,
                "outer_update",
                hbm,
            )
    return out.reshape(fields, count, nodes).swapaxes(0, 1)[None, None, None]


def solution(mesh):
    sizes = tuple((axis, mesh.shape[axis]) for axis in mesh.axis_names)
    lead = ("gx", "gy", "ha")
    placed = (
        P(*lead, None, None, None),
        P(),
        P(*lead, None),
        P(*lead, None),
        P(*lead, None),
        P(*lead, None),
        P(*lead, None),
        P(*lead, None, None),
    )
    return jax.shard_map(
        functools.partial(shards, sizes),
        mesh=mesh,
        in_specs=placed,
        out_specs=P(*lead, None, None, None),
        check_vma=False,
    )
```

```python
import functools
import itertools
import math

import jax
import jax.numpy as jnp
from jax import lax
from jax.experimental import pallas as pl
from jax.experimental.pallas import tpu as pltpu
from jax.sharding import PartitionSpec as P

STEPS = 2
DT = 0.8
LIFT = 2.0
ORDER = ((1, 1), (2, 0), (2, 1), (0, 0), (0, 1), (1, 0))
PICKED = ((0, 1, 2, 3, 6, 8), (0, 1, 2, 6, 4, 7), (0, 1, 2, 8, 7, 5))
F32 = jnp.float32
BF16 = jnp.bfloat16
VMEM_LIMIT = 24 << 20
TABLE_LIMIT = 50 << 20


def wide(column, count):
    return jnp.concatenate([column] * count, axis=1)


def get(field, rows, cols):
    return jnp.concatenate([field[t, rows, :] for t in range(cols.start // 128, cols.stop // 128)], axis=1)


def put(field, rows, cols, value):
    for t in range(cols.start // 128, cols.stop // 128):
        field[t, rows, :] = value[:, t * 128 - cols.start : (t + 1) * 128 - cols.start]


def add(field, rows, cols, value):
    put(field, rows, cols, get(field, rows, cols) + value)


def split(value):
    high = value.astype(BF16)
    return high, (value - high.astype(F32)).astype(BF16)


def dot(left, right):
    return jnp.dot(left, right, preferred_element_type=F32)


def moved(table, source, cols, rows_in, rows_out):
    body, whole = table.shape[1], source.shape[0]
    first = dot(table[...], source[0:body, cols])
    rest = dot(table[0:rows_out, 0:rows_in], source[body:whole, cols])
    return jnp.concatenate([first, rest], axis=0)


def lanes_of(rows):
    return lax.broadcasted_iota(jnp.int32, (rows, 128), 1)


def combine(deriv, rows, inv_rho, lame, shear, shear2, cols, emit):
    part = lambda dim, row: deriv[dim][row * rows : (row + 1) * rows]
    div = lame * (part(0, 0) + part(1, 1) + part(2, 2))
    emit(0, cols, inv_rho * (part(0, 3) + part(1, 3) + part(2, 3)))
    emit(1, cols, inv_rho * (part(0, 4) + part(1, 4) + part(2, 4)))
    emit(2, cols, inv_rho * (part(0, 5) + part(1, 5) + part(2, 5)))
    emit(3, cols, div + shear2 * part(0, 0))
    emit(4, cols, div + shear2 * part(1, 1))
    emit(5, cols, div + shear2 * part(2, 2))
    emit(6, cols, shear * (part(0, 1) + part(1, 0)))
    emit(7, cols, shear * (part(1, 2) + part(2, 1)))
    emit(8, cols, shear * (part(0, 2) + part(2, 0)))


def rate(high, low, w_high, w_low, par, stride, rows, emit, block=256):
    nodes = w_high.shape[-1]
    inv_rho = wide(par[0:rows], block // 128)
    lame = wide(par[stride : stride + rows], block // 128)
    shear = wide(par[2 * stride : 2 * stride + rows], block // 128)
    shear2 = 2.0 * shear
    for start in range(0, nodes, block):
        cols = slice(start, start + block)
        deriv = [None] * 3
        for k in range(0, nodes, 256):
            depth = slice(k, k + 256)
            for dim in range(3):
                top = jnp.concatenate([high[f * stride : f * stride + rows, depth] for f in PICKED[dim]], axis=0)
                rest = jnp.concatenate([low[f * stride : f * stride + rows, depth] for f in PICKED[dim]], axis=0)
                both = dot(jnp.concatenate([top, rest], axis=0), w_high[dim, depth, cols])
                part = both[: 6 * rows] + both[6 * rows :] + dot(top, w_low[dim, depth, cols])
                deriv[dim] = part if deriv[dim] is None else deriv[dim] + part
        combine(deriv, rows, inv_rho, lame, shear, shear2, cols, emit)


def correction(jump, par, count, dim, rows):
    take = lambda k: par[k * count : k * count + rows] if not isinstance(rows, slice) else par[
        k * count + rows.start : k * count + rows.stop
    ]
    inv_rho, lame, shear, half_speed = take(0), take(1), take(2), take(3)
    size = jump[0].shape[0]
    sign = jnp.where(lanes_of(size) < 64, -0.5, 0.5)
    inv_rho, lame, shear = sign * inv_rho, sign * lame, sign * shear
    stiff = lame + 2.0 * shear
    if dim == 0:
        flux = [inv_rho * jump[3], inv_rho * jump[6], inv_rho * jump[8]]
        flux += [stiff * jump[0], lame * jump[0], lame * jump[0]]
        flux += [shear * jump[1], None, shear * jump[2]]
    elif dim == 1:
        flux = [inv_rho * jump[6], inv_rho * jump[4], inv_rho * jump[7]]
        flux += [lame * jump[1], stiff * jump[1], lame * jump[1]]
        flux += [shear * jump[0], shear * jump[2], None]
    else:
        flux = [inv_rho * jump[8], inv_rho * jump[7], inv_rho * jump[5]]
        flux += [lame * jump[2], lame * jump[2], stiff * jump[2]]
        flux += [None, shear * jump[1], shear * jump[0]]
    return [
        half_speed * jump[f] if flux[f] is None else half_speed * jump[f] + flux[f] for f in range(len(jump))
    ]


def orient(value, index):
    return jnp.take_along_axis(value, index, axis=1, mode="promise_in_bounds")


def lift_edges(target, face, f, rows, count):
    lanes = lanes_of(face.shape[0])
    scaled = DT * LIFT * face
    top = slice(f * count + rows.start, f * count + rows.stop)
    last = target.shape[0] - 1
    target[0, top] = target[0, top] + jnp.where(lanes < 64, scaled, 0.0)
    target[last, top] = target[last, top] + jnp.where(lanes < 64, 0.0, scaled)


def lift_inner(target, source, face_high, face_low, lift_table):
    rows, nodes = target.shape[1], lift_table.shape[1]
    for start in range(0, nodes, 256):
        cols = slice(start, start + 256)
        lifted = dot(face_high[...], lift_table[:, cols]) + dot(face_low[...], lift_table[:, cols])
        put(target, slice(0, rows), cols, get(source, slice(0, rows), cols) + DT * LIFT * lifted)


def exchanges(sizes):
    return [(dim, parity) for dim, parity in ORDER if parity == 0 or sizes[dim][1] > 2]


def fetch(copies):
    started = [pltpu.make_async_copy(*copy) for copy in copies]
    for copy in started:
        copy.start()
    return started


def send(low, high, up, targets):
    minus = lanes_of(low.shape[0]) < 64
    plus_face = jnp.where(minus, pltpu.roll(low, 64, 1), high)
    minus_face = jnp.where(minus, low, pltpu.roll(high, 64, 1))
    rows = low.shape[0]
    for parity, target in enumerate(targets):
        if target is None:
            continue
        target[0:rows] = jnp.where(up, plus_face, minus_face) if parity == 0 else jnp.where(up, minus_face, plus_face)
        if target.shape[0] > rows:
            target[rows:] = jnp.zeros((target.shape[0] - rows, 128), F32)


def received(pair, rows, axis, size):
    here = lax.axis_index(axis)
    odd = here % 2 == 1
    first = pair[0][0:rows]
    second = first if pair[1] is None else pair[1][0:rows]
    minus = lanes_of(first.shape[0]) < 64
    lower = jnp.where(odd, first, second)
    upper = jnp.where(odd, second, first)
    plus_lane = jnp.logical_and(here > 0, jnp.logical_not(minus))
    minus_lane = jnp.logical_and(here < size - 1, minus)
    return (
        (jnp.where(plus_lane, pltpu.roll(lower, 64, 1), 0.0), jnp.where(plus_lane, lower, 0.0)),
        (jnp.where(minus_lane, upper, 0.0), jnp.where(minus_lane, pltpu.roll(upper, 64, 1), 0.0)),
    )


def predict(count, fields, sizes, q, par, hot_par, pack, unpack, w_high, w_low, face_table, outs, scratch):
    int_high, int_low, trace_x, trace_y, trace_z, *edges = outs
    h0, l0, h1, l1, total, p0, p1, p2, p3, series = scratch
    nodes = h0.shape[1]
    half = count // 2

    def first(f, cols, value):
        rows = slice(f * count, (f + 1) * count)
        put(total, rows, cols, get(q, rows, cols) + DT / 2.0 * value)
        h1[rows, cols], l1[rows, cols] = split(value)

    rate(h0, l0, w_high, w_low, par, count, count, first)

    def then(f, cols, value):
        rows = slice(f * count, (f + 1) * count)
        add(total, rows, cols, DT**2 / 6.0 * value)
        h0[rows, cols], l0[rows, cols] = split(value)

    rate(h1, l1, w_high, w_low, par, count, count, then)

    for start in range(0, nodes, 256):
        cols = slice(start, start + 256)
        p0[:, cols] = moved(pack, h0, cols, count, half).astype(BF16)
        p1[:, cols] = moved(pack, l0, cols, count, half).astype(BF16)
    buffers = [(p0, p1), (p2, p3)]
    for order in (3, 4, 5):
        weight = DT**order / math.factorial(order + 1)
        source, target = buffers[(order - 3) % 2], buffers[(order - 2) % 2]

        def more(f, cols, value, order=order, weight=weight, target=target):
            rows = slice(f * half, (f + 1) * half)
            part = weight * value
            if order > 3:
                part = part + series[rows, cols]
            if order < 5:
                series[rows, cols] = part
                part = value
            target[0][rows, cols], target[1][rows, cols] = split(part)

        rate(source[0], source[1], w_high, w_low, hot_par, half, half, more)
    for start in range(0, nodes, 256):
        cols = slice(start, start + 256)
        extra = moved(unpack, p2, cols, half, count) + moved(unpack, p3, cols, half, count)
        add(total, slice(0, fields * count), cols, extra)
    for f in range(fields):
        rows = slice(f * count, (f + 1) * count)
        int_high[rows], int_low[rows] = split(get(total, rows, slice(0, nodes)))
        trace_x[rows] = jnp.where(lanes_of(count) < 64, total[0, rows], total[total.shape[0] - 1, rows])
    faces = dot(int_high[...], face_table[...]) + dot(int_low[...], face_table[...])
    trace_y[...] = faces[:, 0:128]
    trace_z[...] = faces[:, 128:256]
    targets = [[None, None] for _ in sizes]
    for (dim, parity), edge in zip(exchanges(sizes), edges):
        targets[dim][parity] = edge
    ups = [lax.axis_index(axis) % 2 == 0 for axis, _ in sizes]
    ends = []
    for f in range(fields):
        low, high = trace_x[f * count : f * count + 8], trace_x[(f + 1) * count - 8 : (f + 1) * count]
        ends.append(jnp.where(lanes_of(8) < 64, low, high))
    middle = (fields + 1) // 2
    ends.append(ends[-1])
    send(jnp.concatenate(ends[:middle]), jnp.concatenate(ends[middle : 2 * middle]), ups[0], targets[0])
    tiles = fields * count // 8
    pad = -tiles % 8
    minus = lanes_of(tiles) < 64
    ends = []
    for m in range(2):
        value = jnp.where(minus, trace_y[pl.ds(m, tiles, stride=8), :], trace_y[pl.ds(6 + m, tiles, stride=8), :])
        ends.append(jnp.concatenate([value, jnp.zeros((pad, 128), F32)]) if pad else value)
    send(ends[0], ends[1], ups[1], targets[1])
    pairs = fields * count // 4
    minus = lanes_of(pairs) < 64
    ends = []
    for start in (0, 2 * pairs):
        value = jnp.where(
            minus, trace_z[pl.ds(start, pairs, stride=2), :], trace_z[pl.ds(start + 1, pairs, stride=2), :]
        )
        ends.append(value)
    send(ends[0], ends[1], ups[2], targets[2])


def inner(count, fields, q, int_high, int_low, trace_x, trace_y, trace_z, par, index, w_high, w_low, lift_table,
          base, face_high, face_low):
    def volume(f, cols, value):
        rows = slice(f * count, (f + 1) * count)
        put(base, rows, cols, get(q, rows, cols) + DT * value)

    rate(int_high, int_low, w_high, w_low, par, count, count, volume)
    lanes = lanes_of(count)
    sub = lax.broadcasted_iota(jnp.int32, (count, 128), 0)
    minus = lanes < 64
    zero = jnp.zeros((8, 128), F32)
    for dim, trace in enumerate((trace_x, trace_y, trace_z)):
        jump = []
        for f in range(fields):
            own = trace[f * count : (f + 1) * count]
            if dim == 0:
                above = jnp.concatenate([own[8:], zero], axis=0)
                below = jnp.concatenate([zero, own[:-8]], axis=0)
            elif dim == 1:
                above = jnp.where(sub % 8 < 6, pltpu.roll(own, count - 2, 0), 0.0)
                below = jnp.where(sub % 8 < 2, 0.0, pltpu.roll(own, 2, 0))
            else:
                above = jnp.where(sub % 2 < 1, pltpu.roll(own, count - 1, 0), 0.0)
                below = jnp.where(sub % 2 < 1, 0.0, pltpu.roll(own, 1, 0))
            beside = jnp.where(minus, above, below)
            jump.append(orient(beside, index[dim * count : (dim + 1) * count]) - own)
        fixed = correction(jump, par, count, dim, count)
        for f in range(fields):
            if dim == 0:
                lift_edges(base, fixed[f], f, slice(0, count), count)
            else:
                cols = slice((dim - 1) * 128, dim * 128)
                rows = slice(f * count, (f + 1) * count)
                face_high[rows, cols], face_low[rows, cols] = split(fixed[f])
    lift_inner(base, base, face_high, face_low, lift_table)


def outer(count, fields, sizes, got, base, par, index, lift_table, out, halo, face_high, face_low):
    tiles = fields * count // 8
    pairs = fields * count // 4
    for dim in (1, 2):
        lower, upper = received(got[dim], pairs if dim == 2 else tiles + -tiles % 8, *sizes[dim])
        if dim == 1:
            halo[...] = jnp.zeros_like(halo)
            for m in range(2):
                halo[pl.ds(m, tiles, stride=8), :] = lower[m][0:tiles]
                halo[pl.ds(6 + m, tiles, stride=8), :] = upper[m][0:tiles]
        else:
            for part in range(2):
                halo[pl.ds(2 * part * pairs, pairs, stride=2), :] = lower[part]
                halo[pl.ds(2 * part * pairs + 1, pairs, stride=2), :] = upper[part]
        jump = [
            orient(halo[f * count : (f + 1) * count], index[dim * count : (dim + 1) * count]) for f in range(fields)
        ]
        fixed = correction(jump, par, count, dim, count)
        for f in range(fields):
            cols = slice((dim - 1) * 128, dim * 128)
            rows = slice(f * count, (f + 1) * count)
            face_high[rows, cols], face_low[rows, cols] = split(fixed[f])
    lift_inner(out, base, face_high, face_low, lift_table)
    middle = (fields + 1) // 2
    lower, upper = received(got[0], middle * 8, *sizes[0])
    for end, (low, high) in enumerate((lower, upper)):
        rows = slice(0, 8) if end == 0 else slice(count - 8, count)
        jump = []
        for f in range(fields):
            part, at = (low, f) if f < middle else (high, f - middle)
            jump.append(orient(part[at * 8 : at * 8 + 8], index[rows]))
        fixed = correction(jump, par, count, 0, rows)
        for f in range(fields):
            lift_edges(out, fixed[f], f, rows, count)


def table_kernel(ops_any, w_high, w_low, face_table, lift_table, ops, sems):
    dims, nodes = ops.shape[:2]
    step = nodes // 4
    parts = [(dim, slice(start, start + step)) for dim in range(dims) for start in range(0, nodes, step)]
    waits = fetch([(ops_any.at[dim, rows], ops.at[dim, rows], sems.at[k]) for k, (dim, rows) in enumerate(parts)])

    def on_face(node, column):
        i, j, k = node // 64, node // 8 % 8, node % 8
        plus = column // 64 % 2 * 7
        p, r = column % 64 // 8, column % 8
        along_y = (column < 128) & (j == plus) & (i == p) & (k == r)
        along_z = (column >= 128) & (k == plus) & (i == p) & (j == r)
        return jnp.where(along_y | along_z, 1.0, 0.0).astype(BF16)

    table = face_table.shape
    face_table[...] = on_face(lax.broadcasted_iota(jnp.int32, table, 0), lax.broadcasted_iota(jnp.int32, table, 1))
    table = table[::-1]
    lift_table[...] = on_face(lax.broadcasted_iota(jnp.int32, table, 1), lax.broadcasted_iota(jnp.int32, table, 0))
    for wait, (dim, rows) in zip(waits, parts):
        wait.wait()
        w_high[dim, rows, :], w_low[dim, rows, :] = split(ops[dim, rows, :])


def first_kernel(count, fields, sizes, wave, density, lame, shear, cell, flag, orient_code, w_high, w_low, face_table,
                 q, par, index, hot_par, place_back, pack, unpack, *rest):
    outs, place, scratch = rest[:-11], rest[-11], rest[-10:]
    h0, l0, h1, l1 = scratch[:4]
    half, blocks = count // 2, fields - 1
    iota = lambda shape, axis: lax.broadcasted_iota(jnp.int32, shape, axis)
    ones = lambda mask: jnp.where(mask, 1.0, 0.0).astype(BF16)
    cells = cell[...]
    square = (count, count)
    tiled = dot(
        jnp.broadcast_to(cells.astype(F32).astype(BF16), (8, count)),
        ones(iota((count, blocks * count), 1) % count == iota((count, blocks * count), 0)),
    )[0:1].astype(jnp.int32)
    shape = place.shape
    target = tiled + iota((1, shape[1]), 1) // count * count
    place[...] = ones(iota(shape, 0) == target)
    for f in range(fields):
        rows = slice(f * count, (f + 1) * count)
        h1[rows], l1[rows] = split(wave[rows])
    for start in range(0, h0.shape[1], 256):
        cols = slice(start, start + 256)
        high = moved(place, h1, cols, count, count)
        low = moved(place, l1, cols, count, count)
        h0[:, cols], l0[:, cols] = high.astype(BF16), low.astype(BF16)
        put(q, slice(0, fields * count), cols, high + low)

    fills = cells == iota(square, 0)
    gather = lambda mask, row: jnp.sum(jnp.where(mask, row, 0.0), axis=1, keepdims=True)
    in_cell = lambda row: jnp.broadcast_to(gather(fills, row), (count, 128))
    inv_row = 1.0 / density[...]
    inv_rho = in_cell(inv_row)
    lame_col = in_cell(lame[...])
    shear_col = in_cell(shear[...])
    par[0:count] = inv_rho
    par[count : 2 * count] = lame_col
    par[2 * count : 3 * count] = shear_col
    par[3 * count : 4 * count] = 0.5 * jnp.sqrt((lame_col + 2.0 * shear_col) * inv_rho)

    flags = flag[...].astype(F32)
    before = ones(iota(square, 0) < iota(square, 1))
    rank = dot(jnp.broadcast_to(flags.astype(BF16), (8, count)), before)[0:1]
    slots = (rank.astype(jnp.int32) == iota((half, count), 0)) & (flags > 0.0)
    in_slot = lambda row: jnp.broadcast_to(gather(slots, row), (half, 128))
    hot_par[0:half] = in_slot(inv_row)
    hot_par[half : 2 * half] = in_slot(lame[...])
    hot_par[2 * half : 3 * half] = in_slot(shear[...])
    hot_par[3 * half : 4 * half] = in_slot(flags)
    twice = lambda column, times: jnp.concatenate([column] * times, axis=0).astype(jnp.int32)
    shape = pack.shape
    target = twice(in_slot(cells.astype(F32)), blocks) + iota((shape[0], 128), 0) // half * count
    used = twice(in_slot(flags), blocks) > 0
    target = jnp.where(used, target, -1)
    pack[...] = ones(iota(shape, 1) == wide(target, shape[1] // 128))
    shape = unpack.shape
    target = twice(in_cell(rank), blocks) + iota((shape[0], 128), 0) // count * half
    target = jnp.where(twice(in_cell(flags), blocks) > 0, target, -1)
    unpack[...] = ones(iota(shape, 1) == wide(target, shape[1] // 128))
    own = gather(iota(square, 0) == iota(square, 1), cells.astype(F32))
    shape = place_back.shape
    target = twice(jnp.broadcast_to(own, (count, 128)), blocks) + iota((shape[0], 128), 0) // count * count
    place_back[...] = ones(iota(shape, 1) == wide(target, shape[1] // 128))

    lanes = lanes_of(count)
    p_lane, r_lane = lanes % 64 // 8, lanes % 8
    for dim in range(3):
        code = jnp.where(
            lanes < 64,
            in_cell(orient_code[2 * dim].astype(F32)),
            in_cell(orient_code[2 * dim + 1].astype(F32)),
        ).astype(jnp.int32)
        p_from = jnp.where(code % 2 == 1, 7 - p_lane, p_lane)
        r_from = jnp.where(code // 2 % 2 == 1, 7 - r_lane, r_lane)
        source = jnp.where(code >= 4, r_from * 8 + p_from, p_from * 8 + r_from)
        index[dim * count : (dim + 1) * count] = source + jnp.where(lanes < 64, 64, 0)
    predict(count, fields, sizes, q, par, hot_par, pack, unpack, w_high, w_low, face_table, outs, scratch)


def inner_kernel(count, fields, *refs):
    inner(count, fields, *refs)


def unpack_got(sizes, refs):
    got = [[None, None] for _ in sizes]
    places = exchanges(sizes)
    for (dim, parity), ref in zip(places, refs):
        got[dim][parity] = ref
    return got, refs[len(places) :]


def middle_kernel(count, fields, sizes, *refs):
    got, refs = unpack_got(sizes, refs)
    base, par, index, hot_par, pack, unpack, w_high, w_low, face_table, lift_table, q = refs[:11]
    outs, (halo, face_high, face_low), scratch = refs[11:-13], refs[-13:-10], refs[-10:]
    outer(count, fields, sizes, got, base, par, index, lift_table, q, halo, face_high, face_low)
    h0, l0 = scratch[:2]
    for f in range(fields):
        rows = slice(f * count, (f + 1) * count)
        h0[rows], l0[rows] = split(get(q, rows, slice(0, h0.shape[1])))
    predict(count, fields, sizes, q, par, hot_par, pack, unpack, w_high, w_low, face_table, outs, scratch)


def last_kernel(count, fields, sizes, *refs):
    got, refs = unpack_got(sizes, refs)
    base, par, index, place_back, lift_table, out, q, high, low, staged, halo, face_high, face_low, sems = refs
    outer(count, fields, sizes, got, base, par, index, lift_table, q, halo, face_high, face_low)
    done = []
    for k, start in enumerate(range(0, staged.shape[1], 256)):
        cols = slice(start, start + 256)
        for f in range(fields):
            rows = slice(f * count, (f + 1) * count)
            high[rows, cols], low[rows, cols] = split(get(q, rows, cols))
        staged[:, cols] = moved(place_back, high, cols, count, count) + moved(place_back, low, cols, count, count)
        done += fetch([(staged.at[:, cols], out.at[:, cols], sems.at[k])])
    for wait in done:
        wait.wait()


def swaps(sizes, dim, parity):
    lengths = [size for _, size in sizes]
    size, pairs = lengths[dim], []
    for place in itertools.product(*[range(length) for length in lengths]):
        other = list(place)
        other[dim] += 1 if place[dim] % 2 == parity else -1
        if not 0 <= other[dim] < size:
            if dim == 0 and lengths[1] % 2 == 0:
                other[dim], other[1] = place[dim], place[1] ^ 1
            else:
                other[dim] = other[dim] % size if size % 2 == 0 else place[dim]
        flat = [0, 0]
        for length, mine, theirs in zip(lengths, place, other):
            flat = [flat[0] * length + mine, flat[1] * length + theirs]
        pairs.append(tuple(flat))
    return pairs


def exchange(edges, sizes):
    axes = tuple(axis for axis, _ in sizes)
    return [lax.ppermute(edge, axes, swaps(sizes, *place)) for edge, place in zip(edges, exchanges(sizes))]


def shards(sizes, wavefield, deriv_ops, density, lame_first, shear_modulus, high_order, element_cell, face_orient):
    count, fields, nodes = wavefield.shape[-3:]
    rows = fields * count
    wave = wavefield[0, 0, 0].swapaxes(0, 1).reshape(rows, nodes)
    half, blocks = count // 2, fields - 1
    row = lambda value: value.reshape(1, count)
    codes = face_orient.reshape(6, 1, count)
    vmem = pl.BlockSpec(memory_space=pltpu.VMEM)
    hbm = pl.BlockSpec(memory_space=pltpu.HBM)
    shape = jax.ShapeDtypeStruct
    field_shape = shape((nodes // 128, rows, 128), F32)
    edge_rows = {0: (fields + 1) // 2 * 8, 1: -(-(rows // 8) // 8) * 8, 2: rows // 4}
    predicted = [
        shape((rows, nodes), BF16),
        shape((rows, nodes), BF16),
        shape((rows, 128), F32),
        shape((rows, 128), F32),
        shape((rows, 128), F32),
    ]
    for place in exchanges(sizes):
        padded = edge_rows[place[0]] if place == ORDER[0] else max(edge_rows.values())
        predicted.append(shape((padded, 128), F32))
    hot_rows = half * fields
    predict_scratch = [pltpu.VMEM((rows, nodes), BF16)] * 4 + [pltpu.VMEM(field_shape.shape, F32)]
    predict_scratch += [pltpu.VMEM((hot_rows, nodes), BF16)] * 4 + [pltpu.VMEM((hot_rows, nodes), F32)]
    face_scratch = [pltpu.VMEM((rows, 256), BF16), pltpu.VMEM((rows, 256), BF16)]
    halo_scratch = [pltpu.VMEM((rows, 128), F32)] + face_scratch

    def call(kernel, operands, in_specs, out_shape, scratch, products, name, out_spec=vmem, limit=VMEM_LIMIT):
        single = not isinstance(out_shape, list)
        return pl.pallas_call(
            kernel,
            out_shape=out_shape,
            in_specs=in_specs,
            out_specs=out_spec if single else [out_spec] * len(out_shape),
            scratch_shapes=scratch,
            compiler_params=pltpu.CompilerParams(vmem_limit_bytes=limit),
            cost_estimate=pl.CostEstimate(
                flops=products * 6 * rows * nodes * nodes * 4, bytes_accessed=4 * rows * nodes * 4, transcendentals=0
            ),
            name=name,
        )(*operands)

    w_high, w_low, face_table, lift_table = call(
        table_kernel,
        [deriv_ops],
        [hbm],
        [
            shape(deriv_ops.shape, BF16),
            shape(deriv_ops.shape, BF16),
            shape((nodes, 256), BF16),
            shape((256, nodes), BF16),
        ],
        [pltpu.VMEM(deriv_ops.shape, F32), pltpu.SemaphoreType.DMA((4 * deriv_ops.shape[0],))],
        2,
        "split_operators",
        limit=TABLE_LIMIT,
    )
    q, par, index, hot_par, place_back, pack, unpack, *ahead = call(
        functools.partial(first_kernel, count, fields, sizes),
        [wave, row(density), row(lame_first), row(shear_modulus), row(element_cell), row(high_order), codes]
        + [w_high, w_low, face_table],
        [vmem] * 10,
        [
            field_shape,
            shape((4 * count, 128), F32),
            shape((3 * count, 128), jnp.int32),
            shape((4 * half, 128), F32),
            shape((blocks * count, blocks * count), BF16),
            shape((blocks * half, blocks * count), BF16),
            shape((blocks * count, blocks * half), BF16),
        ]
        + predicted,
        [pltpu.VMEM((blocks * count, blocks * count), BF16)] + predict_scratch,
        4,
        "first_predictor",
    )
    for step in range(STEPS):
        traces, edges = ahead[:5], ahead[5:]
        got = exchange(edges, sizes)
        base = call(
            functools.partial(inner_kernel, count, fields),
            [q, *traces, par, index, w_high, w_low, lift_table],
            [vmem] * 11,
            field_shape,
            face_scratch,
            1,
            "inner_update",
        )
        if step < STEPS - 1:
            q, *ahead = call(
                functools.partial(middle_kernel, count, fields, sizes),
                [*got, base, par, index, hot_par, pack, unpack, w_high, w_low, face_table, lift_table],
                [vmem] * (len(got) + 10),
                [field_shape] + predicted,
                halo_scratch + predict_scratch,
                4,
                "outer_update_predictor",
            )
        else:
            out = call(
                functools.partial(last_kernel, count, fields, sizes),
                [*got, base, par, index, place_back, lift_table],
                [vmem] * (len(got) + 5),
                shape((rows, nodes), F32),
                [pltpu.VMEM(field_shape.shape, F32)]
                + [pltpu.VMEM((rows, nodes), BF16)] * 2
                + [pltpu.VMEM((rows, nodes), F32)]
                + halo_scratch
                + [pltpu.SemaphoreType.DMA((nodes // 256,))],
                1,
                "outer_update",
                hbm,
            )
    return out.reshape(fields, count, nodes).swapaxes(0, 1)[None, None, None]


def solution(mesh):
    sizes = tuple((axis, mesh.shape[axis]) for axis in mesh.axis_names)
    lead = ("gx", "gy", "ha")
    placed = (
        P(*lead, None, None, None),
        P(),
        P(*lead, None),
        P(*lead, None),
        P(*lead, None),
        P(*lead, None),
        P(*lead, None),
        P(*lead, None, None),
    )
    return jax.shard_map(
        functools.partial(shards, sizes),
        mesh=mesh,
        in_specs=placed,
        out_specs=P(*lead, None, None, None),
        check_vma=False,
    )
```

```python
import functools
import itertools
import math

import jax
import jax.numpy as jnp
from jax import lax
from jax.experimental import pallas as pl
from jax.experimental.pallas import tpu as pltpu
from jax.sharding import PartitionSpec as P

STEPS = 2
DT = 0.8
LIFT = 2.0
ORDER = ((1, 1), (2, 0), (2, 1), (0, 0), (0, 1), (1, 0))
PICKED = ((0, 1, 2, 3, 6, 8), (0, 1, 2, 6, 4, 7), (0, 1, 2, 8, 7, 5))
F32 = jnp.float32
BF16 = jnp.bfloat16
VMEM_LIMIT = 24 << 20
TABLE_LIMIT = 50 << 20


def wide(column, count):
    return jnp.concatenate([column] * count, axis=1)


def get(field, rows, cols):
    return jnp.concatenate([field[t, rows, :] for t in range(cols.start // 128, cols.stop // 128)], axis=1)


def put(field, rows, cols, value):
    for t in range(cols.start // 128, cols.stop // 128):
        field[t, rows, :] = value[:, t * 128 - cols.start : (t + 1) * 128 - cols.start]


def add(field, rows, cols, value):
    put(field, rows, cols, get(field, rows, cols) + value)


def split(value):
    high = value.astype(BF16)
    return high, (value - high.astype(F32)).astype(BF16)


def dot(left, right):
    return jnp.dot(left, right, preferred_element_type=F32)


def moved(table, source, cols, rows_in, rows_out):
    body, whole = table.shape[1], source.shape[0]
    first = dot(table[...], source[0:body, cols])
    rest = dot(table[0:rows_out, 0:rows_in], source[body:whole, cols])
    return jnp.concatenate([first, rest], axis=0)


def lanes_of(rows):
    return lax.broadcasted_iota(jnp.int32, (rows, 128), 1)


def combine(deriv, rows, inv_rho, lame, shear, shear2, cols, emit):
    part = lambda dim, row: deriv[dim][row * rows : (row + 1) * rows]
    div = lame * (part(0, 0) + part(1, 1) + part(2, 2))
    emit(0, cols, inv_rho * (part(0, 3) + part(1, 3) + part(2, 3)))
    emit(1, cols, inv_rho * (part(0, 4) + part(1, 4) + part(2, 4)))
    emit(2, cols, inv_rho * (part(0, 5) + part(1, 5) + part(2, 5)))
    emit(3, cols, div + shear2 * part(0, 0))
    emit(4, cols, div + shear2 * part(1, 1))
    emit(5, cols, div + shear2 * part(2, 2))
    emit(6, cols, shear * (part(0, 1) + part(1, 0)))
    emit(7, cols, shear * (part(1, 2) + part(2, 1)))
    emit(8, cols, shear * (part(0, 2) + part(2, 0)))


def rate(high, low, w_high, w_low, par, stride, rows, emit, block=256):
    nodes = w_high.shape[-1]
    inv_rho = wide(par[0:rows], block // 128)
    lame = wide(par[stride : stride + rows], block // 128)
    shear = wide(par[2 * stride : 2 * stride + rows], block // 128)
    shear2 = 2.0 * shear
    for start in range(0, nodes, block):
        cols = slice(start, start + block)
        deriv = [None] * 3
        for k in range(0, nodes, 256):
            depth = slice(k, k + 256)
            for dim in range(3):
                top = jnp.concatenate([high[f * stride : f * stride + rows, depth] for f in PICKED[dim]], axis=0)
                rest = jnp.concatenate([low[f * stride : f * stride + rows, depth] for f in PICKED[dim]], axis=0)
                both = dot(jnp.concatenate([top, rest], axis=0), w_high[dim, depth, cols])
                part = both[: 6 * rows] + both[6 * rows :] + dot(top, w_low[dim, depth, cols])
                deriv[dim] = part if deriv[dim] is None else deriv[dim] + part
        combine(deriv, rows, inv_rho, lame, shear, shear2, cols, emit)


def correction(jump, par, count, dim, rows):
    take = lambda k: par[k * count : k * count + rows] if not isinstance(rows, slice) else par[
        k * count + rows.start : k * count + rows.stop
    ]
    inv_rho, lame, shear, half_speed = take(0), take(1), take(2), take(3)
    size = jump[0].shape[0]
    sign = jnp.where(lanes_of(size) < 64, -0.5, 0.5)
    inv_rho, lame, shear = sign * inv_rho, sign * lame, sign * shear
    stiff = lame + 2.0 * shear
    if dim == 0:
        flux = [inv_rho * jump[3], inv_rho * jump[6], inv_rho * jump[8]]
        flux += [stiff * jump[0], lame * jump[0], lame * jump[0]]
        flux += [shear * jump[1], None, shear * jump[2]]
    elif dim == 1:
        flux = [inv_rho * jump[6], inv_rho * jump[4], inv_rho * jump[7]]
        flux += [lame * jump[1], stiff * jump[1], lame * jump[1]]
        flux += [shear * jump[0], shear * jump[2], None]
    else:
        flux = [inv_rho * jump[8], inv_rho * jump[7], inv_rho * jump[5]]
        flux += [lame * jump[2], lame * jump[2], stiff * jump[2]]
        flux += [None, shear * jump[1], shear * jump[0]]
    return [
        half_speed * jump[f] if flux[f] is None else half_speed * jump[f] + flux[f] for f in range(len(jump))
    ]


def orient(value, index):
    return jnp.take_along_axis(value, index, axis=1, mode="promise_in_bounds")


def lift_edges(target, face, f, rows, count):
    lanes = lanes_of(face.shape[0])
    scaled = DT * LIFT * face
    top = slice(f * count + rows.start, f * count + rows.stop)
    last = target.shape[0] - 1
    target[0, top] = target[0, top] + jnp.where(lanes < 64, scaled, 0.0)
    target[last, top] = target[last, top] + jnp.where(lanes < 64, 0.0, scaled)


def lift_inner(target, source, face_high, face_low, lift_table):
    rows, nodes = target.shape[1], lift_table.shape[1]
    for start in range(0, nodes, 256):
        cols = slice(start, start + 256)
        lifted = dot(face_high[...], lift_table[:, cols]) + dot(face_low[...], lift_table[:, cols])
        put(target, slice(0, rows), cols, get(source, slice(0, rows), cols) + DT * LIFT * lifted)


def exchanges(sizes):
    return [(dim, parity) for dim, parity in ORDER if parity == 0 or sizes[dim][1] > 2]


def fetch(copies):
    started = [pltpu.make_async_copy(*copy) for copy in copies]
    for copy in started:
        copy.start()
    return started


def send(low, high, up, targets):
    minus = lanes_of(low.shape[0]) < 64
    plus_face = jnp.where(minus, pltpu.roll(low, 64, 1), high)
    minus_face = jnp.where(minus, low, pltpu.roll(high, 64, 1))
    rows = low.shape[0]
    for parity, target in enumerate(targets):
        if target is None:
            continue
        target[0:rows] = jnp.where(up, plus_face, minus_face) if parity == 0 else jnp.where(up, minus_face, plus_face)
        if target.shape[0] > rows:
            target[rows:] = jnp.zeros((target.shape[0] - rows, 128), F32)


def received(pair, rows, axis, size):
    here = lax.axis_index(axis)
    odd = here % 2 == 1
    first = pair[0][0:rows]
    second = first if pair[1] is None else pair[1][0:rows]
    minus = lanes_of(first.shape[0]) < 64
    lower = jnp.where(odd, first, second)
    upper = jnp.where(odd, second, first)
    plus_lane = jnp.logical_and(here > 0, jnp.logical_not(minus))
    minus_lane = jnp.logical_and(here < size - 1, minus)
    return (
        (jnp.where(plus_lane, pltpu.roll(lower, 64, 1), 0.0), jnp.where(plus_lane, lower, 0.0)),
        (jnp.where(minus_lane, upper, 0.0), jnp.where(minus_lane, pltpu.roll(upper, 64, 1), 0.0)),
    )


def predict(count, fields, sizes, q, par, hot_par, pack, unpack, w_high, w_low, face_table, outs, scratch):
    int_high, int_low, trace_x, trace_y, trace_z, *edges = outs
    h0, l0, h1, l1, total, p0, p1, p2, p3, series = scratch
    nodes = h0.shape[1]
    half = count // 2

    def first(f, cols, value):
        rows = slice(f * count, (f + 1) * count)
        put(total, rows, cols, get(q, rows, cols) + DT / 2.0 * value)
        h1[rows, cols], l1[rows, cols] = split(value)

    rate(h0, l0, w_high, w_low, par, count, count, first)

    def then(f, cols, value):
        rows = slice(f * count, (f + 1) * count)
        add(total, rows, cols, DT**2 / 6.0 * value)
        h0[rows, cols], l0[rows, cols] = split(value)

    rate(h1, l1, w_high, w_low, par, count, count, then)

    for start in range(0, nodes, 256):
        cols = slice(start, start + 256)
        p0[:, cols] = moved(pack, h0, cols, count, half).astype(BF16)
        p1[:, cols] = moved(pack, l0, cols, count, half).astype(BF16)
    buffers = [(p0, p1), (p2, p3)]
    for order in (3, 4, 5):
        weight = DT**order / math.factorial(order + 1)
        source, target = buffers[(order - 3) % 2], buffers[(order - 2) % 2]

        def more(f, cols, value, order=order, weight=weight, target=target):
            rows = slice(f * half, (f + 1) * half)
            part = weight * value
            if order > 3:
                part = part + series[rows, cols]
            if order < 5:
                series[rows, cols] = part
                part = value
            target[0][rows, cols], target[1][rows, cols] = split(part)

        rate(source[0], source[1], w_high, w_low, hot_par, half, half, more)
    for start in range(0, nodes, 256):
        cols = slice(start, start + 256)
        extra = moved(unpack, p2, cols, half, count) + moved(unpack, p3, cols, half, count)
        add(total, slice(0, fields * count), cols, extra)
    for f in range(fields):
        rows = slice(f * count, (f + 1) * count)
        int_high[rows], int_low[rows] = split(get(total, rows, slice(0, nodes)))
        trace_x[rows] = jnp.where(lanes_of(count) < 64, total[0, rows], total[total.shape[0] - 1, rows])
    faces = dot(int_high[...], face_table[...]) + dot(int_low[...], face_table[...])
    whole = fields * count
    trace_y[0:whole] = faces[:, 0:128]
    if trace_y.shape[0] > whole:
        trace_y[whole:] = jnp.zeros((trace_y.shape[0] - whole, 128), F32)
    trace_z[...] = faces[:, 128:256]
    targets = [[None, None] for _ in sizes]
    for (dim, parity), edge in zip(exchanges(sizes), edges):
        targets[dim][parity] = edge
    ups = [lax.axis_index(axis) % 2 == 0 for axis, _ in sizes]
    ends = []
    for f in range(fields):
        low, high = trace_x[f * count : f * count + 8], trace_x[(f + 1) * count - 8 : (f + 1) * count]
        ends.append(jnp.where(lanes_of(8) < 64, low, high))
    middle = (fields + 1) // 2
    ends.append(ends[-1])
    send(jnp.concatenate(ends[:middle]), jnp.concatenate(ends[middle : 2 * middle]), ups[0], targets[0])
    tiles = trace_y.shape[0] // 8
    minus = lanes_of(tiles) < 64
    ends = [
        jnp.where(minus, trace_y[pl.ds(m, tiles, stride=8), :], trace_y[pl.ds(6 + m, tiles, stride=8), :])
        for m in range(2)
    ]
    send(ends[0], ends[1], ups[1], targets[1])
    pairs = fields * count // 4
    minus = lanes_of(pairs) < 64
    ends = []
    for start in (0, 2 * pairs):
        value = jnp.where(
            minus, trace_z[pl.ds(start, pairs, stride=2), :], trace_z[pl.ds(start + 1, pairs, stride=2), :]
        )
        ends.append(value)
    send(ends[0], ends[1], ups[2], targets[2])


def inner(count, fields, q, int_high, int_low, trace_x, trace_y, trace_z, par, index, w_high, w_low, lift_table,
          base, face_high, face_low):
    def volume(f, cols, value):
        rows = slice(f * count, (f + 1) * count)
        put(base, rows, cols, get(q, rows, cols) + DT * value)

    rate(int_high, int_low, w_high, w_low, par, count, count, volume)
    lanes = lanes_of(count)
    sub = lax.broadcasted_iota(jnp.int32, (count, 128), 0)
    minus = lanes < 64
    zero = jnp.zeros((8, 128), F32)
    for dim, trace in enumerate((trace_x, trace_y, trace_z)):
        jump = []
        for f in range(fields):
            own = trace[f * count : (f + 1) * count]
            if dim == 0:
                above = jnp.concatenate([own[8:], zero], axis=0)
                below = jnp.concatenate([zero, own[:-8]], axis=0)
            elif dim == 1:
                above = jnp.where(sub % 8 < 6, pltpu.roll(own, count - 2, 0), 0.0)
                below = jnp.where(sub % 8 < 2, 0.0, pltpu.roll(own, 2, 0))
            else:
                above = jnp.where(sub % 2 < 1, pltpu.roll(own, count - 1, 0), 0.0)
                below = jnp.where(sub % 2 < 1, 0.0, pltpu.roll(own, 1, 0))
            beside = jnp.where(minus, above, below)
            jump.append(orient(beside, index[dim * count : (dim + 1) * count]) - own)
        fixed = correction(jump, par, count, dim, count)
        for f in range(fields):
            if dim == 0:
                lift_edges(base, fixed[f], f, slice(0, count), count)
            else:
                cols = slice((dim - 1) * 128, dim * 128)
                rows = slice(f * count, (f + 1) * count)
                face_high[rows, cols], face_low[rows, cols] = split(fixed[f])
    lift_inner(base, base, face_high, face_low, lift_table)


def outer(count, fields, sizes, got, base, par, index, lift_table, out, halo, face_high, face_low):
    tiles = halo.shape[0] // 8
    pairs = fields * count // 4
    for dim in (1, 2):
        lower, upper = received(got[dim], pairs if dim == 2 else tiles, *sizes[dim])
        if dim == 1:
            halo[...] = jnp.zeros_like(halo)
            for m in range(2):
                halo[pl.ds(m, tiles, stride=8), :] = lower[m]
                halo[pl.ds(6 + m, tiles, stride=8), :] = upper[m]
        else:
            for part in range(2):
                halo[pl.ds(2 * part * pairs, pairs, stride=2), :] = lower[part]
                halo[pl.ds(2 * part * pairs + 1, pairs, stride=2), :] = upper[part]
        jump = [
            orient(halo[f * count : (f + 1) * count], index[dim * count : (dim + 1) * count]) for f in range(fields)
        ]
        fixed = correction(jump, par, count, dim, count)
        for f in range(fields):
            cols = slice((dim - 1) * 128, dim * 128)
            rows = slice(f * count, (f + 1) * count)
            face_high[rows, cols], face_low[rows, cols] = split(fixed[f])
    lift_inner(out, base, face_high, face_low, lift_table)
    middle = (fields + 1) // 2
    lower, upper = received(got[0], middle * 8, *sizes[0])
    for end, (low, high) in enumerate((lower, upper)):
        rows = slice(0, 8) if end == 0 else slice(count - 8, count)
        jump = []
        for f in range(fields):
            part, at = (low, f) if f < middle else (high, f - middle)
            jump.append(orient(part[at * 8 : at * 8 + 8], index[rows]))
        fixed = correction(jump, par, count, 0, rows)
        for f in range(fields):
            lift_edges(out, fixed[f], f, rows, count)


def table_kernel(ops_any, w_high, w_low, face_table, lift_table, ops, sems):
    dims, nodes = ops.shape[:2]
    step = nodes // 4
    parts = [(dim, slice(start, start + step)) for dim in range(dims) for start in range(0, nodes, step)]
    waits = fetch([(ops_any.at[dim, rows], ops.at[dim, rows], sems.at[k]) for k, (dim, rows) in enumerate(parts)])

    def on_face(node, column):
        i, j, k = node // 64, node // 8 % 8, node % 8
        plus = column // 64 % 2 * 7
        p, r = column % 64 // 8, column % 8
        along_y = (column < 128) & (j == plus) & (i == p) & (k == r)
        along_z = (column >= 128) & (k == plus) & (i == p) & (j == r)
        return jnp.where(along_y | along_z, 1.0, 0.0).astype(BF16)

    table = face_table.shape
    face_table[...] = on_face(lax.broadcasted_iota(jnp.int32, table, 0), lax.broadcasted_iota(jnp.int32, table, 1))
    table = table[::-1]
    lift_table[...] = on_face(lax.broadcasted_iota(jnp.int32, table, 1), lax.broadcasted_iota(jnp.int32, table, 0))
    for wait, (dim, rows) in zip(waits, parts):
        wait.wait()
        w_high[dim, rows, :], w_low[dim, rows, :] = split(ops[dim, rows, :])


def first_kernel(count, fields, sizes, wave, density, lame, shear, cell, flag, orient_code, w_high, w_low, face_table,
                 q, par, index, hot_par, place_back, pack, unpack, *rest):
    outs, place, scratch = rest[:-11], rest[-11], rest[-10:]
    h0, l0, h1, l1 = scratch[:4]
    half, blocks = count // 2, fields - 1
    iota = lambda shape, axis: lax.broadcasted_iota(jnp.int32, shape, axis)
    ones = lambda mask: jnp.where(mask, 1.0, 0.0).astype(BF16)
    cells = cell[...]
    square = (count, count)
    tiled = dot(
        jnp.broadcast_to(cells.astype(F32).astype(BF16), (8, count)),
        ones(iota((count, blocks * count), 1) % count == iota((count, blocks * count), 0)),
    )[0:1].astype(jnp.int32)
    shape = place.shape
    target = tiled + iota((1, shape[1]), 1) // count * count
    place[...] = ones(iota(shape, 0) == target)
    for f in range(fields):
        rows = slice(f * count, (f + 1) * count)
        h1[rows], l1[rows] = split(wave[rows])
    for start in range(0, h0.shape[1], 256):
        cols = slice(start, start + 256)
        high = moved(place, h1, cols, count, count)
        low = moved(place, l1, cols, count, count)
        h0[:, cols], l0[:, cols] = high.astype(BF16), low.astype(BF16)
        put(q, slice(0, fields * count), cols, high + low)

    fills = cells == iota(square, 0)
    gather = lambda mask, row: jnp.sum(jnp.where(mask, row, 0.0), axis=1, keepdims=True)
    in_cell = lambda row: jnp.broadcast_to(gather(fills, row), (count, 128))
    inv_row = 1.0 / density[...]
    inv_rho = in_cell(inv_row)
    lame_col = in_cell(lame[...])
    shear_col = in_cell(shear[...])
    par[0:count] = inv_rho
    par[count : 2 * count] = lame_col
    par[2 * count : 3 * count] = shear_col
    par[3 * count : 4 * count] = 0.5 * jnp.sqrt((lame_col + 2.0 * shear_col) * inv_rho)

    flags = flag[...].astype(F32)
    before = ones(iota(square, 0) < iota(square, 1))
    rank = dot(jnp.broadcast_to(flags.astype(BF16), (8, count)), before)[0:1]
    slots = (rank.astype(jnp.int32) == iota((half, count), 0)) & (flags > 0.0)
    in_slot = lambda row: jnp.broadcast_to(gather(slots, row), (half, 128))
    hot_par[0:half] = in_slot(inv_row)
    hot_par[half : 2 * half] = in_slot(lame[...])
    hot_par[2 * half : 3 * half] = in_slot(shear[...])
    hot_par[3 * half : 4 * half] = in_slot(flags)
    twice = lambda column, times: jnp.concatenate([column] * times, axis=0).astype(jnp.int32)
    shape = pack.shape
    target = twice(in_slot(cells.astype(F32)), blocks) + iota((shape[0], 128), 0) // half * count
    used = twice(in_slot(flags), blocks) > 0
    target = jnp.where(used, target, -1)
    pack[...] = ones(iota(shape, 1) == wide(target, shape[1] // 128))
    shape = unpack.shape
    target = twice(in_cell(rank), blocks) + iota((shape[0], 128), 0) // count * half
    target = jnp.where(twice(in_cell(flags), blocks) > 0, target, -1)
    unpack[...] = ones(iota(shape, 1) == wide(target, shape[1] // 128))
    own = gather(iota(square, 0) == iota(square, 1), cells.astype(F32))
    shape = place_back.shape
    target = twice(jnp.broadcast_to(own, (count, 128)), blocks) + iota((shape[0], 128), 0) // count * count
    place_back[...] = ones(iota(shape, 1) == wide(target, shape[1] // 128))

    lanes = lanes_of(count)
    p_lane, r_lane = lanes % 64 // 8, lanes % 8
    for dim in range(3):
        code = jnp.where(
            lanes < 64,
            in_cell(orient_code[2 * dim].astype(F32)),
            in_cell(orient_code[2 * dim + 1].astype(F32)),
        ).astype(jnp.int32)
        p_from = jnp.where(code % 2 == 1, 7 - p_lane, p_lane)
        r_from = jnp.where(code // 2 % 2 == 1, 7 - r_lane, r_lane)
        source = jnp.where(code >= 4, r_from * 8 + p_from, p_from * 8 + r_from)
        index[dim * count : (dim + 1) * count] = source + jnp.where(lanes < 64, 64, 0)
    predict(count, fields, sizes, q, par, hot_par, pack, unpack, w_high, w_low, face_table, outs, scratch)


def inner_kernel(count, fields, *refs):
    inner(count, fields, *refs)


def unpack_got(sizes, refs):
    got = [[None, None] for _ in sizes]
    places = exchanges(sizes)
    for (dim, parity), ref in zip(places, refs):
        got[dim][parity] = ref
    return got, refs[len(places) :]


def middle_kernel(count, fields, sizes, *refs):
    got, refs = unpack_got(sizes, refs)
    base, par, index, hot_par, pack, unpack, w_high, w_low, face_table, lift_table, q = refs[:11]
    outs, (halo, face_high, face_low), scratch = refs[11:-13], refs[-13:-10], refs[-10:]
    outer(count, fields, sizes, got, base, par, index, lift_table, q, halo, face_high, face_low)
    h0, l0 = scratch[:2]
    for f in range(fields):
        rows = slice(f * count, (f + 1) * count)
        h0[rows], l0[rows] = split(get(q, rows, slice(0, h0.shape[1])))
    predict(count, fields, sizes, q, par, hot_par, pack, unpack, w_high, w_low, face_table, outs, scratch)


def last_kernel(count, fields, sizes, *refs):
    got, refs = unpack_got(sizes, refs)
    base, par, index, place_back, lift_table, out, q, high, low, staged, halo, face_high, face_low, sems = refs
    outer(count, fields, sizes, got, base, par, index, lift_table, q, halo, face_high, face_low)
    done = []
    for k, start in enumerate(range(0, staged.shape[1], 256)):
        cols = slice(start, start + 256)
        for f in range(fields):
            rows = slice(f * count, (f + 1) * count)
            high[rows, cols], low[rows, cols] = split(get(q, rows, cols))
        staged[:, cols] = moved(place_back, high, cols, count, count) + moved(place_back, low, cols, count, count)
        done += fetch([(staged.at[:, cols], out.at[:, cols], sems.at[k])])
    for wait in done:
        wait.wait()


def swaps(sizes, dim, parity):
    lengths = [size for _, size in sizes]
    size, pairs = lengths[dim], []
    for place in itertools.product(*[range(length) for length in lengths]):
        other = list(place)
        other[dim] += 1 if place[dim] % 2 == parity else -1
        if not 0 <= other[dim] < size:
            if dim == 0 and lengths[1] % 2 == 0:
                other[dim], other[1] = place[dim], place[1] ^ 1
            else:
                other[dim] = other[dim] % size if size % 2 == 0 else place[dim]
        flat = [0, 0]
        for length, mine, theirs in zip(lengths, place, other):
            flat = [flat[0] * length + mine, flat[1] * length + theirs]
        pairs.append(tuple(flat))
    return pairs


def exchange(edges, sizes):
    axes = tuple(axis for axis, _ in sizes)
    return [lax.ppermute(edge, axes, swaps(sizes, *place)) for edge, place in zip(edges, exchanges(sizes))]


def shards(sizes, wavefield, deriv_ops, density, lame_first, shear_modulus, high_order, element_cell, face_orient):
    count, fields, nodes = wavefield.shape[-3:]
    rows = fields * count
    wave = wavefield[0, 0, 0].swapaxes(0, 1).reshape(rows, nodes)
    half, blocks = count // 2, fields - 1
    row = lambda value: value.reshape(1, count)
    codes = face_orient.reshape(6, 1, count)
    vmem = pl.BlockSpec(memory_space=pltpu.VMEM)
    hbm = pl.BlockSpec(memory_space=pltpu.HBM)
    shape = jax.ShapeDtypeStruct
    field_shape = shape((nodes // 128, rows, 128), F32)
    edge_rows = {0: (fields + 1) // 2 * 8, 1: -(-(rows // 8) // 8) * 8, 2: rows // 4}
    predicted = [
        shape((rows, nodes), BF16),
        shape((rows, nodes), BF16),
        shape((rows, 128), F32),
        shape((edge_rows[1] * 8, 128), F32),
        shape((rows, 128), F32),
    ]
    for place in exchanges(sizes):
        padded = edge_rows[place[0]] if place == ORDER[0] else max(edge_rows.values())
        predicted.append(shape((padded, 128), F32))
    hot_rows = half * fields
    predict_scratch = [pltpu.VMEM((rows, nodes), BF16)] * 4 + [pltpu.VMEM(field_shape.shape, F32)]
    predict_scratch += [pltpu.VMEM((hot_rows, nodes), BF16)] * 4 + [pltpu.VMEM((hot_rows, nodes), F32)]
    face_scratch = [pltpu.VMEM((rows, 256), BF16), pltpu.VMEM((rows, 256), BF16)]
    halo_scratch = [pltpu.VMEM((edge_rows[1] * 8, 128), F32)] + face_scratch

    def call(kernel, operands, in_specs, out_shape, scratch, products, name, out_spec=vmem, limit=VMEM_LIMIT):
        single = not isinstance(out_shape, list)
        return pl.pallas_call(
            kernel,
            out_shape=out_shape,
            in_specs=in_specs,
            out_specs=out_spec if single else [out_spec] * len(out_shape),
            scratch_shapes=scratch,
            compiler_params=pltpu.CompilerParams(vmem_limit_bytes=limit),
            cost_estimate=pl.CostEstimate(
                flops=products * 6 * rows * nodes * nodes * 4, bytes_accessed=4 * rows * nodes * 4, transcendentals=0
            ),
            name=name,
        )(*operands)

    w_high, w_low, face_table, lift_table = call(
        table_kernel,
        [deriv_ops],
        [hbm],
        [
            shape(deriv_ops.shape, BF16),
            shape(deriv_ops.shape, BF16),
            shape((nodes, 256), BF16),
            shape((256, nodes), BF16),
        ],
        [pltpu.VMEM(deriv_ops.shape, F32), pltpu.SemaphoreType.DMA((4 * deriv_ops.shape[0],))],
        2,
        "split_operators",
        limit=TABLE_LIMIT,
    )
    q, par, index, hot_par, place_back, pack, unpack, *ahead = call(
        functools.partial(first_kernel, count, fields, sizes),
        [wave, row(density), row(lame_first), row(shear_modulus), row(element_cell), row(high_order), codes]
        + [w_high, w_low, face_table],
        [vmem] * 10,
        [
            field_shape,
            shape((4 * count, 128), F32),
            shape((3 * count, 128), jnp.int32),
            shape((4 * half, 128), F32),
            shape((blocks * count, blocks * count), BF16),
            shape((blocks * half, blocks * count), BF16),
            shape((blocks * count, blocks * half), BF16),
        ]
        + predicted,
        [pltpu.VMEM((blocks * count, blocks * count), BF16)] + predict_scratch,
        4,
        "first_predictor",
    )
    for step in range(STEPS):
        traces, edges = ahead[:5], ahead[5:]
        got = exchange(edges, sizes)
        base = call(
            functools.partial(inner_kernel, count, fields),
            [q, *traces, par, index, w_high, w_low, lift_table],
            [vmem] * 11,
            field_shape,
            face_scratch,
            1,
            "inner_update",
        )
        if step < STEPS - 1:
            q, *ahead = call(
                functools.partial(middle_kernel, count, fields, sizes),
                [*got, base, par, index, hot_par, pack, unpack, w_high, w_low, face_table, lift_table],
                [vmem] * (len(got) + 10),
                [field_shape] + predicted,
                halo_scratch + predict_scratch,
                4,
                "outer_update_predictor",
            )
        else:
            out = call(
                functools.partial(last_kernel, count, fields, sizes),
                [*got, base, par, index, place_back, lift_table],
                [vmem] * (len(got) + 5),
                shape((rows, nodes), F32),
                [pltpu.VMEM(field_shape.shape, F32)]
                + [pltpu.VMEM((rows, nodes), BF16)] * 2
                + [pltpu.VMEM((rows, nodes), F32)]
                + halo_scratch
                + [pltpu.SemaphoreType.DMA((nodes // 256,))],
                1,
                "outer_update",
                hbm,
            )
    return out.reshape(fields, count, nodes).swapaxes(0, 1)[None, None, None]


def solution(mesh):
    sizes = tuple((axis, mesh.shape[axis]) for axis in mesh.axis_names)
    lead = ("gx", "gy", "ha")
    placed = (
        P(*lead, None, None, None),
        P(),
        P(*lead, None),
        P(*lead, None),
        P(*lead, None),
        P(*lead, None),
        P(*lead, None),
        P(*lead, None, None),
    )
    return jax.shard_map(
        functools.partial(shards, sizes),
        mesh=mesh,
        in_specs=placed,
        out_specs=P(*lead, None, None, None),
        check_vma=False,
    )
```

```python
import functools
import itertools
import math

import jax
import jax.numpy as jnp
from jax import lax
from jax.experimental import pallas as pl
from jax.experimental.pallas import tpu as pltpu
from jax.sharding import PartitionSpec as P

STEPS = 2
DT = 0.8
LIFT = 2.0
ORDER = ((1, 1), (2, 0), (2, 1), (0, 0), (0, 1), (1, 0))
PICKED = ((0, 1, 2, 3, 6, 8), (0, 1, 2, 6, 4, 7), (0, 1, 2, 8, 7, 5))
F32 = jnp.float32
BF16 = jnp.bfloat16
VMEM_LIMIT = 24 << 20
TABLE_LIMIT = 50 << 20


def wide(column, count):
    return jnp.concatenate([column] * count, axis=1)


def get(field, rows, cols):
    return jnp.concatenate([field[t, rows, :] for t in range(cols.start // 128, cols.stop // 128)], axis=1)


def put(field, rows, cols, value):
    for t in range(cols.start // 128, cols.stop // 128):
        field[t, rows, :] = value[:, t * 128 - cols.start : (t + 1) * 128 - cols.start]


def add(field, rows, cols, value):
    put(field, rows, cols, get(field, rows, cols) + value)


def split(value):
    high = value.astype(BF16)
    return high, (value - high.astype(F32)).astype(BF16)


def dot(left, right):
    return jnp.dot(left, right, preferred_element_type=F32)


def moved(table, source, cols, rows_in, rows_out):
    body, whole = table.shape[1], source.shape[0]
    first = dot(table[...], source[0:body, cols])
    rest = dot(table[0:rows_out, 0:rows_in], source[body:whole, cols])
    return jnp.concatenate([first, rest], axis=0)


def lanes_of(rows):
    return lax.broadcasted_iota(jnp.int32, (rows, 128), 1)


def combine(deriv, rows, inv_rho, lame, shear, shear2, cols, emit):
    part = lambda dim, row: deriv[dim][row * rows : (row + 1) * rows]
    div = lame * (part(0, 0) + part(1, 1) + part(2, 2))
    emit(0, cols, inv_rho * (part(0, 3) + part(1, 3) + part(2, 3)))
    emit(1, cols, inv_rho * (part(0, 4) + part(1, 4) + part(2, 4)))
    emit(2, cols, inv_rho * (part(0, 5) + part(1, 5) + part(2, 5)))
    emit(3, cols, div + shear2 * part(0, 0))
    emit(4, cols, div + shear2 * part(1, 1))
    emit(5, cols, div + shear2 * part(2, 2))
    emit(6, cols, shear * (part(0, 1) + part(1, 0)))
    emit(7, cols, shear * (part(1, 2) + part(2, 1)))
    emit(8, cols, shear * (part(0, 2) + part(2, 0)))


def rate(high, low, w_high, w_low, par, stride, rows, emit, block=256):
    nodes = w_high.shape[-1]
    inv_rho = wide(par[0:rows], block // 128)
    lame = wide(par[stride : stride + rows], block // 128)
    shear = wide(par[2 * stride : 2 * stride + rows], block // 128)
    shear2 = 2.0 * shear
    for start in range(0, nodes, block):
        cols = slice(start, start + block)
        deriv = [None] * 3
        for k in range(0, nodes, 256):
            depth = slice(k, k + 256)
            for dim in range(3):
                top = jnp.concatenate([high[f * stride : f * stride + rows, depth] for f in PICKED[dim]], axis=0)
                rest = jnp.concatenate([low[f * stride : f * stride + rows, depth] for f in PICKED[dim]], axis=0)
                both = dot(jnp.concatenate([top, rest], axis=0), w_high[dim, depth, cols])
                part = both[: 6 * rows] + (both[6 * rows :] + dot(top, w_low[dim, depth, cols]))
                deriv[dim] = part if deriv[dim] is None else deriv[dim] + part
        combine(deriv, rows, inv_rho, lame, shear, shear2, cols, emit)


def correction(jump, par, count, dim, rows):
    take = lambda k: par[k * count : k * count + rows] if not isinstance(rows, slice) else par[
        k * count + rows.start : k * count + rows.stop
    ]
    inv_rho, lame, shear, half_speed = take(0), take(1), take(2), take(3)
    size = jump[0].shape[0]
    sign = jnp.where(lanes_of(size) < 64, -0.5, 0.5)
    inv_rho, lame, shear = sign * inv_rho, sign * lame, sign * shear
    stiff = lame + 2.0 * shear
    if dim == 0:
        flux = [inv_rho * jump[3], inv_rho * jump[6], inv_rho * jump[8]]
        flux += [stiff * jump[0], lame * jump[0], lame * jump[0]]
        flux += [shear * jump[1], None, shear * jump[2]]
    elif dim == 1:
        flux = [inv_rho * jump[6], inv_rho * jump[4], inv_rho * jump[7]]
        flux += [lame * jump[1], stiff * jump[1], lame * jump[1]]
        flux += [shear * jump[0], shear * jump[2], None]
    else:
        flux = [inv_rho * jump[8], inv_rho * jump[7], inv_rho * jump[5]]
        flux += [lame * jump[2], lame * jump[2], stiff * jump[2]]
        flux += [None, shear * jump[1], shear * jump[0]]
    return [
        half_speed * jump[f] if flux[f] is None else half_speed * jump[f] + flux[f] for f in range(len(jump))
    ]


def orient(value, index):
    return jnp.take_along_axis(value, index, axis=1, mode="promise_in_bounds")


def lift_edges(target, face, f, rows, count):
    lanes = lanes_of(face.shape[0])
    scaled = DT * LIFT * face
    top = slice(f * count + rows.start, f * count + rows.stop)
    last = target.shape[0] - 1
    target[0, top] = target[0, top] + jnp.where(lanes < 64, scaled, 0.0)
    target[last, top] = target[last, top] + jnp.where(lanes < 64, 0.0, scaled)


def lift_inner(target, source, face_high, face_low, lift_table):
    rows, nodes = target.shape[1], lift_table.shape[1]
    for start in range(0, nodes, 256):
        cols = slice(start, start + 256)
        lifted = dot(face_high[...], lift_table[:, cols]) + dot(face_low[...], lift_table[:, cols])
        put(target, slice(0, rows), cols, get(source, slice(0, rows), cols) + DT * LIFT * lifted)


def exchanges(sizes):
    return [(dim, parity) for dim, parity in ORDER if parity == 0 or sizes[dim][1] > 2]


def fetch(copies):
    started = [pltpu.make_async_copy(*copy) for copy in copies]
    for copy in started:
        copy.start()
    return started


def send(low, high, up, targets):
    minus = lanes_of(low.shape[0]) < 64
    plus_face = jnp.where(minus, pltpu.roll(low, 64, 1), high)
    minus_face = jnp.where(minus, low, pltpu.roll(high, 64, 1))
    rows = low.shape[0]
    for parity, target in enumerate(targets):
        if target is None:
            continue
        target[0:rows] = jnp.where(up, plus_face, minus_face) if parity == 0 else jnp.where(up, minus_face, plus_face)
        if target.shape[0] > rows:
            target[rows:] = jnp.zeros((target.shape[0] - rows, 128), F32)


def received(pair, rows, axis, size):
    here = lax.axis_index(axis)
    odd = here % 2 == 1
    first = pair[0][0:rows]
    second = first if pair[1] is None else pair[1][0:rows]
    minus = lanes_of(first.shape[0]) < 64
    lower = jnp.where(odd, first, second)
    upper = jnp.where(odd, second, first)
    plus_lane = jnp.logical_and(here > 0, jnp.logical_not(minus))
    minus_lane = jnp.logical_and(here < size - 1, minus)
    return (
        (jnp.where(plus_lane, pltpu.roll(lower, 64, 1), 0.0), jnp.where(plus_lane, lower, 0.0)),
        (jnp.where(minus_lane, upper, 0.0), jnp.where(minus_lane, pltpu.roll(upper, 64, 1), 0.0)),
    )


def predict(count, fields, sizes, q, par, hot_par, pack, unpack, w_high, w_low, face_table, outs, scratch):
    int_high, int_low, trace_x, trace_y, trace_z, *edges = outs
    h0, l0, h1, l1, total, p0, p1, p2, p3, series = scratch
    nodes = h0.shape[1]
    half = count // 2

    def first(f, cols, value):
        rows = slice(f * count, (f + 1) * count)
        put(total, rows, cols, get(q, rows, cols) + DT / 2.0 * value)
        h1[rows, cols], l1[rows, cols] = split(value)

    rate(h0, l0, w_high, w_low, par, count, count, first)

    def then(f, cols, value):
        rows = slice(f * count, (f + 1) * count)
        add(total, rows, cols, DT**2 / 6.0 * value)
        h0[rows, cols], l0[rows, cols] = split(value)

    rate(h1, l1, w_high, w_low, par, count, count, then)

    for start in range(0, nodes, 256):
        cols = slice(start, start + 256)
        p0[:, cols] = moved(pack, h0, cols, count, half).astype(BF16)
        p1[:, cols] = moved(pack, l0, cols, count, half).astype(BF16)
    buffers = [(p0, p1), (p2, p3)]
    for order in (3, 4, 5):
        weight = DT**order / math.factorial(order + 1)
        source, target = buffers[(order - 3) % 2], buffers[(order - 2) % 2]

        def more(f, cols, value, order=order, weight=weight, target=target):
            rows = slice(f * half, (f + 1) * half)
            part = weight * value
            if order > 3:
                part = part + series[rows, cols]
            if order < 5:
                series[rows, cols] = part
                part = value
            target[0][rows, cols], target[1][rows, cols] = split(part)

        rate(source[0], source[1], w_high, w_low, hot_par, half, half, more)
    for start in range(0, nodes, 256):
        cols = slice(start, start + 256)
        extra = moved(unpack, p2, cols, half, count) + moved(unpack, p3, cols, half, count)
        add(total, slice(0, fields * count), cols, extra)
    for f in range(fields):
        rows = slice(f * count, (f + 1) * count)
        int_high[rows], int_low[rows] = split(get(total, rows, slice(0, nodes)))
        trace_x[rows] = jnp.where(lanes_of(count) < 64, total[0, rows], total[total.shape[0] - 1, rows])
    faces = dot(int_high[...], face_table[...]) + dot(int_low[...], face_table[...])
    whole = fields * count
    trace_y[0:whole] = faces[:, 0:128]
    if trace_y.shape[0] > whole:
        trace_y[whole:] = jnp.zeros((trace_y.shape[0] - whole, 128), F32)
    trace_z[...] = faces[:, 128:256]
    targets = [[None, None] for _ in sizes]
    for (dim, parity), edge in zip(exchanges(sizes), edges):
        targets[dim][parity] = edge
    ups = [lax.axis_index(axis) % 2 == 0 for axis, _ in sizes]
    ends = []
    for f in range(fields):
        low, high = trace_x[f * count : f * count + 8], trace_x[(f + 1) * count - 8 : (f + 1) * count]
        ends.append(jnp.where(lanes_of(8) < 64, low, high))
    middle = (fields + 1) // 2
    ends.append(ends[-1])
    send(jnp.concatenate(ends[:middle]), jnp.concatenate(ends[middle : 2 * middle]), ups[0], targets[0])
    tiles = trace_y.shape[0] // 8
    minus = lanes_of(tiles) < 64
    ends = [
        jnp.where(minus, trace_y[pl.ds(m, tiles, stride=8), :], trace_y[pl.ds(6 + m, tiles, stride=8), :])
        for m in range(2)
    ]
    send(ends[0], ends[1], ups[1], targets[1])
    pairs = fields * count // 4
    minus = lanes_of(pairs) < 64
    ends = []
    for start in (0, 2 * pairs):
        value = jnp.where(
            minus, trace_z[pl.ds(start, pairs, stride=2), :], trace_z[pl.ds(start + 1, pairs, stride=2), :]
        )
        ends.append(value)
    send(ends[0], ends[1], ups[2], targets[2])


def inner(count, fields, q, int_high, int_low, trace_x, trace_y, trace_z, par, index, w_high, w_low, lift_table,
          base, face_high, face_low):
    def volume(f, cols, value):
        rows = slice(f * count, (f + 1) * count)
        put(base, rows, cols, get(q, rows, cols) + DT * value)

    rate(int_high, int_low, w_high, w_low, par, count, count, volume)
    lanes = lanes_of(count)
    sub = lax.broadcasted_iota(jnp.int32, (count, 128), 0)
    minus = lanes < 64
    zero = jnp.zeros((8, 128), F32)
    for dim, trace in enumerate((trace_x, trace_y, trace_z)):
        jump = []
        for f in range(fields):
            own = trace[f * count : (f + 1) * count]
            if dim == 0:
                above = jnp.concatenate([own[8:], zero], axis=0)
                below = jnp.concatenate([zero, own[:-8]], axis=0)
            elif dim == 1:
                above = jnp.where(sub % 8 < 6, pltpu.roll(own, count - 2, 0), 0.0)
                below = jnp.where(sub % 8 < 2, 0.0, pltpu.roll(own, 2, 0))
            else:
                above = jnp.where(sub % 2 < 1, pltpu.roll(own, count - 1, 0), 0.0)
                below = jnp.where(sub % 2 < 1, 0.0, pltpu.roll(own, 1, 0))
            beside = jnp.where(minus, above, below)
            jump.append(orient(beside, index[dim * count : (dim + 1) * count]) - own)
        fixed = correction(jump, par, count, dim, count)
        for f in range(fields):
            if dim == 0:
                lift_edges(base, fixed[f], f, slice(0, count), count)
            else:
                cols = slice((dim - 1) * 128, dim * 128)
                rows = slice(f * count, (f + 1) * count)
                face_high[rows, cols], face_low[rows, cols] = split(fixed[f])
    lift_inner(base, base, face_high, face_low, lift_table)


def outer(count, fields, sizes, got, base, par, index, lift_table, out, halo, face_high, face_low):
    tiles = halo.shape[0] // 8
    pairs = fields * count // 4
    for dim in (1, 2):
        lower, upper = received(got[dim], pairs if dim == 2 else tiles, *sizes[dim])
        if dim == 1:
            halo[...] = jnp.zeros_like(halo)
            for m in range(2):
                halo[pl.ds(m, tiles, stride=8), :] = lower[m]
                halo[pl.ds(6 + m, tiles, stride=8), :] = upper[m]
        else:
            for part in range(2):
                halo[pl.ds(2 * part * pairs, pairs, stride=2), :] = lower[part]
                halo[pl.ds(2 * part * pairs + 1, pairs, stride=2), :] = upper[part]
        jump = [
            orient(halo[f * count : (f + 1) * count], index[dim * count : (dim + 1) * count]) for f in range(fields)
        ]
        fixed = correction(jump, par, count, dim, count)
        for f in range(fields):
            cols = slice((dim - 1) * 128, dim * 128)
            rows = slice(f * count, (f + 1) * count)
            face_high[rows, cols], face_low[rows, cols] = split(fixed[f])
    lift_inner(out, base, face_high, face_low, lift_table)
    middle = (fields + 1) // 2
    lower, upper = received(got[0], middle * 8, *sizes[0])
    for end, (low, high) in enumerate((lower, upper)):
        rows = slice(0, 8) if end == 0 else slice(count - 8, count)
        jump = []
        for f in range(fields):
            part, at = (low, f) if f < middle else (high, f - middle)
            jump.append(orient(part[at * 8 : at * 8 + 8], index[rows]))
        fixed = correction(jump, par, count, 0, rows)
        for f in range(fields):
            lift_edges(out, fixed[f], f, rows, count)


def table_kernel(ops_any, w_high, w_low, face_table, lift_table, ops, sems):
    dims, nodes = ops.shape[:2]
    step = nodes // 4
    parts = [(dim, slice(start, start + step)) for dim in range(dims) for start in range(0, nodes, step)]
    waits = fetch([(ops_any.at[dim, rows], ops.at[dim, rows], sems.at[k]) for k, (dim, rows) in enumerate(parts)])

    def on_face(node, column):
        i, j, k = node // 64, node // 8 % 8, node % 8
        plus = column // 64 % 2 * 7
        p, r = column % 64 // 8, column % 8
        along_y = (column < 128) & (j == plus) & (i == p) & (k == r)
        along_z = (column >= 128) & (k == plus) & (i == p) & (j == r)
        return jnp.where(along_y | along_z, 1.0, 0.0).astype(BF16)

    table = face_table.shape
    face_table[...] = on_face(lax.broadcasted_iota(jnp.int32, table, 0), lax.broadcasted_iota(jnp.int32, table, 1))
    table = table[::-1]
    lift_table[...] = on_face(lax.broadcasted_iota(jnp.int32, table, 1), lax.broadcasted_iota(jnp.int32, table, 0))
    for wait, (dim, rows) in zip(waits, parts):
        wait.wait()
        w_high[dim, rows, :], w_low[dim, rows, :] = split(ops[dim, rows, :])


def first_kernel(count, fields, sizes, wave, density, lame, shear, cell, flag, orient_code, w_high, w_low, face_table,
                 q, par, index, hot_par, place_back, pack, unpack, *rest):
    outs, place, scratch = rest[:-11], rest[-11], rest[-10:]
    h0, l0, h1, l1 = scratch[:4]
    half, blocks = count // 2, fields - 1
    iota = lambda shape, axis: lax.broadcasted_iota(jnp.int32, shape, axis)
    ones = lambda mask: jnp.where(mask, 1.0, 0.0).astype(BF16)
    cells = cell[...]
    square = (count, count)
    tiled = dot(
        jnp.broadcast_to(cells.astype(F32).astype(BF16), (8, count)),
        ones(iota((count, blocks * count), 1) % count == iota((count, blocks * count), 0)),
    )[0:1].astype(jnp.int32)
    shape = place.shape
    target = tiled + iota((1, shape[1]), 1) // count * count
    place[...] = ones(iota(shape, 0) == target)
    for f in range(fields):
        rows = slice(f * count, (f + 1) * count)
        h1[rows], l1[rows] = split(wave[rows])
    for start in range(0, h0.shape[1], 256):
        cols = slice(start, start + 256)
        high = moved(place, h1, cols, count, count)
        low = moved(place, l1, cols, count, count)
        h0[:, cols], l0[:, cols] = high.astype(BF16), low.astype(BF16)
        put(q, slice(0, fields * count), cols, high + low)

    fills = cells == iota(square, 0)
    gather = lambda mask, row: jnp.sum(jnp.where(mask, row, 0.0), axis=1, keepdims=True)
    in_cell = lambda row: jnp.broadcast_to(gather(fills, row), (count, 128))
    inv_row = 1.0 / density[...]
    inv_rho = in_cell(inv_row)
    lame_col = in_cell(lame[...])
    shear_col = in_cell(shear[...])
    par[0:count] = inv_rho
    par[count : 2 * count] = lame_col
    par[2 * count : 3 * count] = shear_col
    par[3 * count : 4 * count] = 0.5 * jnp.sqrt((lame_col + 2.0 * shear_col) * inv_rho)

    flags = flag[...].astype(F32)
    before = ones(iota(square, 0) < iota(square, 1))
    rank = dot(jnp.broadcast_to(flags.astype(BF16), (8, count)), before)[0:1]
    slots = (rank.astype(jnp.int32) == iota((half, count), 0)) & (flags > 0.0)
    in_slot = lambda row: jnp.broadcast_to(gather(slots, row), (half, 128))
    hot_par[0:half] = in_slot(inv_row)
    hot_par[half : 2 * half] = in_slot(lame[...])
    hot_par[2 * half : 3 * half] = in_slot(shear[...])
    hot_par[3 * half : 4 * half] = in_slot(flags)
    twice = lambda column, times: jnp.concatenate([column] * times, axis=0).astype(jnp.int32)
    shape = pack.shape
    target = twice(in_slot(cells.astype(F32)), blocks) + iota((shape[0], 128), 0) // half * count
    used = twice(in_slot(flags), blocks) > 0
    target = jnp.where(used, target, -1)
    pack[...] = ones(iota(shape, 1) == wide(target, shape[1] // 128))
    shape = unpack.shape
    target = twice(in_cell(rank), blocks) + iota((shape[0], 128), 0) // count * half
    target = jnp.where(twice(in_cell(flags), blocks) > 0, target, -1)
    unpack[...] = ones(iota(shape, 1) == wide(target, shape[1] // 128))
    own = gather(iota(square, 0) == iota(square, 1), cells.astype(F32))
    shape = place_back.shape
    target = twice(jnp.broadcast_to(own, (count, 128)), blocks) + iota((shape[0], 128), 0) // count * count
    place_back[...] = ones(iota(shape, 1) == wide(target, shape[1] // 128))

    lanes = lanes_of(count)
    p_lane, r_lane = lanes % 64 // 8, lanes % 8
    for dim in range(3):
        code = jnp.where(
            lanes < 64,
            in_cell(orient_code[2 * dim].astype(F32)),
            in_cell(orient_code[2 * dim + 1].astype(F32)),
        ).astype(jnp.int32)
        p_from = jnp.where(code % 2 == 1, 7 - p_lane, p_lane)
        r_from = jnp.where(code // 2 % 2 == 1, 7 - r_lane, r_lane)
        source = jnp.where(code >= 4, r_from * 8 + p_from, p_from * 8 + r_from)
        index[dim * count : (dim + 1) * count] = source + jnp.where(lanes < 64, 64, 0)
    predict(count, fields, sizes, q, par, hot_par, pack, unpack, w_high, w_low, face_table, outs, scratch)


def inner_kernel(count, fields, *refs):
    inner(count, fields, *refs)


def unpack_got(sizes, refs):
    got = [[None, None] for _ in sizes]
    places = exchanges(sizes)
    for (dim, parity), ref in zip(places, refs):
        got[dim][parity] = ref
    return got, refs[len(places) :]


def middle_kernel(count, fields, sizes, *refs):
    got, refs = unpack_got(sizes, refs)
    base, par, index, hot_par, pack, unpack, w_high, w_low, face_table, lift_table, q = refs[:11]
    outs, (halo, face_high, face_low), scratch = refs[11:-13], refs[-13:-10], refs[-10:]
    outer(count, fields, sizes, got, base, par, index, lift_table, q, halo, face_high, face_low)
    h0, l0 = scratch[:2]
    for f in range(fields):
        rows = slice(f * count, (f + 1) * count)
        h0[rows], l0[rows] = split(get(q, rows, slice(0, h0.shape[1])))
    predict(count, fields, sizes, q, par, hot_par, pack, unpack, w_high, w_low, face_table, outs, scratch)


def last_kernel(count, fields, sizes, *refs):
    got, refs = unpack_got(sizes, refs)
    base, par, index, place_back, lift_table, out, q, high, low, staged, halo, face_high, face_low, sems = refs
    outer(count, fields, sizes, got, base, par, index, lift_table, q, halo, face_high, face_low)
    done = []
    for k, start in enumerate(range(0, staged.shape[1], 256)):
        cols = slice(start, start + 256)
        for f in range(fields):
            rows = slice(f * count, (f + 1) * count)
            high[rows, cols], low[rows, cols] = split(get(q, rows, cols))
        staged[:, cols] = moved(place_back, high, cols, count, count) + moved(place_back, low, cols, count, count)
        done += fetch([(staged.at[:, cols], out.at[:, cols], sems.at[k])])
    for wait in done:
        wait.wait()


def swaps(sizes, dim, parity):
    lengths = [size for _, size in sizes]
    size, pairs = lengths[dim], []
    for place in itertools.product(*[range(length) for length in lengths]):
        other = list(place)
        other[dim] += 1 if place[dim] % 2 == parity else -1
        if not 0 <= other[dim] < size:
            if dim == 0 and lengths[1] % 2 == 0:
                other[dim], other[1] = place[dim], place[1] ^ 1
            else:
                other[dim] = other[dim] % size if size % 2 == 0 else place[dim]
        flat = [0, 0]
        for length, mine, theirs in zip(lengths, place, other):
            flat = [flat[0] * length + mine, flat[1] * length + theirs]
        pairs.append(tuple(flat))
    return pairs


def exchange(edges, sizes):
    axes = tuple(axis for axis, _ in sizes)
    return [lax.ppermute(edge, axes, swaps(sizes, *place)) for edge, place in zip(edges, exchanges(sizes))]


def shards(sizes, wavefield, deriv_ops, density, lame_first, shear_modulus, high_order, element_cell, face_orient):
    count, fields, nodes = wavefield.shape[-3:]
    rows = fields * count
    wave = wavefield[0, 0, 0].swapaxes(0, 1).reshape(rows, nodes)
    half, blocks = count // 2, fields - 1
    row = lambda value: value.reshape(1, count)
    codes = face_orient.reshape(6, 1, count)
    vmem = pl.BlockSpec(memory_space=pltpu.VMEM)
    hbm = pl.BlockSpec(memory_space=pltpu.HBM)
    shape = jax.ShapeDtypeStruct
    field_shape = shape((nodes // 128, rows, 128), F32)
    edge_rows = {0: (fields + 1) // 2 * 8, 1: -(-(rows // 8) // 8) * 8, 2: rows // 4}
    predicted = [
        shape((rows, nodes), BF16),
        shape((rows, nodes), BF16),
        shape((rows, 128), F32),
        shape((edge_rows[1] * 8, 128), F32),
        shape((rows, 128), F32),
    ]
    for place in exchanges(sizes):
        padded = edge_rows[place[0]] if place == ORDER[0] else max(edge_rows.values())
        predicted.append(shape((padded, 128), F32))
    hot_rows = half * fields
    predict_scratch = [pltpu.VMEM((rows, nodes), BF16)] * 4 + [pltpu.VMEM(field_shape.shape, F32)]
    predict_scratch += [pltpu.VMEM((hot_rows, nodes), BF16)] * 4 + [pltpu.VMEM((hot_rows, nodes), F32)]
    face_scratch = [pltpu.VMEM((rows, 256), BF16), pltpu.VMEM((rows, 256), BF16)]
    halo_scratch = [pltpu.VMEM((edge_rows[1] * 8, 128), F32)] + face_scratch

    def call(kernel, operands, in_specs, out_shape, scratch, products, name, out_spec=vmem, limit=VMEM_LIMIT):
        single = not isinstance(out_shape, list)
        return pl.pallas_call(
            kernel,
            out_shape=out_shape,
            in_specs=in_specs,
            out_specs=out_spec if single else [out_spec] * len(out_shape),
            scratch_shapes=scratch,
            compiler_params=pltpu.CompilerParams(vmem_limit_bytes=limit),
            cost_estimate=pl.CostEstimate(
                flops=products * 6 * rows * nodes * nodes * 4, bytes_accessed=4 * rows * nodes * 4, transcendentals=0
            ),
            name=name,
        )(*operands)

    w_high, w_low, face_table, lift_table = call(
        table_kernel,
        [deriv_ops],
        [hbm],
        [
            shape(deriv_ops.shape, BF16),
            shape(deriv_ops.shape, BF16),
            shape((nodes, 256), BF16),
            shape((256, nodes), BF16),
        ],
        [pltpu.VMEM(deriv_ops.shape, F32), pltpu.SemaphoreType.DMA((4 * deriv_ops.shape[0],))],
        2,
        "split_operators",
        limit=TABLE_LIMIT,
    )
    q, par, index, hot_par, place_back, pack, unpack, *ahead = call(
        functools.partial(first_kernel, count, fields, sizes),
        [wave, row(density), row(lame_first), row(shear_modulus), row(element_cell), row(high_order), codes]
        + [w_high, w_low, face_table],
        [vmem] * 10,
        [
            field_shape,
            shape((4 * count, 128), F32),
            shape((3 * count, 128), jnp.int32),
            shape((4 * half, 128), F32),
            shape((blocks * count, blocks * count), BF16),
            shape((blocks * half, blocks * count), BF16),
            shape((blocks * count, blocks * half), BF16),
        ]
        + predicted,
        [pltpu.VMEM((blocks * count, blocks * count), BF16)] + predict_scratch,
        4,
        "first_predictor",
    )
    for step in range(STEPS):
        traces, edges = ahead[:5], ahead[5:]
        got = exchange(edges, sizes)
        base = call(
            functools.partial(inner_kernel, count, fields),
            [q, *traces, par, index, w_high, w_low, lift_table],
            [vmem] * 11,
            field_shape,
            face_scratch,
            1,
            "inner_update",
        )
        if step < STEPS - 1:
            q, *ahead = call(
                functools.partial(middle_kernel, count, fields, sizes),
                [*got, base, par, index, hot_par, pack, unpack, w_high, w_low, face_table, lift_table],
                [vmem] * (len(got) + 10),
                [field_shape] + predicted,
                halo_scratch + predict_scratch,
                4,
                "outer_update_predictor",
            )
        else:
            out = call(
                functools.partial(last_kernel, count, fields, sizes),
                [*got, base, par, index, place_back, lift_table],
                [vmem] * (len(got) + 5),
                shape((rows, nodes), F32),
                [pltpu.VMEM(field_shape.shape, F32)]
                + [pltpu.VMEM((rows, nodes), BF16)] * 2
                + [pltpu.VMEM((rows, nodes), F32)]
                + halo_scratch
                + [pltpu.SemaphoreType.DMA((nodes // 256,))],
                1,
                "outer_update",
                hbm,
            )
    return out.reshape(fields, count, nodes).swapaxes(0, 1)[None, None, None]


def solution(mesh):
    sizes = tuple((axis, mesh.shape[axis]) for axis in mesh.axis_names)
    lead = ("gx", "gy", "ha")
    placed = (
        P(*lead, None, None, None),
        P(),
        P(*lead, None),
        P(*lead, None),
        P(*lead, None),
        P(*lead, None),
        P(*lead, None),
        P(*lead, None, None),
    )
    return jax.shard_map(
        functools.partial(shards, sizes),
        mesh=mesh,
        in_specs=placed,
        out_specs=P(*lead, None, None, None),
        check_vma=False,
    )
```
